256 devices in a mesh: expert: 4 (over x), tensor: 32 (over y, z_lo, core), dp: 2 (over z_hi).
Axes of the slice: x: 4, y: 4, z: 8 (z_hi: 2, z_lo: 4; z = z_hi * 4 + z_lo), core: 2. Of those that a mesh axis runs over, the one named last changes fastest.
Arguments:
- tokens: bfloat16 [2048, 6144], P(('expert', 'dp'), 'tensor'), may hold values from -250 to 250
- norm_gain: bfloat16 [6144], P('tensor'), may hold values from 0.25 to 1.75
- expert_ids: int32 [2048, 2], P(('expert', 'dp')), may hold values from 0 to 7, as said below
- route_weights: float32 [2048, 2], P(('expert', 'dp')), may hold values from 0.1 to 1
- gate_weight: bfloat16 [8, 6144, 11264], P(('expert', 'dp'), None, 'tensor'), may hold values from -0.078125 to 0.078125
- up_weight: bfloat16 [8, 6144, 11264], P(('expert', 'dp'), None, 'tensor'), may hold values from -0.078125 to 0.078125
- down_weight: bfloat16 [8, 11264, 6144], P(('expert', 'dp'), 'tensor'), may hold values from -0.0546875 to 0.0546875
Outputs:
- moe_out: bfloat16 [2048, 6144], P(('expert', 'dp'), 'tensor')
The draws below stay inside these ranges and needn't reach their ends.
Inputs may be any that keep to these rules, and one draw needn't show every extreme that they name: `expert_ids`: each row names two different experts. Within each group of 256 consecutive rows no expert is named by more than 128 rows, and one and the same expert is named by exactly 128 rows in every group.
All inputs are finite; a program needn't handle non-finite values.
Results may differ from the reference program's by a relative error of at most 0.034.
Values may be sent and summed in bfloat16 or wider, within the bound.
A program may use at most 128 MiB of HBM per device.

```python
import math
import jax
import jax.numpy as jnp
from jax import lax

D = 6144
FF_WIN = 11264
TOK_GRP = 256
EXPERTS = 8
CAP = 128
TOKENS = 2048
SHARD_FF = 352


def draw_tokens(key, part):
    key = jax.random.fold_in(key, 5)
    base_key, spread_key, row_key = jax.random.split(key, 3)
    position = jnp.arange(D, dtype=jnp.float32) / float(D - 1)
    spread = jax.random.uniform(spread_key, (D,), jnp.float32)
    values = jnp.clip(jax.random.normal(base_key, (TOKENS, D), jnp.float32), -6.0, 6.0)
    row_scale = jnp.exp(jax.random.uniform(row_key, (TOKENS, 1), jnp.float32) * math.log(10.0))
    column_ramp = jnp.exp(position * math.log(3.0))
    column_scale = column_ramp * jnp.exp(spread * math.log(10.0))
    return (0.1 * values * row_scale * column_scale[None, :]).astype(jnp.bfloat16)


def draw_expert_ids(key, part):
    key = jax.random.fold_in(key, 9)
    shuffled = jax.random.permutation(jax.random.fold_in(key, 0), EXPERTS)
    busiest = shuffled[0]
    others = shuffled[1:]

    def one_group(group_index):
        group_key = jax.random.fold_in(key, group_index + 1)
        sub_keys = jax.random.split(group_key, 7)
        reordered = others[jax.random.permutation(sub_keys[0], EXPERTS - 1)]
        split_at = jax.random.randint(sub_keys[1], (), 1, EXPERTS - 2)
        chosen = jax.random.permutation(sub_keys[2], TOK_GRP) < TOK_GRP // 2
        partner = reordered[jax.random.randint(sub_keys[3], (TOK_GRP,), 0, split_at)]
        pair_width = EXPERTS - 1 - split_at
        first_pick = jax.random.randint(sub_keys[4], (TOK_GRP,), 0, pair_width)
        offset = jax.random.randint(sub_keys[5], (TOK_GRP,), 1, pair_width)
        pair_one = reordered[split_at + first_pick]
        pair_two = reordered[split_at + (first_pick + offset) % pair_width]
        first_col = jnp.where(chosen, busiest, pair_one)
        second_col = jnp.where(chosen, partner, pair_two)
        swapped = jax.random.randint(sub_keys[6], (TOK_GRP,), 0, 2) == 1
        return jnp.stack([jnp.where(swapped, second_col, first_col), jnp.where(swapped, first_col, second_col)], axis=1)
    return jax.vmap(one_group)(jnp.arange(TOKENS // TOK_GRP)).reshape(TOKENS, 2).astype(jnp.int32)


def block_scale(key, shape, cuts, least, top_value):
    gain = 1.0
    for axis_at, blocks in cuts:
        heights = jax.random.uniform(jax.random.fold_in(jax.random.fold_in(key, 6), axis_at), (blocks,), jnp.float32, least / len(cuts), top_value / len(cuts))
        gain = gain * jnp.repeat(jnp.exp(heights), shape[axis_at] // blocks).reshape((-1,) + (1,) * (len(shape) - 1 - axis_at))
    return gain


def centred(key, shape, deviation, most, cuts=(), kind=jnp.bfloat16):
    entries = jax.random.normal(key, shape, jnp.float32) * deviation
    if len(cuts) > 0:
        entries = block_scale(key, shape, cuts, -0.22, 0.18) * entries
    return jnp.clip(entries, min=-most, max=most).astype(kind)


def setup_inputs(seed: int = 0) -> dict:
    arg_keys = jax.random.split(jax.random.key(seed), 8)
    tokens = draw_tokens(jax.random.fold_in(arg_keys[7], 71), 0)
    norm_gain = jnp.clip(1.0 + 0.15 * jax.random.normal(arg_keys[1], (D,), jnp.float32), 0.25, 1.75).astype(jnp.bfloat16)
    expert_ids = draw_expert_ids(jax.random.fold_in(arg_keys[7], 71), 0)
    route_weights = jnp.clip(0.1 + 0.9 * jax.random.uniform(arg_keys[3], (TOKENS, 2), jnp.float32) ** block_scale(arg_keys[3], (TOKENS, 2), ((0, 8),), -0.2, 0.2), 0.1, 1.0)
    gate_weight = centred(arg_keys[4], (EXPERTS, D, FF_WIN), D ** -0.5, 0.078125, ((0, 8), (2, 32)))
    up_weight = centred(arg_keys[5], (EXPERTS, D, FF_WIN), D ** -0.5, 0.078125, ((0, 8), (2, 32)))
    down_weight = centred(arg_keys[6], (EXPERTS, FF_WIN, D), FF_WIN ** -0.5, 0.0546875, ((0, 8), (1, 32)))
    return dict(tokens=tokens, norm_gain=norm_gain, expert_ids=expert_ids, route_weights=route_weights, gate_weight=gate_weight, up_weight=up_weight, down_weight=down_weight)


norm_eps = 1e-05

def slot_targets(group_ids, capacity, expert_count):
    labels = jnp.arange(expert_count, dtype=jnp.int32)[None, :]
    first_hits = (group_ids[:, 0:1] == labels).astype(jnp.int32)
    second_hits = (group_ids[:, 1:2] == labels).astype(jnp.int32)
    both_hits = first_hits + second_hits
    earlier = (jnp.cumsum(both_hits, axis=0) - both_hits).astype(jnp.int32)
    first_slot = lax.optimization_barrier(jnp.sum(earlier * first_hits, axis=1)).astype(jnp.int32)
    second_slot = lax.optimization_barrier(jnp.sum(earlier * second_hits, axis=1)).astype(jnp.int32)
    first_dest = (group_ids[:, 0] * capacity + first_slot).astype(jnp.int32)
    second_dest = (group_ids[:, 1] * capacity + second_slot).astype(jnp.int32)
    return (first_dest, second_dest)

def reference(tokens, norm_gain, expert_ids, route_weights, gate_weight, up_weight, down_weight):
    groups = TOKENS // TOK_GRP
    widened = tokens.astype(jnp.float32)
    squares = lax.optimization_barrier(jnp.sum(widened * widened, axis=1, keepdims=True))
    normed = (widened * lax.rsqrt(squares / D + norm_eps) * norm_gain.astype(jnp.float32)[None, :]).astype(jnp.bfloat16)
    grouped_ids = expert_ids.reshape(groups, TOK_GRP, 2)
    grouped_rows = normed.reshape(groups, TOK_GRP, D)
    places = jnp.arange(EXPERTS * CAP, dtype=jnp.int32)

    def dispatch_group(packed):
        group_ids, group_rows = packed
        first_dest, second_dest = slot_targets(group_ids, CAP, EXPERTS)
        select = ((places[:, None] == first_dest[None, :]) | (places[:, None] == second_dest[None, :])).astype(jnp.bfloat16)
        return jnp.dot(select, group_rows, preferred_element_type=jnp.float32).astype(jnp.bfloat16)
    sent = lax.map(dispatch_group, (grouped_ids, grouped_rows))
    expert_in = sent.reshape(groups, EXPERTS, CAP, D).transpose(1, 0, 2, 3).reshape(EXPERTS, groups * CAP, D)

    def run_expert(packed):
        expert_rows, gate_cols, up_cols, down_rows = packed
        gate_val = jnp.dot(expert_rows, gate_cols, preferred_element_type=jnp.float32)
        up_val = jnp.dot(expert_rows, up_cols, preferred_element_type=jnp.float32)
        hidden = (jax.nn.silu(gate_val) * up_val).astype(jnp.bfloat16)
        row_total = expert_rows.shape[0]
        hidden_parts = hidden.reshape(row_total, FF_WIN // SHARD_FF, SHARD_FF).transpose(1, 0, 2)
        down_parts = down_rows.reshape(FF_WIN // SHARD_FF, SHARD_FF, D)

        def add_part(running, packed_part):
            part_hidden, part_down = packed_part
            block_term = jnp.dot(part_hidden, part_down, preferred_element_type=jnp.float32)
            rounded = lax.optimization_barrier(block_term.astype(jnp.bfloat16))
            return (running + rounded.astype(jnp.float32), None)
        outcome = lax.scan(add_part, jnp.zeros((row_total, D), jnp.float32), (hidden_parts, down_parts))
        return outcome[0].astype(jnp.bfloat16)
    expert_out = lax.map(run_expert, (expert_in, gate_weight, up_weight, down_weight))
    flat_out = expert_out.reshape(EXPERTS * groups * CAP, D)

    def targets_of(group_ids):
        first_dest, second_dest = slot_targets(group_ids, CAP, EXPERTS)
        return jnp.stack([first_dest, second_dest], axis=1)
    destinations = jax.vmap(targets_of)(grouped_ids)
    group_base = jnp.arange(groups, dtype=jnp.int32)[:, None, None] * CAP
    flat_index = (destinations // CAP * (groups * CAP) + group_base + destinations % CAP).astype(jnp.int32)
    picked = jnp.take(flat_out, flat_index.reshape(-1), axis=0).reshape(TOKENS, 2, D).astype(jnp.float32)
    weights = route_weights.astype(jnp.float32)
    combined = weights[:, 0:1] * picked[:, 0] + weights[:, 1:2] * picked[:, 1]
    return combined.astype(jnp.bfloat16)
```

```python
import jax
import jax.numpy as jnp
from jax import lax
from jax.experimental import pallas as pl
from jax.experimental.pallas import tpu as pltpu
from jax.sharding import PartitionSpec as P

D = 6144
NORM_EPS = 1e-05
MESH = pl.DeviceIdType.MESH
NX, NY, NZ, ND = 4, 4, 4, 2
GROUP = 256
CAP = 128
HALF = CAP // 2
FEAT = 384
HID = 352
ROUTES = ((0, 0), (1, 0), (0, 1), (1, 1), (2, 1), (3, 1), (2, 0), (3, 0))
PER = 2
CHUNKS = len(ROUTES) // PER
ROWS = PER * HALF
STEPS = CHUNKS * NZ
SECOND, THIRD, MULTIPLY = 2, 4, 5
FARTHEST, NEIGHBOURS, FINISH = 1, 3, 5
LAG = NZ + MULTIPLY
F32 = jnp.float32
BF16 = jnp.bfloat16


def xor4(a, b):
    low = lax.rem(lax.rem(a, 2) + lax.rem(b, 2), 2)
    high = lax.rem(lax.div(a, 2) + lax.div(b, 2), 2)
    return low + 2 * high


def kernel(
    tok_hbm, gain_ref, ids_hbm, rw_hbm, wg_hbm, wu_hbm, wd_hbm,
    out_ref,
    wgu, wd, x, scaled, acc, sq, hid, gains,
    ids_ref, rw_ref, tokx, sibtok, stage, mine, given, srecv, halves, fulls, zrecv, ret, part, partr,
    wsem, dsem, tok_s, tok_r, disp_s, disp_r, gz_s, gz_r, gy_s, gy_r, gf_s, gf_r,
    z_s, z_r, y_s, y_r, f_s, f_r, b_s, b_r,
    sib_s, sib_r, h_s, h_r, w_s, w_r, zz_s, zz_r, ret_s, ret_r, part_s, part_r,
):
    xi = lax.axis_index("expert")
    di = lax.axis_index("dp")
    me = lax.axis_index("tensor")
    c = lax.rem(me, 2)
    z = lax.rem(lax.div(me, 2), NZ)
    y = lax.div(me, 2 * NZ)
    own = y * NZ + z
    yp = lax.rem(y + 1, NY)
    ym = lax.rem(y + NY - 1, NY)

    def tid(yy, zz, cc):
        return (yy * NZ + zz) * 2 + cc

    sib = {"tensor": tid(y, z, 1 - c)}
    up = {"tensor": tid(yp, z, c)}
    down = {"tensor": tid(ym, z, c)}

    def zdev(i):
        return {"tensor": tid(y, xor4(z, i), c)}

    def expert_of(k):
        dx, dd = ROUTES[k]
        return {"expert": lax.rem(xi + dx, NX), "dp": lax.rem(di + dd, ND)}

    def group_of(k):
        dx, dd = ROUTES[k]
        return {"expert": lax.rem(xi + NX - dx, NX), "dp": lax.rem(di + dd, ND)}

    def rcopy(src, dst, ssem, rsem, dev):
        return pltpu.make_async_remote_copy(
            src_ref=src, dst_ref=dst, send_sem=ssem, recv_sem=rsem, device_id=dev, device_id_type=MESH
        )

    barrier = pltpu.get_barrier_semaphore()
    partners = [sib, up, down] + [zdev(i) for i in range(1, NZ)] + [expert_of(k) for k in range(1, len(ROUTES))]
    for dev in partners:
        pl.semaphore_signal(barrier, inc=1, device_id=dev, device_id_type=MESH)

    share = FEAT // 2
    small = [
        pltpu.make_async_copy(ids_hbm, ids_ref, wsem.at[0]),
        pltpu.make_async_copy(tok_hbm, tokx.at[pl.ds(0, share)], wsem.at[1]),
        pltpu.make_async_copy(rw_hbm, rw_ref, wsem.at[2]),
    ]
    for load in small:
        load.start()
    tokx[share:, :] = jnp.zeros((16, GROUP), BF16)
    tokx[share:, 0:share] = jnp.broadcast_to(gain_ref[...].astype(F32).reshape(1, share), (16, share)).astype(BF16)

    before = (
        lax.broadcasted_iota(jnp.int32, (GROUP, GROUP), 0) < lax.broadcasted_iota(jnp.int32, (GROUP, GROUP), 1)
    ).astype(F32).astype(BF16)
    labels = lax.broadcasted_iota(jnp.int32, (16, GROUP), 0)
    spot = lax.broadcasted_iota(jnp.int32, (HALF, 1), 0) + HALF * c
    place = []
    for k in range(len(ROUTES)):
        dev = expert_of(k)
        place.append(spot + (dev["expert"] * ND + dev["dp"]) * CAP)
    place = jnp.concatenate(place, axis=0)
    small[0].wait()
    e0 = ids_ref[0:1, :]
    e1 = ids_ref[1:2, :]
    hit0 = (e0 == labels).astype(F32)
    hit1 = (e1 == labels).astype(F32)
    earlier = jnp.dot((hit0 + hit1).astype(BF16), before, preferred_element_type=F32)
    slot0 = jnp.sum(earlier * hit0, axis=0, keepdims=True).astype(jnp.int32)
    slot1 = jnp.sum(earlier * hit1, axis=0, keepdims=True).astype(jnp.int32)
    dest0 = e0 * CAP + slot0
    dest1 = e1 * CAP + slot1
    small[1].wait()

    pl.semaphore_wait(barrier, len(partners))

    tok_copy = rcopy(tokx, sibtok, tok_s, tok_r, sib)
    tok_copy.start()
    select = ((place == dest0) | (place == dest1)).astype(F32).astype(BF16)

    loads = []
    for zz in range(NZ):
        for yy in range(NY):
            for k, source in enumerate((wg_hbm, wu_hbm)):
                loads.append(
                    pltpu.make_async_copy(
                        source.at[0, :, pl.ds((yy * NZ + zz) * FEAT, FEAT)],
                        wgu.at[zz, pl.ds(k * HID, HID), pl.ds(yy * FEAT, FEAT)],
                        wsem.at[3 + len(loads)],
                    )
                )
    dloads = [
        pltpu.make_async_copy(wd_hbm.at[0, :, pl.ds(j * FEAT, FEAT)], wd.at[j], dsem.at[j])
        for j in range(NY * NZ)
    ]

    tok_copy.wait_recv()
    here = tokx[...].astype(F32)
    there = sibtok[...].astype(F32)
    first_core = jnp.where(c == 0, here, there)
    second_core = jnp.where(c == 0, there, here)
    both = jnp.concatenate([first_core[:share], second_core[:share]], axis=0).astype(BF16)
    rows = lax.dot_general(
        select, both, (((1,), (1,)), ((), ())), preferred_element_type=F32
    ).astype(BF16)
    x[0, own, c, 0:HALF, :] = rows[0:HALF]

    def disp_copy(k):
        target = x.at[k // PER, own, c, pl.ds((k % PER) * HALF, HALF)]
        return rcopy(stage.at[k], target, disp_s.at[k], disp_r.at[k], expert_of(k))

    for k in range(1, len(ROUTES)):
        stage[k] = rows[k * HALF : (k + 1) * HALF]
        disp_copy(k).start()

    gain_row = jnp.concatenate(
        [first_core[share : share + 1, 0:share], second_core[share : share + 1, 0:share]], axis=1
    )
    index = lax.broadcasted_iota(jnp.int32, (16, 128), 0)
    tile = jnp.zeros((16, 128), F32)
    for j in range(3):
        tile = jnp.where(index == j, jnp.broadcast_to(gain_row[:, 128 * j : 128 * (j + 1)], (16, 128)), tile)
    gains[y, z] = tile.astype(BF16)

    def gzc(i):
        return rcopy(gains.at[y, z], gains.at[y, z], gz_s.at[i], gz_r.at[i], zdev(i))

    def gyc(i, way):
        ref = gains.at[y, xor4(z, i)]
        return rcopy(ref, ref, gy_s.at[i, way], gy_r.at[i, way], (up, down)[way])

    def gfc(i):
        ref = gains.at[ym, xor4(z, i)]
        return rcopy(ref, ref, gf_s.at[i], gf_r.at[i], up)

    for i in range(1, NZ):
        gzc(i).start()

    def at_step(s):
        q = lax.div(s, NZ)
        i = lax.rem(s, NZ)
        return q, i, xor4(z, i)

    def zc(q, i):
        return rcopy(x.at[q, own, c], x.at[q, own, c], z_s.at[q, i], z_r.at[q, i], zdev(i))

    def yc(s, way):
        q, i, zi = at_step(s)
        b = y * NZ + zi
        return rcopy(x.at[q, b, c], x.at[q, b, c], y_s.at[s, way], y_r.at[s, way], (up, down)[way])

    def fc(s, way):
        q, i, zi = at_step(s)
        b = (ym, yp)[way] * NZ + zi
        ref = x.at[q, b, c, pl.ds(way * (ROWS // 2), ROWS // 2)]
        return rcopy(ref, ref, f_s.at[s, way], f_r.at[s, way], (up, down)[way])

    def bc(s, r):
        q, i, zi = at_step(s)
        b = lax.rem(y + r, NY) * NZ + zi
        return rcopy(x.at[q, b, c], x.at[q, b, c], b_s.at[s, r], b_r.at[s, r], sib)

    def open_chunk(chunk):
        for k in range(max(1, chunk * PER), (chunk + 1) * PER):
            disp_copy(k).wait_recv()
        for j in range(1, NZ):
            zc(chunk, j).start()

    def first(s):
        q, i, zi = at_step(s)

        @pl.when(i > 0)
        def _():
            zc(q, i).wait_recv()

        yc(s, 0).start()
        yc(s, 1).start()
        bc(s, 0).start()

        @pl.when((s > 0) & (s < NZ))
        def _():
            gzc(i).wait_recv()

        @pl.when(s < NZ)
        def _():
            gyc(i, 0).start()
            gyc(i, 1).start()

        for chunk in range(1, CHUNKS):

            @pl.when(s == chunk * NZ - 1)
            def _():
                open_chunk(chunk)

    def second(s):
        q, i, zi = at_step(s)
        yc(s, 0).wait_recv()
        fc(s, 0).start()
        yc(s, 1).wait_recv()
        fc(s, 1).start()
        bc(s, 3).start()
        bc(s, 1).start()

        @pl.when(s < NZ)
        def _():
            gyc(i, 0).wait_recv()
            gfc(i).start()
            gyc(i, 1).wait_recv()

    def third(s):
        q, i, zi = at_step(s)
        fc(s, 0).wait_recv()
        fc(s, 1).wait_recv()
        bc(s, 2).start()

        @pl.when(s < NZ)
        def _():
            gfc(i).wait_recv()

    def gate_up(s):
        q, i, zi = at_step(s)
        for r in range(NY):
            bc(s, r).wait_recv()
        squares = sq[...]
        for yy in range(NY):
            block = x[q, yy * NZ + zi].reshape(2 * ROWS, FEAT)
            gain = gains[yy, zi].astype(F32)
            for j in range(3):
                slab = block[:, 128 * j : 128 * (j + 1)].astype(F32)
                squares = squares + slab * slab
                at = yy * FEAT + 128 * j
                scaled[:, at : at + 128] = (slab * gain[j : j + 1, :]).astype(BF16)
        sq[...] = squares
        acc[...] += lax.dot_general(
            scaled[...], wgu[zi], (((1,), (1,)), ((), ())), preferred_element_type=F32
        )

        @pl.when(i == NZ - 1)
        def _():
            total = jnp.sum(sq[...], axis=1, keepdims=True)
            scale = lax.rsqrt(total / D + NORM_EPS)
            gate = acc[:, 0:HID] * scale
            lift = acc[:, HID:] * scale
            value = (gate / (1.0 + jnp.exp(-gate)) * lift).astype(BF16)
            for h in range(2):
                hid[q, lax.rem(c + h, 2)] = value[h * ROWS : (h + 1) * ROWS]
            acc[...] = jnp.zeros_like(acc)
            sq[...] = jnp.zeros_like(sq)

    def out_step(s):
        return lax.div(s, NZ), (NZ - 1) - lax.rem(s, NZ)

    def sc(s, r):
        return rcopy(given.at[s, r], srecv.at[s, r], sib_s.at[s, r], sib_r.at[s, r], sib)

    def hc(s, way):
        span = pl.ds(way * (ROWS // 2), ROWS // 2)
        return rcopy(mine.at[s, 2, span], halves.at[s, way], h_s.at[s, way], h_r.at[s, way], (up, down)[way])

    def wc(s, way):
        return rcopy(mine.at[s, (1, 3)[way]], fulls.at[s, way], w_s.at[s, way], w_r.at[s, way], (up, down)[way])

    def zzc(s):
        q, i = out_step(s)
        return rcopy(mine.at[s, 0], zrecv.at[q, i], zz_s.at[q, i], zz_r.at[q, i], zdev(i))

    def retc(k):
        source = mine.at[k // PER * NZ + NZ - 1, 0, pl.ds((k % PER) * HALF, HALF)]
        return rcopy(source, ret.at[k], ret_s.at[k], ret_r.at[k], group_of(k))

    def produce(s):
        q, i = out_step(s)
        zi = xor4(z, i)
        left = hid[q].reshape(2 * ROWS, HID)
        for r in (2, 1, 3, 0):
            b = lax.rem(y + r, NY) * NZ + zi
            block = jnp.dot(left, wd[b], preferred_element_type=F32).astype(BF16)
            given[s, r] = block[ROWS:]
            sc(s, r).start()
            mine[s, r] = block[:ROWS]

    def chip_sum(s, r):
        sc(s, r).wait_recv()
        return mine[s, r].astype(F32) + srecv[s, r].astype(F32)

    def farthest(s):
        mine[s, 2] = chip_sum(s, 2).astype(BF16)
        hc(s, 0).start()
        hc(s, 1).start()

    def neighbours(s):
        half = ROWS // 2
        total = chip_sum(s, 1)
        hc(s, 0).wait_recv()
        total = jnp.concatenate([total[:half] + halves[s, 0].astype(F32), total[half:]], axis=0)
        mine[s, 1] = total.astype(BF16)
        wc(s, 0).start()
        total = chip_sum(s, 3)
        hc(s, 1).wait_recv()
        total = jnp.concatenate([total[:half], total[half:] + halves[s, 1].astype(F32)], axis=0)
        mine[s, 3] = total.astype(BF16)
        wc(s, 1).start()

    def finish(s):
        q, i = out_step(s)
        total = chip_sum(s, 0)
        wc(s, 0).wait_recv()
        total = total + fulls[s, 0].astype(F32)
        wc(s, 1).wait_recv()
        total = total + fulls[s, 1].astype(F32)

        @pl.when(i > 0)
        def _():
            mine[s, 0] = total.astype(BF16)
            zzc(s).start()

        @pl.when(i == 0)
        def _():
            whole = total
            for j in range(1, NZ):
                zzc(s - j).wait_recv()
                whole = whole + zrecv[q, j].astype(F32)
            whole = whole.astype(BF16)
            mine[s, 0] = whole

            @pl.when(q == 0)
            def _():
                ret[0] = whole[0:HALF]

            for chunk in range(CHUNKS):

                @pl.when(q == chunk)
                def _():
                    for k in range(max(1, chunk * PER), (chunk + 1) * PER):
                        retc(k).start()

    def step(t, carry):
        u = t - LAG
        stages = (
            (first, t, 0), (second, t, SECOND), (third, t, THIRD),
            (finish, u, FINISH), (neighbours, u, NEIGHBOURS), (farthest, u, FARTHEST),
            (gate_up, t, MULTIPLY), (produce, u, 0),
        )
        for stage_of, now, behind in stages:

            @pl.when((now >= behind) & (now < STEPS + behind))
            def _():
                stage_of(now - behind)

        return carry

    open_chunk(0)
    first(jnp.int32(0))
    for load in loads + dloads:
        load.start()
    acc[...] = jnp.zeros_like(acc)
    sq[...] = jnp.zeros_like(sq)
    for load in loads + dloads:
        load.wait()
    lax.fori_loop(1, LAG + STEPS + FINISH, step, 0)

    small[2].wait()
    combined = jnp.zeros((FEAT, GROUP), F32)
    for chunk in range(CHUNKS):
        for k in range(max(1, chunk * PER), (chunk + 1) * PER):
            retc(k).wait_recv()
        came = ret[chunk * PER : (chunk + 1) * PER].reshape(ROWS, FEAT)
        spots = place[chunk * ROWS : (chunk + 1) * ROWS]
        for k, dest in enumerate((dest0, dest1)):
            pick = (spots == dest).astype(F32).astype(BF16)
            combined += rw_ref[k : k + 1, :] * lax.dot_general(
                came, pick, (((0,), (0,)), ((), ())), preferred_element_type=F32
            )
    left = combined[:share]
    right = combined[share:]
    part[...] = jnp.where(c == 0, right, left)
    part_copy = rcopy(part, partr, part_s, part_r, sib)
    part_copy.start()
    kept = jnp.where(c == 0, left, right)
    part_copy.wait_recv()
    out_ref[...] = (kept + partr[...]).astype(BF16)

    part_copy.wait_send()
    tok_copy.wait_send()
    for k in range(1, len(ROUTES)):
        disp_copy(k).wait_send()
        retc(k).wait_send()
    for i in range(NZ):
        if i > 0:
            gzc(i).wait_send()
        gyc(i, 0).wait_send()
        gyc(i, 1).wait_send()
        gfc(i).wait_send()

    def drain(s, carry):
        for way in range(2):
            yc(s, way).wait_send()
            fc(s, way).wait_send()
            hc(s, way).wait_send()
            wc(s, way).wait_send()
        for r in range(NY):
            bc(s, r).wait_send()
            sc(s, r).wait_send()
        q, i, zi = at_step(s)

        @pl.when(i > 0)
        def _():
            zc(q, i).wait_send()

        q, i = out_step(s)

        @pl.when(i > 0)
        def _():
            zzc(s).wait_send()

        return carry

    lax.fori_loop(0, STEPS, drain, 0)


def per_device(tokens, norm_gain, expert_ids, route_weights, gate_weight, up_weight, down_weight):
    vmem = pl.BlockSpec(memory_space=pltpu.VMEM)
    hbm = pl.BlockSpec(memory_space=pl.ANY)
    blocks = NY * NZ
    dma = pltpu.SemaphoreType.DMA
    scratch = [
        pltpu.VMEM((NZ, 2 * HID, NY * FEAT), BF16),
        pltpu.VMEM((blocks, HID, FEAT), BF16),
        pltpu.VMEM((CHUNKS, blocks, 2, ROWS, FEAT), BF16),
        pltpu.VMEM((2 * ROWS, NY * FEAT), BF16),
        pltpu.VMEM((2 * ROWS, 2 * HID), F32),
        pltpu.VMEM((2 * ROWS, 128), F32),
        pltpu.VMEM((CHUNKS, 2, ROWS, HID), BF16),
        pltpu.VMEM((NY, NZ, 16, 128), BF16),
        pltpu.VMEM((2, GROUP), jnp.int32),
        pltpu.VMEM((2, GROUP), F32),
        pltpu.VMEM((FEAT // 2 + 16, GROUP), BF16),
        pltpu.VMEM((FEAT // 2 + 16, GROUP), BF16),
        pltpu.VMEM((len(ROUTES), HALF, FEAT), BF16),
        pltpu.VMEM((STEPS, NY, ROWS, FEAT), BF16),
        pltpu.VMEM((STEPS, NY, ROWS, FEAT), BF16),
        pltpu.VMEM((STEPS, NY, ROWS, FEAT), BF16),
        pltpu.VMEM((STEPS, 2, ROWS // 2, FEAT), BF16),
        pltpu.VMEM((STEPS, 2, ROWS, FEAT), BF16),
        pltpu.VMEM((CHUNKS, NZ, ROWS, FEAT), BF16),
        pltpu.VMEM((len(ROUTES), HALF, FEAT), BF16),
        pltpu.VMEM((FEAT // 2, GROUP), F32),
        pltpu.VMEM((FEAT // 2, GROUP), F32),
        dma((3 + 2 * blocks,)), dma((blocks,)),
        dma, dma, dma((len(ROUTES),)), dma((len(ROUTES),)),
        dma((NZ,)), dma((NZ,)), dma((NZ, 2)), dma((NZ, 2)), dma((NZ,)), dma((NZ,)),
        dma((CHUNKS, NZ)), dma((CHUNKS, NZ)), dma((STEPS, 2)), dma((STEPS, 2)),
        dma((STEPS, 2)), dma((STEPS, 2)), dma((STEPS, NY)), dma((STEPS, NY)),
        dma((STEPS, NY)), dma((STEPS, NY)), dma((STEPS, 2)), dma((STEPS, 2)),
        dma((STEPS, 2)), dma((STEPS, 2)), dma((CHUNKS, NZ)), dma((CHUNKS, NZ)),
        dma((len(ROUTES),)), dma((len(ROUTES),)), dma, dma,
    ]
    rows = CHUNKS * 2 * ROWS
    out = pl.pallas_call(
        kernel,
        out_shape=jax.ShapeDtypeStruct((FEAT // 2, GROUP), BF16),
        in_specs=[hbm, vmem, hbm, hbm, hbm, hbm, hbm],
        out_specs=vmem,
        scratch_shapes=scratch,
        cost_estimate=pl.CostEstimate(
            flops=6 * rows * D * HID, bytes_accessed=6 * D * HID, transcendentals=rows * HID
        ),
        compiler_params=pltpu.CompilerParams(
            collective_id=0, has_side_effects=True, vmem_limit_bytes=61 * 1024 * 1024
        ),
    )(
        tokens.T,
        norm_gain,
        expert_ids.T,
        route_weights.T,
        gate_weight.swapaxes(1, 2),
        up_weight.swapaxes(1, 2),
        down_weight,
    )
    return out.T


def solution(mesh):
    placed = (
        P(("expert", "dp"), "tensor"),
        P("tensor"),
        P(("expert", "dp"), None),
        P(("expert", "dp"), None),
        P(("expert", "dp"), None, "tensor"),
        P(("expert", "dp"), None, "tensor"),
        P(("expert", "dp"), "tensor", None),
    )
    return jax.shard_map(
        per_device,
        mesh=mesh,
        in_specs=placed,
        out_specs=P(("expert", "dp"), "tensor"),
        check_vma=False,
    )
```

```python
import jax
import jax.numpy as jnp
from jax import lax
from jax.experimental import pallas as pl
from jax.experimental.pallas import tpu as pltpu
from jax.sharding import PartitionSpec as P

D = 6144
NORM_EPS = 1e-05
MESH = pl.DeviceIdType.MESH
NX, NY, NZ, ND = 4, 4, 4, 2
GROUP = 256
CAP = 128
HALF = CAP // 2
FEAT = 384
HID = 352
ROUTES = ((0, 0), (1, 0), (0, 1), (1, 1), (2, 1), (3, 1), (2, 0), (3, 0))
PER = 2
CHUNKS = len(ROUTES) // PER
ROWS = PER * HALF
STEPS = CHUNKS * NZ
SECOND, THIRD, MULTIPLY = 2, 4, 5
FARTHEST, NEIGHBOURS, FINISH = 1, 3, 5
LAG = NZ + MULTIPLY
F32 = jnp.float32
BF16 = jnp.bfloat16


def xor4(a, b):
    low = lax.rem(lax.rem(a, 2) + lax.rem(b, 2), 2)
    high = lax.rem(lax.div(a, 2) + lax.div(b, 2), 2)
    return low + 2 * high


def kernel(
    tok_hbm, gain_ref, ids_hbm, rw_hbm, wg_hbm, wu_hbm, wd_hbm,
    out_ref,
    wgu, wd, x, scaled, acc, sq, hid, gains,
    ids_ref, rw_ref, tokx, sibtok, stage, mine, given, srecv, halves, fulls, zrecv, ret, part, partr,
    wsem, dsem, tok_s, tok_r, disp_s, disp_r, gz_s, gz_r, gy_s, gy_r, gf_s, gf_r,
    z_s, z_r, y_s, y_r, f_s, f_r, b_s, b_r,
    sib_s, sib_r, h_s, h_r, w_s, w_r, zz_s, zz_r, ret_s, ret_r, part_s, part_r,
):
    xi = lax.axis_index("expert")
    di = lax.axis_index("dp")
    me = lax.axis_index("tensor")
    c = lax.rem(me, 2)
    z = lax.rem(lax.div(me, 2), NZ)
    y = lax.div(me, 2 * NZ)
    own = y * NZ + z
    yp = lax.rem(y + 1, NY)
    ym = lax.rem(y + NY - 1, NY)

    def tid(yy, zz, cc):
        return (yy * NZ + zz) * 2 + cc

    sib = {"tensor": tid(y, z, 1 - c)}
    up = {"tensor": tid(yp, z, c)}
    down = {"tensor": tid(ym, z, c)}

    def zdev(i):
        return {"tensor": tid(y, xor4(z, i), c)}

    def expert_of(k):
        dx, dd = ROUTES[k]
        return {"expert": lax.rem(xi + dx, NX), "dp": lax.rem(di + dd, ND)}

    def group_of(k):
        dx, dd = ROUTES[k]
        return {"expert": lax.rem(xi + NX - dx, NX), "dp": lax.rem(di + dd, ND)}

    def rcopy(src, dst, ssem, rsem, dev):
        return pltpu.make_async_remote_copy(
            src_ref=src, dst_ref=dst, send_sem=ssem, recv_sem=rsem, device_id=dev, device_id_type=MESH
        )

    barrier = pltpu.get_barrier_semaphore()
    partners = [sib, up, down] + [zdev(i) for i in range(1, NZ)] + [expert_of(k) for k in range(1, len(ROUTES))]
    for dev in partners:
        pl.semaphore_signal(barrier, inc=1, device_id=dev, device_id_type=MESH)

    share = FEAT // 2
    small = [
        pltpu.make_async_copy(ids_hbm, ids_ref, wsem.at[0]),
        pltpu.make_async_copy(tok_hbm, tokx.at[pl.ds(0, share)], wsem.at[1]),
        pltpu.make_async_copy(rw_hbm, rw_ref, wsem.at[2]),
    ]
    for load in small:
        load.start()
    tokx[share:, :] = jnp.zeros((16, GROUP), BF16)
    tokx[share:, 0:share] = jnp.broadcast_to(gain_ref[...].astype(F32).reshape(1, share), (16, share)).astype(BF16)

    before = (
        lax.broadcasted_iota(jnp.int32, (GROUP, GROUP), 0) < lax.broadcasted_iota(jnp.int32, (GROUP, GROUP), 1)
    ).astype(F32).astype(BF16)
    labels = lax.broadcasted_iota(jnp.int32, (16, GROUP), 0)
    spot = lax.broadcasted_iota(jnp.int32, (HALF, 1), 0) + HALF * c
    place = []
    for k in range(len(ROUTES)):
        dev = expert_of(k)
        place.append(spot + (dev["expert"] * ND + dev["dp"]) * CAP)
    place = jnp.concatenate(place, axis=0)
    small[0].wait()
    e0 = ids_ref[0:1, :]
    e1 = ids_ref[1:2, :]
    hit0 = (e0 == labels).astype(F32)
    hit1 = (e1 == labels).astype(F32)
    earlier = jnp.dot((hit0 + hit1).astype(BF16), before, preferred_element_type=F32)
    slot0 = jnp.sum(earlier * hit0, axis=0, keepdims=True).astype(jnp.int32)
    slot1 = jnp.sum(earlier * hit1, axis=0, keepdims=True).astype(jnp.int32)
    dest0 = e0 * CAP + slot0
    dest1 = e1 * CAP + slot1
    small[1].wait()

    pl.semaphore_wait(barrier, len(partners))

    tok_copy = rcopy(tokx, sibtok, tok_s, tok_r, sib)
    tok_copy.start()
    select = ((place == dest0) | (place == dest1)).astype(F32).astype(BF16)

    loads = []
    for zz in range(NZ):
        for yy in range(NY):
            for k, source in enumerate((wg_hbm, wu_hbm)):
                loads.append(
                    pltpu.make_async_copy(
                        source.at[0, :, pl.ds((yy * NZ + zz) * FEAT, FEAT)],
                        wgu.at[zz, pl.ds(k * HID, HID), pl.ds(yy * FEAT, FEAT)],
                        wsem.at[3 + len(loads)],
                    )
                )
    dloads = [
        pltpu.make_async_copy(wd_hbm.at[0, :, pl.ds(j * FEAT, FEAT)], wd.at[j], dsem.at[j])
        for j in range(NY * NZ)
    ]

    tok_copy.wait_recv()
    here = tokx[...].astype(F32)
    there = sibtok[...].astype(F32)
    first_core = jnp.where(c == 0, here, there)
    second_core = jnp.where(c == 0, there, here)
    both = jnp.concatenate([first_core[:share], second_core[:share]], axis=0).astype(BF16)
    rows = lax.dot_general(
        select, both, (((1,), (1,)), ((), ())), preferred_element_type=F32
    ).astype(BF16)
    x[0, own, c, 0:HALF, :] = rows[0:HALF]

    def disp_copy(k):
        target = x.at[k // PER, own, c, pl.ds((k % PER) * HALF, HALF)]
        return rcopy(stage.at[k], target, disp_s.at[k], disp_r.at[k], expert_of(k))

    for k in range(1, len(ROUTES)):
        stage[k] = rows[k * HALF : (k + 1) * HALF]
        disp_copy(k).start()

    gain_row = jnp.concatenate(
        [first_core[share : share + 1, 0:share], second_core[share : share + 1, 0:share]], axis=1
    )
    index = lax.broadcasted_iota(jnp.int32, (16, 128), 0)
    tile = jnp.zeros((16, 128), F32)
    for j in range(3):
        tile = jnp.where(index == j, jnp.broadcast_to(gain_row[:, 128 * j : 128 * (j + 1)], (16, 128)), tile)
    gains[y, z] = tile.astype(BF16)

    def gzc(i):
        return rcopy(gains.at[y, z], gains.at[y, z], gz_s.at[i], gz_r.at[i], zdev(i))

    def gyc(i, way):
        ref = gains.at[y, xor4(z, i)]
        return rcopy(ref, ref, gy_s.at[i, way], gy_r.at[i, way], (up, down)[way])

    def gfc(i):
        ref = gains.at[ym, xor4(z, i)]
        return rcopy(ref, ref, gf_s.at[i], gf_r.at[i], up)

    for i in range(1, NZ):
        gzc(i).start()

    def at_step(s):
        q = lax.div(s, NZ)
        i = lax.rem(s, NZ)
        return q, i, xor4(z, i)

    def zc(q, i):
        return rcopy(x.at[q, own, c], x.at[q, own, c], z_s.at[q, i], z_r.at[q, i], zdev(i))

    def yc(s, way):
        q, i, zi = at_step(s)
        b = y * NZ + zi
        return rcopy(x.at[q, b, c], x.at[q, b, c], y_s.at[s, way], y_r.at[s, way], (up, down)[way])

    def fc(s, way):
        q, i, zi = at_step(s)
        b = (ym, yp)[way] * NZ + zi
        ref = x.at[q, b, c, pl.ds(way * (ROWS // 2), ROWS // 2)]
        return rcopy(ref, ref, f_s.at[s, way], f_r.at[s, way], (up, down)[way])

    def bc(s, r):
        q, i, zi = at_step(s)
        b = lax.rem(y + r, NY) * NZ + zi
        return rcopy(x.at[q, b, c], x.at[q, b, c], b_s.at[s, r], b_r.at[s, r], sib)

    def open_chunk(chunk):
        for k in range(max(1, chunk * PER), (chunk + 1) * PER):
            disp_copy(k).wait_recv()
        for j in range(1, NZ):
            zc(chunk, j).start()

    def first(s):
        q, i, zi = at_step(s)

        @pl.when(i > 0)
        def _():
            zc(q, i).wait_recv()

        yc(s, 0).start()
        yc(s, 1).start()
        bc(s, 0).start()

        @pl.when((s > 0) & (s < NZ))
        def _():
            gzc(i).wait_recv()

        @pl.when(s < NZ)
        def _():
            gyc(i, 0).start()
            gyc(i, 1).start()

        for chunk in range(1, CHUNKS):

            @pl.when(s == chunk * NZ - 1)
            def _():
                open_chunk(chunk)

    def second(s):
        q, i, zi = at_step(s)
        yc(s, 0).wait_recv()
        fc(s, 0).start()
        yc(s, 1).wait_recv()
        fc(s, 1).start()
        bc(s, 3).start()
        bc(s, 1).start()

        @pl.when(s < NZ)
        def _():
            gyc(i, 0).wait_recv()
            gfc(i).start()
            gyc(i, 1).wait_recv()

    def third(s):
        q, i, zi = at_step(s)
        fc(s, 0).wait_recv()
        fc(s, 1).wait_recv()
        bc(s, 2).start()

        @pl.when(s < NZ)
        def _():
            gfc(i).wait_recv()

    def gate_up(s):
        q, i, zi = at_step(s)
        for r in range(NY):
            bc(s, r).wait_recv()
        squares = sq[...]
        for yy in range(NY):
            block = x[q, yy * NZ + zi].reshape(2 * ROWS, FEAT)
            gain = gains[yy, zi].astype(F32)
            for j in range(3):
                slab = block[:, 128 * j : 128 * (j + 1)].astype(F32)
                squares = squares + slab * slab
                at = yy * FEAT + 128 * j
                scaled[:, at : at + 128] = (slab * gain[j : j + 1, :]).astype(BF16)
        sq[...] = squares
        acc[...] += lax.dot_general(
            wgu[zi], scaled[...], (((1,), (1,)), ((), ())), preferred_element_type=F32
        )

        @pl.when(i == NZ - 1)
        def _():
            total = jnp.sum(jnp.transpose(sq[...]), axis=0, keepdims=True)
            scale = lax.rsqrt(total / D + NORM_EPS)
            gate = acc[0:HID, :] * scale
            lift = acc[HID:, :] * scale
            value = jnp.transpose(gate / (1.0 + jnp.exp(-gate)) * lift).astype(BF16)
            for h in range(2):
                hid[q, lax.rem(c + h, 2)] = value[h * ROWS : (h + 1) * ROWS]
            acc[...] = jnp.zeros_like(acc)
            sq[...] = jnp.zeros_like(sq)

    def out_step(s):
        return lax.div(s, NZ), (NZ - 1) - lax.rem(s, NZ)

    def sc(s, r):
        return rcopy(given.at[s, r], srecv.at[s, r], sib_s.at[s, r], sib_r.at[s, r], sib)

    def hc(s, way):
        span = pl.ds(way * (ROWS // 2), ROWS // 2)
        return rcopy(mine.at[s, 2, span], halves.at[s, way], h_s.at[s, way], h_r.at[s, way], (up, down)[way])

    def wc(s, way):
        return rcopy(mine.at[s, (1, 3)[way]], fulls.at[s, way], w_s.at[s, way], w_r.at[s, way], (up, down)[way])

    def zzc(s):
        q, i = out_step(s)
        return rcopy(mine.at[s, 0], zrecv.at[q, i], zz_s.at[q, i], zz_r.at[q, i], zdev(i))

    def retc(k):
        source = mine.at[k // PER * NZ + NZ - 1, 0, pl.ds((k % PER) * HALF, HALF)]
        return rcopy(source, ret.at[k], ret_s.at[k], ret_r.at[k], group_of(k))

    def produce(s):
        q, i = out_step(s)
        zi = xor4(z, i)
        left = hid[q].reshape(2 * ROWS, HID)
        for r in (2, 1, 3, 0):
            b = lax.rem(y + r, NY) * NZ + zi
            block = jnp.dot(left, wd[b], preferred_element_type=F32).astype(BF16)
            given[s, r] = block[ROWS:]
            sc(s, r).start()
            mine[s, r] = block[:ROWS]

    def chip_sum(s, r):
        sc(s, r).wait_recv()
        return mine[s, r].astype(F32) + srecv[s, r].astype(F32)

    def farthest(s):
        mine[s, 2] = chip_sum(s, 2).astype(BF16)
        hc(s, 0).start()
        hc(s, 1).start()

    def neighbours(s):
        half = ROWS // 2
        total = chip_sum(s, 1)
        hc(s, 0).wait_recv()
        total = jnp.concatenate([total[:half] + halves[s, 0].astype(F32), total[half:]], axis=0)
        mine[s, 1] = total.astype(BF16)
        wc(s, 0).start()
        total = chip_sum(s, 3)
        hc(s, 1).wait_recv()
        total = jnp.concatenate([total[:half], total[half:] + halves[s, 1].astype(F32)], axis=0)
        mine[s, 3] = total.astype(BF16)
        wc(s, 1).start()

    def finish(s):
        q, i = out_step(s)
        total = chip_sum(s, 0)
        wc(s, 0).wait_recv()
        total = total + fulls[s, 0].astype(F32)
        wc(s, 1).wait_recv()
        total = total + fulls[s, 1].astype(F32)

        @pl.when(i > 0)
        def _():
            mine[s, 0] = total.astype(BF16)
            zzc(s).start()

        @pl.when(i == 0)
        def _():
            whole = total
            for j in range(1, NZ):
                zzc(s - j).wait_recv()
                whole = whole + zrecv[q, j].astype(F32)
            whole = whole.astype(BF16)
            mine[s, 0] = whole

            @pl.when(q == 0)
            def _():
                ret[0] = whole[0:HALF]

            for chunk in range(CHUNKS):

                @pl.when(q == chunk)
                def _():
                    for k in range(max(1, chunk * PER), (chunk + 1) * PER):
                        retc(k).start()

    def step(t, carry):
        u = t - LAG
        stages = (
            (first, t, 0), (second, t, SECOND), (third, t, THIRD),
            (finish, u, FINISH), (neighbours, u, NEIGHBOURS), (farthest, u, FARTHEST),
            (gate_up, t, MULTIPLY), (produce, u, 0),
        )
        for stage_of, now, behind in stages:

            @pl.when((now >= behind) & (now < STEPS + behind))
            def _():
                stage_of(now - behind)

        return carry

    open_chunk(0)
    first(jnp.int32(0))
    for load in loads + dloads:
        load.start()
    acc[...] = jnp.zeros_like(acc)
    sq[...] = jnp.zeros_like(sq)
    for load in loads + dloads:
        load.wait()
    lax.fori_loop(1, LAG + STEPS + FINISH, step, 0)

    small[2].wait()
    combined = jnp.zeros((FEAT, GROUP), F32)
    for chunk in range(CHUNKS):
        for k in range(max(1, chunk * PER), (chunk + 1) * PER):
            retc(k).wait_recv()
        came = ret[chunk * PER : (chunk + 1) * PER].reshape(ROWS, FEAT)
        spots = place[chunk * ROWS : (chunk + 1) * ROWS]
        for k, dest in enumerate((dest0, dest1)):
            pick = (spots == dest).astype(F32).astype(BF16)
            combined += rw_ref[k : k + 1, :] * lax.dot_general(
                came, pick, (((0,), (0,)), ((), ())), preferred_element_type=F32
            )
    left = combined[:share]
    right = combined[share:]
    part[...] = jnp.where(c == 0, right, left)
    part_copy = rcopy(part, partr, part_s, part_r, sib)
    part_copy.start()
    kept = jnp.where(c == 0, left, right)
    part_copy.wait_recv()
    out_ref[...] = (kept + partr[...]).astype(BF16)

    part_copy.wait_send()
    tok_copy.wait_send()
    for k in range(1, len(ROUTES)):
        disp_copy(k).wait_send()
        retc(k).wait_send()
    for i in range(NZ):
        if i > 0:
            gzc(i).wait_send()
        gyc(i, 0).wait_send()
        gyc(i, 1).wait_send()
        gfc(i).wait_send()

    def drain(s, carry):
        for way in range(2):
            yc(s, way).wait_send()
            fc(s, way).wait_send()
            hc(s, way).wait_send()
            wc(s, way).wait_send()
        for r in range(NY):
            bc(s, r).wait_send()
            sc(s, r).wait_send()
        q, i, zi = at_step(s)

        @pl.when(i > 0)
        def _():
            zc(q, i).wait_send()

        q, i = out_step(s)

        @pl.when(i > 0)
        def _():
            zzc(s).wait_send()

        return carry

    lax.fori_loop(0, STEPS, drain, 0)


def per_device(tokens, norm_gain, expert_ids, route_weights, gate_weight, up_weight, down_weight):
    vmem = pl.BlockSpec(memory_space=pltpu.VMEM)
    hbm = pl.BlockSpec(memory_space=pl.ANY)
    blocks = NY * NZ
    dma = pltpu.SemaphoreType.DMA
    scratch = [
        pltpu.VMEM((NZ, 2 * HID, NY * FEAT), BF16),
        pltpu.VMEM((blocks, HID, FEAT), BF16),
        pltpu.VMEM((CHUNKS, blocks, 2, ROWS, FEAT), BF16),
        pltpu.VMEM((2 * ROWS, NY * FEAT), BF16),
        pltpu.VMEM((2 * HID, 2 * ROWS), F32),
        pltpu.VMEM((2 * ROWS, 128), F32),
        pltpu.VMEM((CHUNKS, 2, ROWS, HID), BF16),
        pltpu.VMEM((NY, NZ, 16, 128), BF16),
        pltpu.VMEM((2, GROUP), jnp.int32),
        pltpu.VMEM((2, GROUP), F32),
        pltpu.VMEM((FEAT // 2 + 16, GROUP), BF16),
        pltpu.VMEM((FEAT // 2 + 16, GROUP), BF16),
        pltpu.VMEM((len(ROUTES), HALF, FEAT), BF16),
        pltpu.VMEM((STEPS, NY, ROWS, FEAT), BF16),
        pltpu.VMEM((STEPS, NY, ROWS, FEAT), BF16),
        pltpu.VMEM((STEPS, NY, ROWS, FEAT), BF16),
        pltpu.VMEM((STEPS, 2, ROWS // 2, FEAT), BF16),
        pltpu.VMEM((STEPS, 2, ROWS, FEAT), BF16),
        pltpu.VMEM((CHUNKS, NZ, ROWS, FEAT), BF16),
        pltpu.VMEM((len(ROUTES), HALF, FEAT), BF16),
        pltpu.VMEM((FEAT // 2, GROUP), F32),
        pltpu.VMEM((FEAT // 2, GROUP), F32),
        dma((3 + 2 * blocks,)), dma((blocks,)),
        dma, dma, dma((len(ROUTES),)), dma((len(ROUTES),)),
        dma((NZ,)), dma((NZ,)), dma((NZ, 2)), dma((NZ, 2)), dma((NZ,)), dma((NZ,)),
        dma((CHUNKS, NZ)), dma((CHUNKS, NZ)), dma((STEPS, 2)), dma((STEPS, 2)),
        dma((STEPS, 2)), dma((STEPS, 2)), dma((STEPS, NY)), dma((STEPS, NY)),
        dma((STEPS, NY)), dma((STEPS, NY)), dma((STEPS, 2)), dma((STEPS, 2)),
        dma((STEPS, 2)), dma((STEPS, 2)), dma((CHUNKS, NZ)), dma((CHUNKS, NZ)),
        dma((len(ROUTES),)), dma((len(ROUTES),)), dma, dma,
    ]
    rows = CHUNKS * 2 * ROWS
    out = pl.pallas_call(
        kernel,
        out_shape=jax.ShapeDtypeStruct((FEAT // 2, GROUP), BF16),
        in_specs=[hbm, vmem, hbm, hbm, hbm, hbm, hbm],
        out_specs=vmem,
        scratch_shapes=scratch,
        cost_estimate=pl.CostEstimate(
            flops=6 * rows * D * HID, bytes_accessed=6 * D * HID, transcendentals=rows * HID
        ),
        compiler_params=pltpu.CompilerParams(
            collective_id=0, has_side_effects=True, vmem_limit_bytes=61 * 1024 * 1024
        ),
    )(
        tokens.T,
        norm_gain,
        expert_ids.T,
        route_weights.T,
        gate_weight.swapaxes(1, 2),
        up_weight.swapaxes(1, 2),
        down_weight,
    )
    return out.T


def solution(mesh):
    placed = (
        P(("expert", "dp"), "tensor"),
        P("tensor"),
        P(("expert", "dp"), None),
        P(("expert", "dp"), None),
        P(("expert", "dp"), None, "tensor"),
        P(("expert", "dp"), None, "tensor"),
        P(("expert", "dp"), "tensor", None),
    )
    return jax.shard_map(
        per_device,
        mesh=mesh,
        in_specs=placed,
        out_specs=P(("expert", "dp"), "tensor"),
        check_vma=False,
    )
```

```python
import jax
import jax.numpy as jnp
from jax import lax
from jax.experimental import pallas as pl
from jax.experimental.pallas import tpu as pltpu
from jax.sharding import PartitionSpec as P

D = 6144
NORM_EPS = 1e-05
MESH = pl.DeviceIdType.MESH
NX, NY, NZ, ND = 4, 4, 4, 2
GROUP = 256
CAP = 128
HALF = CAP // 2
FEAT = 384
HID = 352
ROUTES = ((0, 0), (1, 0), (0, 1), (1, 1), (2, 1), (3, 1), (2, 0), (3, 0))
PER = 2
CHUNKS = len(ROUTES) // PER
ROWS = PER * HALF
STEPS = CHUNKS * NZ
SECOND, THIRD, MULTIPLY = 2, 4, 5
FARTHEST, NEIGHBOURS, FINISH = 1, 3, 5
DRAIN_GATHER, DRAIN_REDUCE, COMBINE = 8, 7, 2
LAG = NZ + MULTIPLY
F32 = jnp.float32
BF16 = jnp.bfloat16


def xor4(a, b):
    low = lax.rem(lax.rem(a, 2) + lax.rem(b, 2), 2)
    high = lax.rem(lax.div(a, 2) + lax.div(b, 2), 2)
    return low + 2 * high


def kernel(
    tok_hbm, gain_ref, ids_hbm, rw_hbm, wg_hbm, wu_hbm, wd_hbm,
    out_ref,
    wgu, wd, x, scaled, acc, sq, hid, gains,
    ids_ref, rw_ref, tokx, sibtok, stage, mine, given, srecv, halves, fulls, zrecv, ret, comb, part, partr,
    wsem, dsem, tok_s, tok_r, disp_s, disp_r, gz_s, gz_r, gy_s, gy_r, gf_s, gf_r,
    z_s, z_r, y_s, y_r, f_s, f_r, b_s, b_r,
    sib_s, sib_r, h_s, h_r, w_s, w_r, zz_s, zz_r, ret_s, ret_r, part_s, part_r,
):
    xi = lax.axis_index("expert")
    di = lax.axis_index("dp")
    me = lax.axis_index("tensor")
    c = lax.rem(me, 2)
    z = lax.rem(lax.div(me, 2), NZ)
    y = lax.div(me, 2 * NZ)
    own = y * NZ + z
    yp = lax.rem(y + 1, NY)
    ym = lax.rem(y + NY - 1, NY)

    def tid(yy, zz, cc):
        return (yy * NZ + zz) * 2 + cc

    sib = {"tensor": tid(y, z, 1 - c)}
    up = {"tensor": tid(yp, z, c)}
    down = {"tensor": tid(ym, z, c)}

    def zdev(i):
        return {"tensor": tid(y, xor4(z, i), c)}

    def expert_of(k):
        dx, dd = ROUTES[k]
        return {"expert": lax.rem(xi + dx, NX), "dp": lax.rem(di + dd, ND)}

    def group_of(k):
        dx, dd = ROUTES[k]
        return {"expert": lax.rem(xi + NX - dx, NX), "dp": lax.rem(di + dd, ND)}

    def rcopy(src, dst, ssem, rsem, dev):
        return pltpu.make_async_remote_copy(
            src_ref=src, dst_ref=dst, send_sem=ssem, recv_sem=rsem, device_id=dev, device_id_type=MESH
        )

    barrier = pltpu.get_barrier_semaphore()
    partners = [sib, up, down] + [zdev(i) for i in range(1, NZ)] + [expert_of(k) for k in range(1, len(ROUTES))]
    for dev in partners:
        pl.semaphore_signal(barrier, inc=1, device_id=dev, device_id_type=MESH)

    share = FEAT // 2
    small = [
        pltpu.make_async_copy(ids_hbm, ids_ref, wsem.at[0]),
        pltpu.make_async_copy(tok_hbm, tokx.at[pl.ds(0, share)], wsem.at[1]),
        pltpu.make_async_copy(rw_hbm, rw_ref, wsem.at[2]),
    ]
    for load in small:
        load.start()
    tokx[share:, :] = jnp.zeros((16, GROUP), BF16)
    tokx[share:, 0:share] = jnp.broadcast_to(gain_ref[...].astype(F32).reshape(1, share), (16, share)).astype(BF16)

    before = (
        lax.broadcasted_iota(jnp.int32, (GROUP, GROUP), 0) < lax.broadcasted_iota(jnp.int32, (GROUP, GROUP), 1)
    ).astype(F32).astype(BF16)
    labels = lax.broadcasted_iota(jnp.int32, (16, GROUP), 0)
    spot = lax.broadcasted_iota(jnp.int32, (HALF, 1), 0) + HALF * c
    place = []
    for k in range(len(ROUTES)):
        dev = expert_of(k)
        place.append(spot + (dev["expert"] * ND + dev["dp"]) * CAP)
    place = jnp.concatenate(place, axis=0)
    small[0].wait()
    e0 = ids_ref[0:1, :]
    e1 = ids_ref[1:2, :]
    hit0 = (e0 == labels).astype(F32)
    hit1 = (e1 == labels).astype(F32)
    earlier = jnp.dot((hit0 + hit1).astype(BF16), before, preferred_element_type=F32)
    slot0 = jnp.sum(earlier * hit0, axis=0, keepdims=True).astype(jnp.int32)
    slot1 = jnp.sum(earlier * hit1, axis=0, keepdims=True).astype(jnp.int32)
    dest0 = e0 * CAP + slot0
    dest1 = e1 * CAP + slot1
    small[1].wait()

    pl.semaphore_wait(barrier, len(partners))

    tok_copy = rcopy(tokx, sibtok, tok_s, tok_r, sib)
    tok_copy.start()
    select = ((place == dest0) | (place == dest1)).astype(F32).astype(BF16)

    loads = []
    for zz in range(NZ):
        for yy in range(NY):
            for k, source in enumerate((wg_hbm, wu_hbm)):
                loads.append(
                    pltpu.make_async_copy(
                        source.at[0, :, pl.ds((yy * NZ + zz) * FEAT, FEAT)],
                        wgu.at[zz, pl.ds(k * HID, HID), pl.ds(yy * FEAT, FEAT)],
                        wsem.at[3 + len(loads)],
                    )
                )
    dloads = [
        pltpu.make_async_copy(wd_hbm.at[0, :, pl.ds(j * FEAT, FEAT)], wd.at[j], dsem.at[j])
        for j in range(NY * NZ)
    ]

    tok_copy.wait_recv()
    here = tokx[...].astype(F32)
    there = sibtok[...].astype(F32)
    first_core = jnp.where(c == 0, here, there)
    second_core = jnp.where(c == 0, there, here)
    both = jnp.concatenate([first_core[:share], second_core[:share]], axis=0).astype(BF16)
    rows = lax.dot_general(
        select, both, (((1,), (1,)), ((), ())), preferred_element_type=F32
    ).astype(BF16)
    x[0, own, c, 0:HALF, :] = rows[0:HALF]

    def disp_copy(k):
        target = x.at[k // PER, own, c, pl.ds((k % PER) * HALF, HALF)]
        return rcopy(stage.at[k], target, disp_s.at[k], disp_r.at[k], expert_of(k))

    for k in range(1, len(ROUTES)):
        stage[k] = rows[k * HALF : (k + 1) * HALF]
        disp_copy(k).start()

    gain_row = jnp.concatenate(
        [first_core[share : share + 1, 0:share], second_core[share : share + 1, 0:share]], axis=1
    )
    index = lax.broadcasted_iota(jnp.int32, (16, 128), 0)
    tile = jnp.zeros((16, 128), F32)
    for j in range(3):
        tile = jnp.where(index == j, jnp.broadcast_to(gain_row[:, 128 * j : 128 * (j + 1)], (16, 128)), tile)
    gains[y, z] = tile.astype(BF16)

    def gzc(i):
        return rcopy(gains.at[y, z], gains.at[y, z], gz_s.at[i], gz_r.at[i], zdev(i))

    def gyc(i, way):
        ref = gains.at[y, xor4(z, i)]
        return rcopy(ref, ref, gy_s.at[i, way], gy_r.at[i, way], (up, down)[way])

    def gfc(i):
        ref = gains.at[ym, xor4(z, i)]
        return rcopy(ref, ref, gf_s.at[i], gf_r.at[i], up)

    for i in range(1, NZ):
        gzc(i).start()

    def at_step(s):
        q = lax.div(s, NZ)
        i = lax.rem(s, NZ)
        return q, i, xor4(z, i)

    def zc(q, i):
        return rcopy(x.at[q, own, c], x.at[q, own, c], z_s.at[q, i], z_r.at[q, i], zdev(i))

    def yc(s, way):
        q, i, zi = at_step(s)
        b = y * NZ + zi
        return rcopy(x.at[q, b, c], x.at[q, b, c], y_s.at[s, way], y_r.at[s, way], (up, down)[way])

    def fc(s, way):
        q, i, zi = at_step(s)
        b = (ym, yp)[way] * NZ + zi
        ref = x.at[q, b, c, pl.ds(way * (ROWS // 2), ROWS // 2)]
        return rcopy(ref, ref, f_s.at[s, way], f_r.at[s, way], (up, down)[way])

    def bc(s, r):
        q, i, zi = at_step(s)
        b = lax.rem(y + r, NY) * NZ + zi
        return rcopy(x.at[q, b, c], x.at[q, b, c], b_s.at[s, r], b_r.at[s, r], sib)

    def open_chunk(chunk):
        for k in range(max(1, chunk * PER), (chunk + 1) * PER):
            disp_copy(k).wait_recv()
        for j in range(1, NZ):
            zc(chunk, j).start()

    def first(s):
        q, i, zi = at_step(s)

        @pl.when(i > 0)
        def _():
            zc(q, i).wait_recv()

        yc(s, 0).start()
        yc(s, 1).start()
        bc(s, 0).start()

        @pl.when((s > 0) & (s < NZ))
        def _():
            gzc(i).wait_recv()

        @pl.when(s < NZ)
        def _():
            gyc(i, 0).start()
            gyc(i, 1).start()

        for chunk in range(1, CHUNKS):

            @pl.when(s == chunk * NZ - 1)
            def _():
                open_chunk(chunk)

    def second(s):
        q, i, zi = at_step(s)
        yc(s, 0).wait_recv()
        fc(s, 0).start()
        yc(s, 1).wait_recv()
        fc(s, 1).start()
        bc(s, 3).start()
        bc(s, 1).start()

        @pl.when(s < NZ)
        def _():
            gyc(i, 0).wait_recv()
            gfc(i).start()
            gyc(i, 1).wait_recv()

    def third(s):
        q, i, zi = at_step(s)
        fc(s, 0).wait_recv()
        fc(s, 1).wait_recv()
        bc(s, 2).start()

        @pl.when(s < NZ)
        def _():
            gfc(i).wait_recv()

    def gate_up(s):
        q, i, zi = at_step(s)
        for r in range(NY):
            bc(s, r).wait_recv()
        squares = sq[...]
        for yy in range(NY):
            block = x[q, yy * NZ + zi].reshape(2 * ROWS, FEAT)
            gain = gains[yy, zi].astype(F32)
            for j in range(3):
                slab = block[:, 128 * j : 128 * (j + 1)].astype(F32)
                squares = squares + slab * slab
                at = yy * FEAT + 128 * j
                scaled[:, at : at + 128] = (slab * gain[j : j + 1, :]).astype(BF16)
        sq[...] = squares
        acc[...] += lax.dot_general(
            wgu[zi], scaled[...], (((1,), (1,)), ((), ())), preferred_element_type=F32
        )

        @pl.when(i == NZ - 1)
        def _():
            total = jnp.sum(jnp.transpose(sq[...]), axis=0, keepdims=True)
            scale = lax.rsqrt(total / D + NORM_EPS)
            gate = acc[0:HID, :] * scale
            lift = acc[HID:, :] * scale
            value = jnp.transpose(gate / (1.0 + jnp.exp(-gate)) * lift).astype(BF16)
            for h in range(2):
                hid[q, lax.rem(c + h, 2)] = value[h * ROWS : (h + 1) * ROWS]
            acc[...] = jnp.zeros_like(acc)
            sq[...] = jnp.zeros_like(sq)

    def out_step(s):
        return lax.div(s, NZ), (NZ - 1) - lax.rem(s, NZ)

    def sc(s, r):
        return rcopy(given.at[s, r], srecv.at[s, r], sib_s.at[s, r], sib_r.at[s, r], sib)

    def hc(s, way):
        span = pl.ds(way * (ROWS // 2), ROWS // 2)
        return rcopy(mine.at[s, 2, span], halves.at[s, way], h_s.at[s, way], h_r.at[s, way], (up, down)[way])

    def wc(s, way):
        return rcopy(mine.at[s, (1, 3)[way]], fulls.at[s, way], w_s.at[s, way], w_r.at[s, way], (up, down)[way])

    def zzc(s):
        q, i = out_step(s)
        return rcopy(mine.at[s, 0], zrecv.at[q, i], zz_s.at[q, i], zz_r.at[q, i], zdev(i))

    def retc(k):
        source = mine.at[k // PER * NZ + NZ - 1, 0, pl.ds((k % PER) * HALF, HALF)]
        return rcopy(source, ret.at[k], ret_s.at[k], ret_r.at[k], group_of(k))

    def produce(s):
        q, i = out_step(s)
        zi = xor4(z, i)
        left = hid[q].reshape(2 * ROWS, HID)
        for r in (2, 1, 3, 0):
            b = lax.rem(y + r, NY) * NZ + zi
            block = jnp.dot(left, wd[b], preferred_element_type=F32).astype(BF16)
            given[s, r] = block[ROWS:]
            sc(s, r).start()
            mine[s, r] = block[:ROWS]

    def chip_sum(s, r):
        sc(s, r).wait_recv()
        return mine[s, r].astype(F32) + srecv[s, r].astype(F32)

    def farthest(s):
        mine[s, 2] = chip_sum(s, 2).astype(BF16)
        hc(s, 0).start()
        hc(s, 1).start()

    def neighbours(s):
        half = ROWS // 2
        total = chip_sum(s, 1)
        hc(s, 0).wait_recv()
        total = jnp.concatenate([total[:half] + halves[s, 0].astype(F32), total[half:]], axis=0)
        mine[s, 1] = total.astype(BF16)
        wc(s, 0).start()
        total = chip_sum(s, 3)
        hc(s, 1).wait_recv()
        total = jnp.concatenate([total[:half], total[half:] + halves[s, 1].astype(F32)], axis=0)
        mine[s, 3] = total.astype(BF16)
        wc(s, 1).start()

    def finish(s):
        q, i = out_step(s)
        total = chip_sum(s, 0)
        wc(s, 0).wait_recv()
        total = total + fulls[s, 0].astype(F32)
        wc(s, 1).wait_recv()
        total = total + fulls[s, 1].astype(F32)

        @pl.when(i > 0)
        def _():
            mine[s, 0] = total.astype(BF16)
            zzc(s).start()

        @pl.when(i == 0)
        def _():
            whole = total
            for j in range(1, NZ):
                zzc(s - j).wait_recv()
                whole = whole + zrecv[q, j].astype(F32)
            whole = whole.astype(BF16)
            mine[s, 0] = whole

            @pl.when(q == 0)
            def _():
                ret[0] = whole[0:HALF]

            for chunk in range(CHUNKS):

                @pl.when(q == chunk)
                def _():
                    for k in range(max(1, chunk * PER), (chunk + 1) * PER):
                        retc(k).start()

    def drain_gather(s):
        q, i, zi = at_step(s)
        for way in range(2):
            yc(s, way).wait_send()
            fc(s, way).wait_send()
        for r in range(NY):
            bc(s, r).wait_send()

        @pl.when(i > 0)
        def _():
            zc(q, i).wait_send()

    def drain_reduce(s):
        q, i = out_step(s)
        for way in range(2):
            hc(s, way).wait_send()
            wc(s, way).wait_send()
        for r in range(NY):
            sc(s, r).wait_send()

        @pl.when(i > 0)
        def _():
            zzc(s).wait_send()

    def combine(chunk):
        for k in range(max(1, chunk * PER), (chunk + 1) * PER):
            retc(k).wait_recv()
        came = ret[chunk * PER : (chunk + 1) * PER].reshape(ROWS, FEAT)
        spots = place[chunk * ROWS : (chunk + 1) * ROWS]
        total = comb[...]
        for k, dest in enumerate((dest0, dest1)):
            pick = (spots == dest).astype(F32).astype(BF16)
            total += rw_ref[k : k + 1, :] * lax.dot_general(
                came, pick, (((0,), (0,)), ((), ())), preferred_element_type=F32
            )
        return total

    def step(t, carry):
        u = t - LAG
        stages = (
            (first, t, 0), (second, t, SECOND), (third, t, THIRD),
            (finish, u, FINISH), (neighbours, u, NEIGHBOURS), (farthest, u, FARTHEST),
        )

        def run(stages):
            for stage_of, now, behind in stages:

                @pl.when((now >= behind) & (now < STEPS + behind))
                def _():
                    stage_of(now - behind)

        run(stages)

        @pl.when(t == MULTIPLY)
        def _():
            for load in loads + dloads:
                load.wait()

        run(((gate_up, t, MULTIPLY), (produce, u, 0)))
        run(((drain_gather, t, DRAIN_GATHER), (drain_reduce, u, DRAIN_REDUCE)))

        for chunk in range(CHUNKS - 1):

            @pl.when(u == chunk * NZ + NZ - 1 + FINISH + COMBINE)
            def _():
                comb[...] = combine(chunk)

        return carry

    open_chunk(0)
    first(jnp.int32(0))
    for load in loads + dloads:
        load.start()
    acc[...] = jnp.zeros_like(acc)
    sq[...] = jnp.zeros_like(sq)
    comb[...] = jnp.zeros_like(comb)
    small[2].wait()
    lax.fori_loop(1, LAG + STEPS + FINISH, step, 0)

    combined = combine(CHUNKS - 1)
    left = combined[:share]
    right = combined[share:]
    part[...] = jnp.where(c == 0, right, left)
    part_copy = rcopy(part, partr, part_s, part_r, sib)
    part_copy.start()
    kept = jnp.where(c == 0, left, right)
    part_copy.wait_recv()
    out_ref[...] = (kept + partr[...]).astype(BF16)

    part_copy.wait_send()
    tok_copy.wait_send()
    for k in range(1, len(ROUTES)):
        disp_copy(k).wait_send()
        retc(k).wait_send()
    for i in range(NZ):
        if i > 0:
            gzc(i).wait_send()
        gyc(i, 0).wait_send()
        gyc(i, 1).wait_send()
        gfc(i).wait_send()

    for s in range(STEPS + FINISH - DRAIN_REDUCE, STEPS):
        drain_reduce(jnp.int32(s))


def per_device(tokens, norm_gain, expert_ids, route_weights, gate_weight, up_weight, down_weight):
    vmem = pl.BlockSpec(memory_space=pltpu.VMEM)
    hbm = pl.BlockSpec(memory_space=pl.ANY)
    blocks = NY * NZ
    dma = pltpu.SemaphoreType.DMA
    scratch = [
        pltpu.VMEM((NZ, 2 * HID, NY * FEAT), BF16),
        pltpu.VMEM((blocks, HID, FEAT), BF16),
        pltpu.VMEM((CHUNKS, blocks, 2, ROWS, FEAT), BF16),
        pltpu.VMEM((2 * ROWS, NY * FEAT), BF16),
        pltpu.VMEM((2 * HID, 2 * ROWS), F32),
        pltpu.VMEM((2 * ROWS, 128), F32),
        pltpu.VMEM((CHUNKS, 2, ROWS, HID), BF16),
        pltpu.VMEM((NY, NZ, 16, 128), BF16),
        pltpu.VMEM((2, GROUP), jnp.int32),
        pltpu.VMEM((2, GROUP), F32),
        pltpu.VMEM((FEAT // 2 + 16, GROUP), BF16),
        pltpu.VMEM((FEAT // 2 + 16, GROUP), BF16),
        pltpu.VMEM((len(ROUTES), HALF, FEAT), BF16),
        pltpu.VMEM((STEPS, NY, ROWS, FEAT), BF16),
        pltpu.VMEM((STEPS, NY, ROWS, FEAT), BF16),
        pltpu.VMEM((STEPS, NY, ROWS, FEAT), BF16),
        pltpu.VMEM((STEPS, 2, ROWS // 2, FEAT), BF16),
        pltpu.VMEM((STEPS, 2, ROWS, FEAT), BF16),
        pltpu.VMEM((CHUNKS, NZ, ROWS, FEAT), BF16),
        pltpu.VMEM((len(ROUTES), HALF, FEAT), BF16),
        pltpu.VMEM((FEAT, GROUP), F32),
        pltpu.VMEM((FEAT // 2, GROUP), F32),
        pltpu.VMEM((FEAT // 2, GROUP), F32),
        dma((3 + 2 * blocks,)), dma((blocks,)),
        dma, dma, dma((len(ROUTES),)), dma((len(ROUTES),)),
        dma((NZ,)), dma((NZ,)), dma((NZ, 2)), dma((NZ, 2)), dma((NZ,)), dma((NZ,)),
        dma((CHUNKS, NZ)), dma((CHUNKS, NZ)), dma((STEPS, 2)), dma((STEPS, 2)),
        dma((STEPS, 2)), dma((STEPS, 2)), dma((STEPS, NY)), dma((STEPS, NY)),
        dma((STEPS, NY)), dma((STEPS, NY)), dma((STEPS, 2)), dma((STEPS, 2)),
        dma((STEPS, 2)), dma((STEPS, 2)), dma((CHUNKS, NZ)), dma((CHUNKS, NZ)),
        dma((len(ROUTES),)), dma((len(ROUTES),)), dma, dma,
    ]
    rows = CHUNKS * 2 * ROWS
    out = pl.pallas_call(
        kernel,
        out_shape=jax.ShapeDtypeStruct((FEAT // 2, GROUP), BF16),
        in_specs=[hbm, vmem, hbm, hbm, hbm, hbm, hbm],
        out_specs=vmem,
        scratch_shapes=scratch,
        cost_estimate=pl.CostEstimate(
            flops=6 * rows * D * HID, bytes_accessed=6 * D * HID, transcendentals=rows * HID
        ),
        compiler_params=pltpu.CompilerParams(
            collective_id=0, has_side_effects=True, vmem_limit_bytes=61 * 1024 * 1024
        ),
    )(
        tokens.T,
        norm_gain,
        expert_ids.T,
        route_weights.T,
        gate_weight.swapaxes(1, 2),
        up_weight.swapaxes(1, 2),
        down_weight,
    )
    return out.T


def solution(mesh):
    placed = (
        P(("expert", "dp"), "tensor"),
        P("tensor"),
        P(("expert", "dp"), None),
        P(("expert", "dp"), None),
        P(("expert", "dp"), None, "tensor"),
        P(("expert", "dp"), None, "tensor"),
        P(("expert", "dp"), "tensor", None),
    )
    return jax.shard_map(
        per_device,
        mesh=mesh,
        in_specs=placed,
        out_specs=P(("expert", "dp"), "tensor"),
        check_vma=False,
    )
```

```python
import jax
import jax.numpy as jnp
from jax import lax
from jax.experimental import pallas as pl
from jax.experimental.pallas import tpu as pltpu
from jax.sharding import PartitionSpec as P

D = 6144
NORM_EPS = 1e-05
MESH = pl.DeviceIdType.MESH
NX, NY, NZ, ND = 4, 4, 4, 2
GROUP = 256
CAP = 128
HALF = CAP // 2
FEAT = 384
HID = 352
ROUTES = ((0, 0), (1, 0), (0, 1), (1, 1), (2, 1), (3, 1), (2, 0), (3, 0))
PER = 2
CHUNKS = len(ROUTES) // PER
ROWS = PER * HALF
FAR = tuple(k for k in range(len(ROUTES)) if ROUTES[k][1] == 1)
HANDED = 1
STEPS = CHUNKS * NZ
SECOND, THIRD, MULTIPLY = 2, 4, 5
FARTHEST, NEIGHBOURS, FINISH = 1, 3, 5
DRAIN_GATHER, DRAIN_REDUCE, COMBINE = 8, 7, 3
LAG = NZ + MULTIPLY
F32 = jnp.float32
BF16 = jnp.bfloat16


def xor4(a, b):
    low = lax.rem(lax.rem(a, 2) + lax.rem(b, 2), 2)
    high = lax.rem(lax.div(a, 2) + lax.div(b, 2), 2)
    return low + 2 * high


def kernel(
    tok_hbm, gain_ref, ids_hbm, rw_hbm, wg_hbm, wu_hbm, wd_hbm,
    out_ref,
    wgu, wd, x, scaled, acc, sq, hid, gains,
    ids_ref, rw_ref, tokx, sibtok, stage, relay, back, farin, mine, given, srecv, halves, fulls, zrecv, ret, comb, part, partr,
    wsem, dsem, tok_s, tok_r, disp_s, disp_r, gz_s, gz_r, gy_s, gy_r, gf_s, gf_r,
    z_s, z_r, y_s, y_r, f_s, f_r, b_s, b_r,
    fz_s, fz_r, fr_s, fr_r, rel_s, rel_r, back_s, back_r,
    sib_s, sib_r, h_s, h_r, w_s, w_r, zz_s, zz_r, ret_s, ret_r, part_s, part_r,
):
    xi = lax.axis_index("expert")
    di = lax.axis_index("dp")
    me = lax.axis_index("tensor")
    c = lax.rem(me, 2)
    z = lax.rem(lax.div(me, 2), NZ)
    y = lax.div(me, 2 * NZ)
    own = y * NZ + z
    yp = lax.rem(y + 1, NY)
    ym = lax.rem(y + NY - 1, NY)

    def tid(yy, zz, cc):
        return (yy * NZ + zz) * 2 + cc

    sib = {"tensor": tid(y, z, 1 - c)}
    up = {"tensor": tid(yp, z, c)}
    down = {"tensor": tid(ym, z, c)}

    def zdev(i):
        return {"tensor": tid(y, xor4(z, i), c)}

    def expert_of(k):
        dx, dd = ROUTES[k]
        return {"expert": lax.rem(xi + dx, NX), "dp": lax.rem(di + dd, ND)}

    def group_of(k):
        dx, dd = ROUTES[k]
        return {"expert": lax.rem(xi + NX - dx, NX), "dp": lax.rem(di + dd, ND)}

    def leg(dx, forward):
        spot = lax.rem(di * NZ + z + (2 + 4 * c if forward else 6 - 4 * c), ND * NZ)
        return {
            "expert": lax.rem(xi + dx + NX, NX),
            "tensor": tid(y, lax.rem(spot, NZ), c),
            "dp": lax.div(spot, NZ),
        }

    def rcopy(src, dst, ssem, rsem, dev):
        return pltpu.make_async_remote_copy(
            src_ref=src, dst_ref=dst, send_sem=ssem, recv_sem=rsem, device_id=dev, device_id_type=MESH
        )

    barrier = pltpu.get_barrier_semaphore()
    partners = [sib, up, down] + [zdev(i) for i in range(1, NZ)]
    partners += [expert_of(k) for k in range(1, len(ROUTES)) if k not in FAR]
    partners += [leg(dx, forward) for dx in range(NX) for forward in (True, False)]
    for dev in partners:
        pl.semaphore_signal(barrier, inc=1, device_id=dev, device_id_type=MESH)

    share = FEAT // 2
    small = [
        pltpu.make_async_copy(ids_hbm, ids_ref, wsem.at[0]),
        pltpu.make_async_copy(tok_hbm, tokx.at[pl.ds(0, share)], wsem.at[1]),
        pltpu.make_async_copy(rw_hbm, rw_ref, wsem.at[2]),
    ]
    for load in small:
        load.start()
    tokx[share:, :] = jnp.zeros((16, GROUP), BF16)
    tokx[share:, 0:share] = jnp.broadcast_to(gain_ref[...].astype(F32).reshape(1, share), (16, share)).astype(BF16)

    before = (
        lax.broadcasted_iota(jnp.int32, (GROUP, GROUP), 0) < lax.broadcasted_iota(jnp.int32, (GROUP, GROUP), 1)
    ).astype(F32).astype(BF16)
    labels = lax.broadcasted_iota(jnp.int32, (16, GROUP), 0)
    spot = lax.broadcasted_iota(jnp.int32, (HALF, 1), 0) + HALF * c
    place = []
    for k in range(len(ROUTES)):
        dev = expert_of(k)
        place.append(spot + (dev["expert"] * ND + dev["dp"]) * CAP)
    place = jnp.concatenate(place, axis=0)
    small[0].wait()
    e0 = ids_ref[0:1, :]
    e1 = ids_ref[1:2, :]
    hit0 = (e0 == labels).astype(F32)
    hit1 = (e1 == labels).astype(F32)
    earlier = jnp.dot((hit0 + hit1).astype(BF16), before, preferred_element_type=F32)
    slot0 = jnp.sum(earlier * hit0, axis=0, keepdims=True).astype(jnp.int32)
    slot1 = jnp.sum(earlier * hit1, axis=0, keepdims=True).astype(jnp.int32)
    dest0 = e0 * CAP + slot0
    dest1 = e1 * CAP + slot1
    small[1].wait()

    pl.semaphore_wait(barrier, len(partners))

    tok_copy = rcopy(tokx, sibtok, tok_s, tok_r, sib)
    tok_copy.start()
    select = ((place == dest0) | (place == dest1)).astype(F32).astype(BF16)

    loads = []
    for zz in range(NZ):
        for yy in range(NY):
            for k, source in enumerate((wg_hbm, wu_hbm)):
                loads.append(
                    pltpu.make_async_copy(
                        source.at[0, :, pl.ds((yy * NZ + zz) * FEAT, FEAT)],
                        wgu.at[zz, pl.ds(k * HID, HID), pl.ds(yy * FEAT, FEAT)],
                        wsem.at[3 + len(loads)],
                    )
                )
    dloads = [
        pltpu.make_async_copy(wd_hbm.at[0, :, pl.ds(j * FEAT, FEAT)], wd.at[j], dsem.at[j])
        for j in range(NY * NZ)
    ]

    tok_copy.wait_recv()
    here = tokx[...].astype(F32)
    there = sibtok[...].astype(F32)
    first_core = jnp.where(c == 0, here, there)
    second_core = jnp.where(c == 0, there, here)
    both = jnp.concatenate([first_core[:share], second_core[:share]], axis=0).astype(BF16)
    rows = lax.dot_general(
        select, both, (((1,), (1,)), ((), ())), preferred_element_type=F32
    ).astype(BF16)
    x[0, own, c, 0:HALF, :] = rows[0:HALF]

    def disp_copy(k):
        q, span = k // PER, pl.ds((k % PER) * HALF, HALF)
        if k in FAR:
            target = x.at[q, y * NZ + lax.rem(z + 2, NZ), c, span]
            return rcopy(relay.at[k - FAR[0]], target, disp_s.at[k], disp_r.at[k], leg(ROUTES[k][0], True))
        return rcopy(stage.at[k], x.at[q, own, c, span], disp_s.at[k], disp_r.at[k], expert_of(k))

    def relay_copy(part):
        first_k = FAR[0] + part * PER
        target = relay.at[pl.ds(part * PER, PER)]
        return rcopy(stage.at[pl.ds(first_k, PER)], target, rel_s.at[part], rel_r.at[part], leg(0, True))

    def relay_on(part):
        relay_copy(part).wait_recv()
        for k in range(FAR[0] + part * PER, FAR[0] + (part + 1) * PER):
            disp_copy(k).start()

    for k in range(1, len(ROUTES)):
        stage[k] = rows[k * HALF : (k + 1) * HALF]
        if k < PER:
            disp_copy(k).start()

    gain_row = jnp.concatenate(
        [first_core[share : share + 1, 0:share], second_core[share : share + 1, 0:share]], axis=1
    )
    index = lax.broadcasted_iota(jnp.int32, (16, 128), 0)
    tile = jnp.zeros((16, 128), F32)
    for j in range(3):
        tile = jnp.where(index == j, jnp.broadcast_to(gain_row[:, 128 * j : 128 * (j + 1)], (16, 128)), tile)
    gains[y, z] = tile.astype(BF16)

    def gzc(i):
        return rcopy(gains.at[y, z], gains.at[y, z], gz_s.at[i], gz_r.at[i], zdev(i))

    def gyc(i, way):
        ref = gains.at[y, xor4(z, i)]
        return rcopy(ref, ref, gy_s.at[i, way], gy_r.at[i, way], (up, down)[way])

    def gfc(i):
        ref = gains.at[ym, xor4(z, i)]
        return rcopy(ref, ref, gf_s.at[i], gf_r.at[i], up)

    for i in range(1, NZ):
        gzc(i).start()

    def at_step(s):
        q = lax.div(s, NZ)
        i = lax.rem(s, NZ)
        return q, i, xor4(z, i)

    def zc(q, i):
        return rcopy(x.at[q, own, c], x.at[q, own, c], z_s.at[q, i], z_r.at[q, i], zdev(i))

    def yc(s, way):
        q, i, zi = at_step(s)
        b = y * NZ + zi
        return rcopy(x.at[q, b, c], x.at[q, b, c], y_s.at[s, way], y_r.at[s, way], (up, down)[way])

    def fc(s, way):
        q, i, zi = at_step(s)
        b = (ym, yp)[way] * NZ + zi
        ref = x.at[q, b, c, pl.ds(way * (ROWS // 2), ROWS // 2)]
        return rcopy(ref, ref, f_s.at[s, way], f_r.at[s, way], (up, down)[way])

    def fzc(q):
        ref = x.at[q, lax.rem(y + 2, NY) * NZ + z, c]
        return rcopy(ref, ref, fz_s.at[q], fz_r.at[q], zdev(HANDED))

    def bc(s, r):
        q, i, zi = at_step(s)
        b = lax.rem(y + r, NY) * NZ + zi
        return rcopy(x.at[q, b, c], x.at[q, b, c], b_s.at[s, r], b_r.at[s, r], sib)

    def open_chunk(chunk):
        for k in range(max(1, chunk * PER), (chunk + 1) * PER):
            disp_copy(k).wait_recv()
        for j in range(1, NZ):
            zc(chunk, j).start()

    def first(s):
        q, i, zi = at_step(s)

        @pl.when(i > 0)
        def _():
            zc(q, i).wait_recv()

        yc(s, 0).start()
        yc(s, 1).start()
        bc(s, 0).start()

        @pl.when((s > 0) & (s < NZ))
        def _():
            gzc(i).wait_recv()

        @pl.when(s < NZ)
        def _():
            gyc(i, 0).start()
            gyc(i, 1).start()

        for chunk in range(1, CHUNKS):

            @pl.when(s == chunk * NZ - 1)
            def _():
                open_chunk(chunk)

    def second(s):
        q, i, zi = at_step(s)
        yc(s, 0).wait_recv()

        @pl.when(i != HANDED)
        def _():
            fc(s, 0).start()

        yc(s, 1).wait_recv()

        @pl.when(i != HANDED)
        def _():
            fc(s, 1).start()

        bc(s, 3).start()
        bc(s, 1).start()

        @pl.when(s < NZ)
        def _():
            gyc(i, 0).wait_recv()
            gfc(i).start()
            gyc(i, 1).wait_recv()

    def third(s):
        q, i, zi = at_step(s)
        @pl.when(i != HANDED)
        def _():
            fc(s, 0).wait_recv()
            fc(s, 1).wait_recv()

        @pl.when(i == 0)
        def _():
            fzc(q).start()

        @pl.when(i == HANDED)
        def _():
            fzc(q).wait_recv()

        bc(s, 2).start()

        @pl.when(s < NZ)
        def _():
            gfc(i).wait_recv()

    def gate_up(s):
        q, i, zi = at_step(s)
        for r in range(NY):
            bc(s, r).wait_recv()
        squares = sq[...]
        for yy in range(NY):
            block = x[q, yy * NZ + zi].reshape(2 * ROWS, FEAT)
            gain = gains[yy, zi].astype(F32)
            for j in range(3):
                slab = block[:, 128 * j : 128 * (j + 1)].astype(F32)
                squares = squares + slab * slab
                at = yy * FEAT + 128 * j
                scaled[:, at : at + 128] = (slab * gain[j : j + 1, :]).astype(BF16)
        sq[...] = squares
        acc[...] += lax.dot_general(
            wgu[zi], scaled[...], (((1,), (1,)), ((), ())), preferred_element_type=F32
        )

        @pl.when(i == NZ - 1)
        def _():
            total = jnp.sum(jnp.transpose(sq[...]), axis=0, keepdims=True)
            scale = lax.rsqrt(total / D + NORM_EPS)
            gate = acc[0:HID, :] * scale
            lift = acc[HID:, :] * scale
            value = jnp.transpose(gate / (1.0 + jnp.exp(-gate)) * lift).astype(BF16)
            for h in range(2):
                hid[q, lax.rem(c + h, 2)] = value[h * ROWS : (h + 1) * ROWS]
            acc[...] = jnp.zeros_like(acc)
            sq[...] = jnp.zeros_like(sq)

    def out_step(s):
        return lax.div(s, NZ), (NZ - 1) - lax.rem(s, NZ)

    def sc(s, r):
        return rcopy(given.at[s, r], srecv.at[s, r], sib_s.at[s, r], sib_r.at[s, r], sib)

    def hc(s, way):
        span = pl.ds(way * (ROWS // 2), ROWS // 2)
        return rcopy(mine.at[s, 2, span], halves.at[s, way], h_s.at[s, way], h_r.at[s, way], (up, down)[way])

    def wc(s, way):
        return rcopy(mine.at[s, (1, 3)[way]], fulls.at[s, way], w_s.at[s, way], w_r.at[s, way], (up, down)[way])

    def zzc(s):
        q, i = out_step(s)
        return rcopy(mine.at[s, 0], zrecv.at[q, i], zz_s.at[q, i], zz_r.at[q, i], zdev(i))

    def frc(s):
        q, i = out_step(s)
        return rcopy(mine.at[s, 2], farin.at[q], fr_s.at[q], fr_r.at[q], zdev(HANDED))

    def retc(k):
        chunk, span = k // PER, pl.ds((k % PER) * HALF, HALF)
        if k in FAR:
            source = back.at[chunk - FAR[0] // PER, span]
            return rcopy(source, ret.at[k], ret_s.at[k], ret_r.at[k], leg(-ROUTES[k][0], True))
        return rcopy(mine.at[chunk * NZ + NZ - 1, 0, span], ret.at[k], ret_s.at[k], ret_r.at[k], group_of(k))

    def back_copy(part):
        chunk = FAR[0] // PER + part
        return rcopy(mine.at[chunk * NZ + NZ - 1, 0], back.at[part], back_s.at[part], back_r.at[part], leg(0, True))

    def back_on(part):
        back_copy(part).wait_recv()
        for k in range(FAR[0] + part * PER, FAR[0] + (part + 1) * PER):
            retc(k).start()

    def produce(s):
        q, i = out_step(s)
        zi = xor4(z, i)
        left = hid[q].reshape(2 * ROWS, HID)
        for r in (2, 1, 3, 0):
            b = lax.rem(y + r, NY) * NZ + zi
            block = jnp.dot(left, wd[b], preferred_element_type=F32).astype(BF16)
            given[s, r] = block[ROWS:]
            sc(s, r).start()
            mine[s, r] = block[:ROWS]

    def chip_sum(s, r):
        sc(s, r).wait_recv()
        return mine[s, r].astype(F32) + srecv[s, r].astype(F32)

    def farthest(s):
        q, i = out_step(s)
        total = chip_sum(s, 2)

        @pl.when(i == HANDED)
        def _():
            mine[s, 2] = total.astype(BF16)
            frc(s).start()

        @pl.when(i == 0)
        def _():
            frc(s - 1).wait_recv()
            mine[s, 2] = (total + farin[q].astype(F32)).astype(BF16)

        @pl.when(i > HANDED)
        def _():
            mine[s, 2] = total.astype(BF16)

        @pl.when(i != HANDED)
        def _():
            hc(s, 0).start()
            hc(s, 1).start()

    def neighbours(s):
        q, i = out_step(s)
        half = ROWS // 2
        for way, r in enumerate((1, 3)):
            total = chip_sum(s, r)

            @pl.when(i == HANDED)
            def _():
                mine[s, r] = total.astype(BF16)

            @pl.when(i != HANDED)
            def _():
                hc(s, way).wait_recv()
                parts = [total[:half], total[half:]]
                parts[way] = parts[way] + halves[s, way].astype(F32)
                mine[s, r] = jnp.concatenate(parts, axis=0).astype(BF16)

            wc(s, way).start()

    def finish(s):
        q, i = out_step(s)
        total = chip_sum(s, 0)
        wc(s, 0).wait_recv()
        total = total + fulls[s, 0].astype(F32)
        wc(s, 1).wait_recv()
        total = total + fulls[s, 1].astype(F32)

        @pl.when(i > 0)
        def _():
            mine[s, 0] = total.astype(BF16)
            zzc(s).start()

        @pl.when(i == 0)
        def _():
            whole = total
            for j in range(1, NZ):
                zzc(s - j).wait_recv()
                whole = whole + zrecv[q, j].astype(F32)
            whole = whole.astype(BF16)
            mine[s, 0] = whole

            @pl.when(q == 0)
            def _():
                ret[0] = whole[0:HALF]

            for chunk in range(CHUNKS):

                @pl.when(q == chunk)
                def _():
                    if chunk * PER in FAR:
                        back_copy(chunk - FAR[0] // PER).start()
                    else:
                        for k in range(max(1, chunk * PER), (chunk + 1) * PER):
                            retc(k).start()

    def drain_gather(s):
        q, i, zi = at_step(s)
        for way in range(2):
            yc(s, way).wait_send()
        for r in range(NY):
            bc(s, r).wait_send()

        @pl.when(i != HANDED)
        def _():
            fc(s, 0).wait_send()
            fc(s, 1).wait_send()

        @pl.when(i == 0)
        def _():
            fzc(q).wait_send()

        @pl.when(i > 0)
        def _():
            zc(q, i).wait_send()

    def drain_reduce(s):
        q, i = out_step(s)
        for way in range(2):
            wc(s, way).wait_send()
        for r in range(NY):
            sc(s, r).wait_send()

        @pl.when(i != HANDED)
        def _():
            hc(s, 0).wait_send()
            hc(s, 1).wait_send()

        @pl.when(i == HANDED)
        def _():
            frc(s).wait_send()

        @pl.when(i > 0)
        def _():
            zzc(s).wait_send()

    def combine(chunk):
        for k in range(max(1, chunk * PER), (chunk + 1) * PER):
            retc(k).wait_recv()
        came = ret[chunk * PER : (chunk + 1) * PER].reshape(ROWS, FEAT)
        spots = place[chunk * ROWS : (chunk + 1) * ROWS]
        total = comb[...]
        for k, dest in enumerate((dest0, dest1)):
            pick = (spots == dest).astype(F32).astype(BF16)
            total += rw_ref[k : k + 1, :] * lax.dot_general(
                came, pick, (((0,), (0,)), ((), ())), preferred_element_type=F32
            )
        return total

    def step(t, carry):
        u = t - LAG
        stages = (
            (first, t, 0), (second, t, SECOND), (third, t, THIRD),
            (finish, u, FINISH), (neighbours, u, NEIGHBOURS), (farthest, u, FARTHEST),
        )

        def run(stages):
            for stage_of, now, behind in stages:

                @pl.when((now >= behind) & (now < STEPS + behind))
                def _():
                    stage_of(now - behind)

        run(stages)

        @pl.when(t == 1)
        def _():
            relay_copy(1).start()

        @pl.when(t == 2)
        def _():
            relay_on(0)

        @pl.when(t == 4)
        def _():
            relay_on(1)
            for k in range((CHUNKS - 1) * PER, CHUNKS * PER):
                disp_copy(k).start()

        for part in range(len(FAR) // PER):

            @pl.when(u == (FAR[0] // PER + part) * NZ + NZ + FINISH)
            def _():
                back_on(part)

        @pl.when(t == MULTIPLY)
        def _():
            for load in loads + dloads:
                load.wait()

        run(((gate_up, t, MULTIPLY), (produce, u, 0)))
        run(((drain_gather, t, DRAIN_GATHER), (drain_reduce, u, DRAIN_REDUCE)))

        for chunk in range(CHUNKS - 1):

            @pl.when(u == chunk * NZ + NZ - 1 + FINISH + COMBINE)
            def _():
                comb[...] = combine(chunk)

        return carry

    open_chunk(0)
    first(jnp.int32(0))
    relay_copy(0).start()
    for load in loads + dloads:
        load.start()
    acc[...] = jnp.zeros_like(acc)
    sq[...] = jnp.zeros_like(sq)
    comb[...] = jnp.zeros_like(comb)
    small[2].wait()
    lax.fori_loop(1, LAG + STEPS + FINISH, step, 0)

    combined = combine(CHUNKS - 1)
    left = combined[:share]
    right = combined[share:]
    part[...] = jnp.where(c == 0, right, left)
    part_copy = rcopy(part, partr, part_s, part_r, sib)
    part_copy.start()
    kept = jnp.where(c == 0, left, right)
    part_copy.wait_recv()
    out_ref[...] = (kept + partr[...]).astype(BF16)

    part_copy.wait_send()
    tok_copy.wait_send()
    for k in range(1, len(ROUTES)):
        disp_copy(k).wait_send()
        retc(k).wait_send()
    for part in range(len(FAR) // PER):
        relay_copy(part).wait_send()
        back_copy(part).wait_send()
    for i in range(NZ):
        if i > 0:
            gzc(i).wait_send()
        gyc(i, 0).wait_send()
        gyc(i, 1).wait_send()
        gfc(i).wait_send()

    for s in range(STEPS + FINISH - DRAIN_REDUCE, STEPS):
        drain_reduce(jnp.int32(s))


def per_device(tokens, norm_gain, expert_ids, route_weights, gate_weight, up_weight, down_weight):
    vmem = pl.BlockSpec(memory_space=pltpu.VMEM)
    hbm = pl.BlockSpec(memory_space=pl.ANY)
    blocks = NY * NZ
    dma = pltpu.SemaphoreType.DMA
    scratch = [
        pltpu.VMEM((NZ, 2 * HID, NY * FEAT), BF16),
        pltpu.VMEM((blocks, HID, FEAT), BF16),
        pltpu.VMEM((CHUNKS, blocks, 2, ROWS, FEAT), BF16),
        pltpu.VMEM((2 * ROWS, NY * FEAT), BF16),
        pltpu.VMEM((2 * HID, 2 * ROWS), F32),
        pltpu.VMEM((2 * ROWS, 128), F32),
        pltpu.VMEM((CHUNKS, 2, ROWS, HID), BF16),
        pltpu.VMEM((NY, NZ, 16, 128), BF16),
        pltpu.VMEM((2, GROUP), jnp.int32),
        pltpu.VMEM((2, GROUP), F32),
        pltpu.VMEM((FEAT // 2 + 16, GROUP), BF16),
        pltpu.VMEM((FEAT // 2 + 16, GROUP), BF16),
        pltpu.VMEM((len(ROUTES), HALF, FEAT), BF16),
        pltpu.VMEM((len(FAR), HALF, FEAT), BF16),
        pltpu.VMEM((len(FAR) // PER, ROWS, FEAT), BF16),
        pltpu.VMEM((CHUNKS, ROWS, FEAT), BF16),
        pltpu.VMEM((STEPS, NY, ROWS, FEAT), BF16),
        pltpu.VMEM((STEPS, NY, ROWS, FEAT), BF16),
        pltpu.VMEM((STEPS, NY, ROWS, FEAT), BF16),
        pltpu.VMEM((STEPS, 2, ROWS // 2, FEAT), BF16),
        pltpu.VMEM((STEPS, 2, ROWS, FEAT), BF16),
        pltpu.VMEM((CHUNKS, NZ, ROWS, FEAT), BF16),
        pltpu.VMEM((len(ROUTES), HALF, FEAT), BF16),
        pltpu.VMEM((FEAT, GROUP), F32),
        pltpu.VMEM((FEAT // 2, GROUP), F32),
        pltpu.VMEM((FEAT // 2, GROUP), F32),
        dma((3 + 2 * blocks,)), dma((blocks,)),
        dma, dma, dma((len(ROUTES),)), dma((len(ROUTES),)),
        dma((NZ,)), dma((NZ,)), dma((NZ, 2)), dma((NZ, 2)), dma((NZ,)), dma((NZ,)),
        dma((CHUNKS, NZ)), dma((CHUNKS, NZ)), dma((STEPS, 2)), dma((STEPS, 2)),
        dma((STEPS, 2)), dma((STEPS, 2)), dma((STEPS, NY)), dma((STEPS, NY)),
        dma((CHUNKS,)), dma((CHUNKS,)), dma((CHUNKS,)), dma((CHUNKS,)),
        dma((len(FAR) // PER,)), dma((len(FAR) // PER,)), dma((len(FAR) // PER,)), dma((len(FAR) // PER,)),
        dma((STEPS, NY)), dma((STEPS, NY)), dma((STEPS, 2)), dma((STEPS, 2)),
        dma((STEPS, 2)), dma((STEPS, 2)), dma((CHUNKS, NZ)), dma((CHUNKS, NZ)),
        dma((len(ROUTES),)), dma((len(ROUTES),)), dma, dma,
    ]
    rows = CHUNKS * 2 * ROWS
    out = pl.pallas_call(
        kernel,
        out_shape=jax.ShapeDtypeStruct((FEAT // 2, GROUP), BF16),
        in_specs=[hbm, vmem, hbm, hbm, hbm, hbm, hbm],
        out_specs=vmem,
        scratch_shapes=scratch,
        cost_estimate=pl.CostEstimate(
            flops=6 * rows * D * HID, bytes_accessed=6 * D * HID, transcendentals=rows * HID
        ),
        compiler_params=pltpu.CompilerParams(
            collective_id=0, has_side_effects=True, vmem_limit_bytes=61 * 1024 * 1024
        ),
    )(
        tokens.T,
        norm_gain,
        expert_ids.T,
        route_weights.T,
        gate_weight.swapaxes(1, 2),
        up_weight.swapaxes(1, 2),
        down_weight,
    )
    return out.T


def solution(mesh):
    placed = (
        P(("expert", "dp"), "tensor"),
        P("tensor"),
        P(("expert", "dp"), None),
        P(("expert", "dp"), None),
        P(("expert", "dp"), None, "tensor"),
        P(("expert", "dp"), None, "tensor"),
        P(("expert", "dp"), "tensor", None),
    )
    return jax.shard_map(
        per_device,
        mesh=mesh,
        in_specs=placed,
        out_specs=P(("expert", "dp"), "tensor"),
        check_vma=False,
    )
```

```python
import jax
import jax.numpy as jnp
from jax import lax
from jax.experimental import pallas as pl
from jax.experimental.pallas import tpu as pltpu
from jax.sharding import PartitionSpec as P

D = 6144
NORM_EPS = 1e-05
MESH = pl.DeviceIdType.MESH
NX, NY, NZ, ND = 4, 4, 4, 2
GROUP = 256
CAP = 128
HALF = CAP // 2
FEAT = 384
HID = 352
ROUTES = ((0, 0), (1, 0), (0, 1), (1, 1), (2, 1), (3, 1), (2, 0), (3, 0))
PER = 2
CHUNKS = len(ROUTES) // PER
ROWS = PER * HALF
FAR = tuple(k for k in range(len(ROUTES)) if ROUTES[k][1] == 1)
HANDED = 1
STEPS = CHUNKS * NZ
SECOND, THIRD, MULTIPLY = 2, 4, 5
NEIGHBOURS, FINISH = 2, 4
DRAIN_GATHER, DRAIN_REDUCE, COMBINE = 8, 6, 3
LAG = NZ + MULTIPLY
F32 = jnp.float32
BF16 = jnp.bfloat16


def xor4(a, b):
    low = lax.rem(lax.rem(a, 2) + lax.rem(b, 2), 2)
    high = lax.rem(lax.div(a, 2) + lax.div(b, 2), 2)
    return low + 2 * high


def kernel(
    tok_hbm, gain_ref, ids_hbm, rw_hbm, wg_hbm, wu_hbm, wd_hbm,
    out_ref,
    wgu, wd, wd2, x, scaled, acc, sq, hid, hidout, hidin, gains,
    ids_ref, rw_ref, tokx, sibtok, stage, relay, back, farin, mine, halves, fulls, zrecv, ret, comb, part, partr,
    wsem, dsem, tok_s, tok_r, disp_s, disp_r, gz_s, gz_r, gy_s, gy_r, gf_s, gf_r,
    z_s, z_r, y_s, y_r, f_s, f_r, b_s, b_r,
    fz_s, fz_r, fr_s, fr_r, rel_s, rel_r, back_s, back_r,
    wd2_s, wd2_r, hid_s, hid_r, h_s, h_r, w_s, w_r, zz_s, zz_r, ret_s, ret_r, part_s, part_r,
):
    xi = lax.axis_index("expert")
    di = lax.axis_index("dp")
    me = lax.axis_index("tensor")
    c = lax.rem(me, 2)
    z = lax.rem(lax.div(me, 2), NZ)
    y = lax.div(me, 2 * NZ)
    own = y * NZ + z
    yp = lax.rem(y + 1, NY)
    ym = lax.rem(y + NY - 1, NY)

    def tid(yy, zz, cc):
        return (yy * NZ + zz) * 2 + cc

    sib = {"tensor": tid(y, z, 1 - c)}
    up = {"tensor": tid(yp, z, c)}
    down = {"tensor": tid(ym, z, c)}

    def zdev(i):
        return {"tensor": tid(y, xor4(z, i), c)}

    def expert_of(k):
        dx, dd = ROUTES[k]
        return {"expert": lax.rem(xi + dx, NX), "dp": lax.rem(di + dd, ND)}

    def group_of(k):
        dx, dd = ROUTES[k]
        return {"expert": lax.rem(xi + NX - dx, NX), "dp": lax.rem(di + dd, ND)}

    def leg(dx, forward):
        spot = lax.rem(di * NZ + z + (2 + 4 * c if forward else 6 - 4 * c), ND * NZ)
        return {
            "expert": lax.rem(xi + dx + NX, NX),
            "tensor": tid(y, lax.rem(spot, NZ), c),
            "dp": lax.div(spot, NZ),
        }

    def rcopy(src, dst, ssem, rsem, dev):
        return pltpu.make_async_remote_copy(
            src_ref=src, dst_ref=dst, send_sem=ssem, recv_sem=rsem, device_id=dev, device_id_type=MESH
        )

    barrier = pltpu.get_barrier_semaphore()
    partners = [sib, up, down] + [zdev(i) for i in range(1, NZ)]
    partners += [expert_of(k) for k in range(1, len(ROUTES)) if k not in FAR]
    partners += [leg(dx, forward) for dx in range(NX) for forward in (True, False)]
    for dev in partners:
        pl.semaphore_signal(barrier, inc=1, device_id=dev, device_id_type=MESH)

    share = FEAT // 2
    small = [
        pltpu.make_async_copy(ids_hbm, ids_ref, wsem.at[0]),
        pltpu.make_async_copy(tok_hbm, tokx.at[pl.ds(0, share)], wsem.at[1]),
        pltpu.make_async_copy(rw_hbm, rw_ref, wsem.at[2]),
    ]
    for load in small:
        load.start()
    tokx[share:, :] = jnp.zeros((16, GROUP), BF16)
    tokx[share:, 0:share] = jnp.broadcast_to(gain_ref[...].astype(F32).reshape(1, share), (16, share)).astype(BF16)

    before = (
        lax.broadcasted_iota(jnp.int32, (GROUP, GROUP), 0) < lax.broadcasted_iota(jnp.int32, (GROUP, GROUP), 1)
    ).astype(F32).astype(BF16)
    labels = lax.broadcasted_iota(jnp.int32, (16, GROUP), 0)
    spot = lax.broadcasted_iota(jnp.int32, (HALF, 1), 0) + HALF * c
    place = []
    for k in range(len(ROUTES)):
        dev = expert_of(k)
        place.append(spot + (dev["expert"] * ND + dev["dp"]) * CAP)
    place = jnp.concatenate(place, axis=0)
    small[0].wait()
    e0 = ids_ref[0:1, :]
    e1 = ids_ref[1:2, :]
    hit0 = (e0 == labels).astype(F32)
    hit1 = (e1 == labels).astype(F32)
    earlier = jnp.dot((hit0 + hit1).astype(BF16), before, preferred_element_type=F32)
    slot0 = jnp.sum(earlier * hit0, axis=0, keepdims=True).astype(jnp.int32)
    slot1 = jnp.sum(earlier * hit1, axis=0, keepdims=True).astype(jnp.int32)
    dest0 = e0 * CAP + slot0
    dest1 = e1 * CAP + slot1
    small[1].wait()

    pl.semaphore_wait(barrier, len(partners))

    tok_copy = rcopy(tokx, sibtok, tok_s, tok_r, sib)
    tok_copy.start()
    select = ((place == dest0) | (place == dest1)).astype(F32).astype(BF16)

    loads = []
    for zz in range(NZ):
        for yy in range(NY):
            for k, source in enumerate((wg_hbm, wu_hbm)):
                loads.append(
                    pltpu.make_async_copy(
                        source.at[0, :, pl.ds((yy * NZ + zz) * FEAT, FEAT)],
                        wgu.at[zz, pl.ds(k * HID, HID), pl.ds(yy * FEAT, FEAT)],
                        wsem.at[3 + len(loads)],
                    )
                )
    dloads = [
        pltpu.make_async_copy(wd_hbm.at[0, :, pl.ds(j * FEAT, FEAT)], wd.at[j], dsem.at[j])
        for j in range(NY * NZ)
    ]
    shared = [
        rcopy(wd_hbm.at[0, :, pl.ds(j * FEAT, FEAT)], wd2.at[j], wd2_s.at[j], wd2_r.at[j], sib)
        for j in range(NY * NZ)
    ]

    tok_copy.wait_recv()
    here = tokx[...].astype(F32)
    there = sibtok[...].astype(F32)
    first_core = jnp.where(c == 0, here, there)
    second_core = jnp.where(c == 0, there, here)
    both = jnp.concatenate([first_core[:share], second_core[:share]], axis=0).astype(BF16)
    rows = lax.dot_general(
        select, both, (((1,), (1,)), ((), ())), preferred_element_type=F32
    ).astype(BF16)
    x[0, own, c, 0:HALF, :] = rows[0:HALF]

    def disp_copy(k):
        q, span = k // PER, pl.ds((k % PER) * HALF, HALF)
        if k in FAR:
            target = x.at[q, y * NZ + lax.rem(z + 2, NZ), c, span]
            return rcopy(relay.at[k - FAR[0]], target, disp_s.at[k], disp_r.at[k], leg(ROUTES[k][0], True))
        return rcopy(stage.at[k], x.at[q, own, c, span], disp_s.at[k], disp_r.at[k], expert_of(k))

    def relay_copy(part):
        first_k = FAR[0] + part * PER
        target = relay.at[pl.ds(part * PER, PER)]
        return rcopy(stage.at[pl.ds(first_k, PER)], target, rel_s.at[part], rel_r.at[part], leg(0, True))

    def relay_on(part):
        relay_copy(part).wait_recv()
        for k in range(FAR[0] + part * PER, FAR[0] + (part + 1) * PER):
            disp_copy(k).start()

    for k in range(1, len(ROUTES)):
        stage[k] = rows[k * HALF : (k + 1) * HALF]
        if k < PER:
            disp_copy(k).start()

    gain_row = jnp.concatenate(
        [first_core[share : share + 1, 0:share], second_core[share : share + 1, 0:share]], axis=1
    )
    index = lax.broadcasted_iota(jnp.int32, (16, 128), 0)
    tile = jnp.zeros((16, 128), F32)
    for j in range(3):
        tile = jnp.where(index == j, jnp.broadcast_to(gain_row[:, 128 * j : 128 * (j + 1)], (16, 128)), tile)
    gains[y, z] = tile.astype(BF16)

    def gzc(i):
        return rcopy(gains.at[y, z], gains.at[y, z], gz_s.at[i], gz_r.at[i], zdev(i))

    def gyc(i, way):
        ref = gains.at[y, xor4(z, i)]
        return rcopy(ref, ref, gy_s.at[i, way], gy_r.at[i, way], (up, down)[way])

    def gfc(i):
        ref = gains.at[ym, xor4(z, i)]
        return rcopy(ref, ref, gf_s.at[i], gf_r.at[i], up)

    for i in range(1, NZ):
        gzc(i).start()

    def at_step(s):
        q = lax.div(s, NZ)
        i = lax.rem(s, NZ)
        return q, i, xor4(z, i)

    def zc(q, i):
        return rcopy(x.at[q, own, c], x.at[q, own, c], z_s.at[q, i], z_r.at[q, i], zdev(i))

    def yc(s, way):
        q, i, zi = at_step(s)
        b = y * NZ + zi
        return rcopy(x.at[q, b, c], x.at[q, b, c], y_s.at[s, way], y_r.at[s, way], (up, down)[way])

    def fc(s, way):
        q, i, zi = at_step(s)
        b = (ym, yp)[way] * NZ + zi
        ref = x.at[q, b, c, pl.ds(way * (ROWS // 2), ROWS // 2)]
        return rcopy(ref, ref, f_s.at[s, way], f_r.at[s, way], (up, down)[way])

    def fzc(q):
        ref = x.at[q, lax.rem(y + 2, NY) * NZ + z, c]
        return rcopy(ref, ref, fz_s.at[q], fz_r.at[q], zdev(HANDED))

    def bc(s, r):
        q, i, zi = at_step(s)
        b = lax.rem(y + r, NY) * NZ + zi
        return rcopy(x.at[q, b, c], x.at[q, b, c], b_s.at[s, r], b_r.at[s, r], sib)

    def open_chunk(chunk):
        for k in range(max(1, chunk * PER), (chunk + 1) * PER):
            disp_copy(k).wait_recv()
        for j in range(1, NZ):
            zc(chunk, j).start()

    def first(s):
        q, i, zi = at_step(s)

        @pl.when(i > 0)
        def _():
            zc(q, i).wait_recv()

        yc(s, 0).start()
        yc(s, 1).start()
        bc(s, 0).start()

        @pl.when((s > 0) & (s < NZ))
        def _():
            gzc(i).wait_recv()

        @pl.when(s < NZ)
        def _():
            gyc(i, 0).start()
            gyc(i, 1).start()

        for chunk in range(1, CHUNKS):

            @pl.when(s == chunk * NZ - 1)
            def _():
                open_chunk(chunk)

    def second(s):
        q, i, zi = at_step(s)
        yc(s, 0).wait_recv()

        @pl.when(i != HANDED)
        def _():
            fc(s, 0).start()

        yc(s, 1).wait_recv()

        @pl.when(i != HANDED)
        def _():
            fc(s, 1).start()

        bc(s, 3).start()
        bc(s, 1).start()

        @pl.when(s < NZ)
        def _():
            gyc(i, 0).wait_recv()
            gfc(i).start()
            gyc(i, 1).wait_recv()

    def third(s):
        q, i, zi = at_step(s)
        @pl.when(i != HANDED)
        def _():
            fc(s, 0).wait_recv()
            fc(s, 1).wait_recv()

        @pl.when(i == 0)
        def _():
            fzc(q).start()

        @pl.when(i == HANDED)
        def _():
            fzc(q).wait_recv()

        bc(s, 2).start()

        @pl.when(s < NZ)
        def _():
            gfc(i).wait_recv()

    def hidc(q):
        return rcopy(hidout.at[q], hidin.at[q], hid_s.at[q], hid_r.at[q], sib)

    def gate_up(s):
        q, i, zi = at_step(s)
        for r in range(NY):
            bc(s, r).wait_recv()
        squares = sq[...]
        for yy in range(NY):
            block = x[q, yy * NZ + zi].reshape(2 * ROWS, FEAT)
            gain = gains[yy, zi].astype(F32)
            for j in range(3):
                slab = block[:, 128 * j : 128 * (j + 1)].astype(F32)
                squares = squares + slab * slab
                at = yy * FEAT + 128 * j
                scaled[:, at : at + 128] = (slab * gain[j : j + 1, :]).astype(BF16)
        sq[...] = squares
        acc[...] += lax.dot_general(
            wgu[zi], scaled[...], (((1,), (1,)), ((), ())), preferred_element_type=F32
        )

        @pl.when(i == NZ - 1)
        def _():
            total = jnp.sum(jnp.transpose(sq[...]), axis=0, keepdims=True)
            scale = lax.rsqrt(total / D + NORM_EPS)
            gate = acc[0:HID, :] * scale
            lift = acc[HID:, :] * scale
            value = jnp.transpose(gate / (1.0 + jnp.exp(-gate)) * lift)
            lower, upper = value[:ROWS], value[ROWS:]
            hidout[q] = jnp.where(c == 0, upper, lower).astype(BF16)
            hidc(q).start()
            hid[q] = jnp.where(c == 0, lower, upper).astype(BF16)
            acc[...] = jnp.zeros_like(acc)
            sq[...] = jnp.zeros_like(sq)

    def out_step(s):
        return lax.div(s, NZ), (NZ - 1) - lax.rem(s, NZ)

    def hc(s, way):
        span = pl.ds(way * (ROWS // 2), ROWS // 2)
        return rcopy(mine.at[s, 2, span], halves.at[s, way], h_s.at[s, way], h_r.at[s, way], (up, down)[way])

    def wc(s, way):
        return rcopy(mine.at[s, (1, 3)[way]], fulls.at[s, way], w_s.at[s, way], w_r.at[s, way], (up, down)[way])

    def zzc(s):
        q, i = out_step(s)
        return rcopy(mine.at[s, 0], zrecv.at[q, i], zz_s.at[q, i], zz_r.at[q, i], zdev(i))

    def frc(s):
        q, i = out_step(s)
        return rcopy(mine.at[s, 2], farin.at[q], fr_s.at[q], fr_r.at[q], zdev(HANDED))

    def retc(k):
        chunk, span = k // PER, pl.ds((k % PER) * HALF, HALF)
        if k in FAR:
            source = back.at[chunk - FAR[0] // PER, span]
            return rcopy(source, ret.at[k], ret_s.at[k], ret_r.at[k], leg(-ROUTES[k][0], True))
        return rcopy(mine.at[chunk * NZ + NZ - 1, 0, span], ret.at[k], ret_s.at[k], ret_r.at[k], group_of(k))

    def back_copy(part):
        chunk = FAR[0] // PER + part
        return rcopy(mine.at[chunk * NZ + NZ - 1, 0], back.at[part], back_s.at[part], back_r.at[part], leg(0, True))

    def back_on(part):
        back_copy(part).wait_recv()
        for k in range(FAR[0] + part * PER, FAR[0] + (part + 1) * PER):
            retc(k).start()

    def produce(s):
        q, i = out_step(s)
        zi = xor4(z, i)

        @pl.when(i == NZ - 1)
        def _():
            hidc(q).wait_recv()

        for r in (2, 1, 3, 0):
            b = lax.rem(y + r, NY) * NZ + zi
            total = jnp.dot(hid[q], wd[b], preferred_element_type=F32)
            total += jnp.dot(hidin[q], wd2[b], preferred_element_type=F32)
            if r != 2:
                mine[s, r] = total.astype(BF16)
                continue

            @pl.when(i == HANDED)
            def _():
                mine[s, r] = total.astype(BF16)
                frc(s).start()

            @pl.when(i == 0)
            def _():
                frc(s - 1).wait_recv()
                mine[s, r] = (total + farin[q].astype(F32)).astype(BF16)

            @pl.when(i > HANDED)
            def _():
                mine[s, r] = total.astype(BF16)

            @pl.when(i != HANDED)
            def _():
                hc(s, 0).start()
                hc(s, 1).start()

    def neighbours(s):
        q, i = out_step(s)
        half = ROWS // 2
        for way, r in enumerate((1, 3)):

            @pl.when(i != HANDED)
            def _():
                hc(s, way).wait_recv()
                span = pl.ds(way * half, half)
                mine[s, r, span] = (mine[s, r, span].astype(F32) + halves[s, way].astype(F32)).astype(BF16)

            wc(s, way).start()

    def finish(s):
        q, i = out_step(s)
        total = mine[s, 0].astype(F32)
        wc(s, 0).wait_recv()
        total = total + fulls[s, 0].astype(F32)
        wc(s, 1).wait_recv()
        total = total + fulls[s, 1].astype(F32)

        @pl.when(i > 0)
        def _():
            mine[s, 0] = total.astype(BF16)
            zzc(s).start()

        @pl.when(i == 0)
        def _():
            whole = total
            for j in range(1, NZ):
                zzc(s - j).wait_recv()
                whole = whole + zrecv[q, j].astype(F32)
            whole = whole.astype(BF16)
            mine[s, 0] = whole

            @pl.when(q == 0)
            def _():
                ret[0] = whole[0:HALF]

            for chunk in range(CHUNKS):

                @pl.when(q == chunk)
                def _():
                    if chunk * PER in FAR:
                        back_copy(chunk - FAR[0] // PER).start()
                    else:
                        for k in range(max(1, chunk * PER), (chunk + 1) * PER):
                            retc(k).start()

    def drain_gather(s):
        q, i, zi = at_step(s)
        for way in range(2):
            yc(s, way).wait_send()
        for r in range(NY):
            bc(s, r).wait_send()

        @pl.when(i != HANDED)
        def _():
            fc(s, 0).wait_send()
            fc(s, 1).wait_send()

        @pl.when(i == 0)
        def _():
            fzc(q).wait_send()

        @pl.when(i > 0)
        def _():
            zc(q, i).wait_send()

    def drain_reduce(s):
        q, i = out_step(s)
        for way in range(2):
            wc(s, way).wait_send()
        @pl.when(i != HANDED)
        def _():
            hc(s, 0).wait_send()
            hc(s, 1).wait_send()

        @pl.when(i == HANDED)
        def _():
            frc(s).wait_send()

        @pl.when(i > 0)
        def _():
            zzc(s).wait_send()

    def combine(chunk):
        for k in range(max(1, chunk * PER), (chunk + 1) * PER):
            retc(k).wait_recv()
        came = ret[chunk * PER : (chunk + 1) * PER].reshape(ROWS, FEAT)
        spots = place[chunk * ROWS : (chunk + 1) * ROWS]
        total = comb[...]
        for k, dest in enumerate((dest0, dest1)):
            pick = (spots == dest).astype(F32).astype(BF16)
            total += rw_ref[k : k + 1, :] * lax.dot_general(
                came, pick, (((0,), (0,)), ((), ())), preferred_element_type=F32
            )
        return total

    def step(t, carry):
        u = t - LAG
        stages = (
            (first, t, 0), (second, t, SECOND), (third, t, THIRD),
            (finish, u, FINISH), (neighbours, u, NEIGHBOURS),
        )

        def run(stages):
            for stage_of, now, behind in stages:

                @pl.when((now >= behind) & (now < STEPS + behind))
                def _():
                    stage_of(now - behind)

        run(stages)

        @pl.when(t == 1)
        def _():
            relay_copy(1).start()

        @pl.when(t == 2)
        def _():
            relay_on(0)

        @pl.when(t == 4)
        def _():
            relay_on(1)
            for k in range((CHUNKS - 1) * PER, CHUNKS * PER):
                disp_copy(k).start()

        for part in range(len(FAR) // PER):

            @pl.when(u == (FAR[0] // PER + part) * NZ + NZ + FINISH)
            def _():
                back_on(part)

        @pl.when(t == MULTIPLY)
        def _():
            for load in loads:
                load.wait()

        @pl.when(u == 0)
        def _():
            for load in dloads:
                load.wait()
            for copy in shared:
                copy.wait_recv()

        run(((produce, u, 0), (gate_up, t, MULTIPLY)))
        run(((drain_gather, t, DRAIN_GATHER), (drain_reduce, u, DRAIN_REDUCE)))

        for chunk in range(CHUNKS - 1):

            @pl.when(u == chunk * NZ + NZ - 1 + FINISH + COMBINE)
            def _():
                comb[...] = combine(chunk)

        return carry

    open_chunk(0)
    first(jnp.int32(0))
    relay_copy(0).start()
    for load in loads + dloads + shared:
        load.start()
    acc[...] = jnp.zeros_like(acc)
    sq[...] = jnp.zeros_like(sq)
    comb[...] = jnp.zeros_like(comb)
    small[2].wait()
    lax.fori_loop(1, LAG + STEPS + FINISH, step, 0)

    combined = combine(CHUNKS - 1)
    left = combined[:share]
    right = combined[share:]
    part[...] = jnp.where(c == 0, right, left)
    part_copy = rcopy(part, partr, part_s, part_r, sib)
    part_copy.start()
    kept = jnp.where(c == 0, left, right)
    part_copy.wait_recv()
    out_ref[...] = (kept + partr[...]).astype(BF16)

    part_copy.wait_send()
    tok_copy.wait_send()
    for copy in shared:
        copy.wait_send()
    for q in range(CHUNKS):
        hidc(q).wait_send()
    for k in range(1, len(ROUTES)):
        disp_copy(k).wait_send()
        retc(k).wait_send()
    for part in range(len(FAR) // PER):
        relay_copy(part).wait_send()
        back_copy(part).wait_send()
    for i in range(NZ):
        if i > 0:
            gzc(i).wait_send()
        gyc(i, 0).wait_send()
        gyc(i, 1).wait_send()
        gfc(i).wait_send()

    for s in range(STEPS + FINISH - DRAIN_REDUCE, STEPS):
        drain_reduce(jnp.int32(s))


def per_device(tokens, norm_gain, expert_ids, route_weights, gate_weight, up_weight, down_weight):
    vmem = pl.BlockSpec(memory_space=pltpu.VMEM)
    hbm = pl.BlockSpec(memory_space=pl.ANY)
    blocks = NY * NZ
    dma = pltpu.SemaphoreType.DMA
    scratch = [
        pltpu.VMEM((NZ, 2 * HID, NY * FEAT), BF16),
        pltpu.VMEM((blocks, HID, FEAT), BF16),
        pltpu.VMEM((blocks, HID, FEAT), BF16),
        pltpu.VMEM((CHUNKS, blocks, 2, ROWS, FEAT), BF16),
        pltpu.VMEM((2 * ROWS, NY * FEAT), BF16),
        pltpu.VMEM((2 * HID, 2 * ROWS), F32),
        pltpu.VMEM((2 * ROWS, 128), F32),
        pltpu.VMEM((CHUNKS, ROWS, HID), BF16),
        pltpu.VMEM((CHUNKS, ROWS, HID), BF16),
        pltpu.VMEM((CHUNKS, ROWS, HID), BF16),
        pltpu.VMEM((NY, NZ, 16, 128), BF16),
        pltpu.VMEM((2, GROUP), jnp.int32),
        pltpu.VMEM((2, GROUP), F32),
        pltpu.VMEM((FEAT // 2 + 16, GROUP), BF16),
        pltpu.VMEM((FEAT // 2 + 16, GROUP), BF16),
        pltpu.VMEM((len(ROUTES), HALF, FEAT), BF16),
        pltpu.VMEM((len(FAR), HALF, FEAT), BF16),
        pltpu.VMEM((len(FAR) // PER, ROWS, FEAT), BF16),
        pltpu.VMEM((CHUNKS, ROWS, FEAT), BF16),
        pltpu.VMEM((STEPS, NY, ROWS, FEAT), BF16),
        pltpu.VMEM((STEPS, 2, ROWS // 2, FEAT), BF16),
        pltpu.VMEM((STEPS, 2, ROWS, FEAT), BF16),
        pltpu.VMEM((CHUNKS, NZ, ROWS, FEAT), BF16),
        pltpu.VMEM((len(ROUTES), HALF, FEAT), BF16),
        pltpu.VMEM((FEAT, GROUP), F32),
        pltpu.VMEM((FEAT // 2, GROUP), F32),
        pltpu.VMEM((FEAT // 2, GROUP), F32),
        dma((3 + 2 * blocks,)), dma((blocks,)),
        dma, dma, dma((len(ROUTES),)), dma((len(ROUTES),)),
        dma((NZ,)), dma((NZ,)), dma((NZ, 2)), dma((NZ, 2)), dma((NZ,)), dma((NZ,)),
        dma((CHUNKS, NZ)), dma((CHUNKS, NZ)), dma((STEPS, 2)), dma((STEPS, 2)),
        dma((STEPS, 2)), dma((STEPS, 2)), dma((STEPS, NY)), dma((STEPS, NY)),
        dma((CHUNKS,)), dma((CHUNKS,)), dma((CHUNKS,)), dma((CHUNKS,)),
        dma((len(FAR) // PER,)), dma((len(FAR) // PER,)), dma((len(FAR) // PER,)), dma((len(FAR) // PER,)),
        dma((blocks,)), dma((blocks,)), dma((CHUNKS,)), dma((CHUNKS,)), dma((STEPS, 2)), dma((STEPS, 2)),
        dma((STEPS, 2)), dma((STEPS, 2)), dma((CHUNKS, NZ)), dma((CHUNKS, NZ)),
        dma((len(ROUTES),)), dma((len(ROUTES),)), dma, dma,
    ]
    rows = CHUNKS * 2 * ROWS
    out = pl.pallas_call(
        kernel,
        out_shape=jax.ShapeDtypeStruct((FEAT // 2, GROUP), BF16),
        in_specs=[hbm, vmem, hbm, hbm, hbm, hbm, hbm],
        out_specs=vmem,
        scratch_shapes=scratch,
        cost_estimate=pl.CostEstimate(
            flops=6 * rows * D * HID, bytes_accessed=6 * D * HID, transcendentals=rows * HID
        ),
        compiler_params=pltpu.CompilerParams(
            collective_id=0, has_side_effects=True, vmem_limit_bytes=61 * 1024 * 1024
        ),
    )(
        tokens.T,
        norm_gain,
        expert_ids.T,
        route_weights.T,
        gate_weight.swapaxes(1, 2),
        up_weight.swapaxes(1, 2),
        down_weight,
    )
    return out.T


def solution(mesh):
    placed = (
        P(("expert", "dp"), "tensor"),
        P("tensor"),
        P(("expert", "dp"), None),
        P(("expert", "dp"), None),
        P(("expert", "dp"), None, "tensor"),
        P(("expert", "dp"), None, "tensor"),
        P(("expert", "dp"), "tensor", None),
    )
    return jax.shard_map(
        per_device,
        mesh=mesh,
        in_specs=placed,
        out_specs=P(("expert", "dp"), "tensor"),
        check_vma=False,
    )
```

```python
import jax
import jax.numpy as jnp
from jax import lax
from jax.experimental import pallas as pl
from jax.experimental.pallas import tpu as pltpu
from jax.sharding import PartitionSpec as P

D = 6144
NORM_EPS = 1e-05
MESH = pl.DeviceIdType.MESH
NX, NY, NZ, ND = 4, 4, 4, 2
GROUP = 256
CAP = 128
HALF = CAP // 2
FEAT = 384
HID = 352
ROUTES = ((0, 0), (1, 0), (0, 1), (1, 1), (2, 1), (3, 1), (2, 0), (3, 0))
PER = 2
CHUNKS = len(ROUTES) // PER
ROWS = PER * HALF
STEPS = CHUNKS * NZ
SECOND, THIRD, MULTIPLY = 2, 4, 5
FARTHEST, NEIGHBOURS, FINISH = 1, 3, 5
LAG = NZ + MULTIPLY
F32 = jnp.float32
BF16 = jnp.bfloat16


def xor4(a, b):
    low = lax.rem(lax.rem(a, 2) + lax.rem(b, 2), 2)
    high = lax.rem(lax.div(a, 2) + lax.div(b, 2), 2)
    return low + 2 * high


def kernel(
    tok_hbm, gain_ref, ids_hbm, rw_hbm, wg_hbm, wu_hbm, wd_hbm,
    out_ref,
    wgu, wd, x, scaled, acc, sq, hid, gains,
    ids_ref, rw_ref, tokx, sibtok, stage, mine, given, srecv, halves, fulls, zrecv, ret, part, partr,
    wsem, dsem, tok_s, tok_r, disp_s, disp_r, gz_s, gz_r, gy_s, gy_r, gf_s, gf_r,
    z_s, z_r, y_s, y_r, f_s, f_r, b_s, b_r,
    sib_s, sib_r, h_s, h_r, w_s, w_r, zz_s, zz_r, ret_s, ret_r, part_s, part_r,
):
    xi = lax.axis_index("expert")
    di = lax.axis_index("dp")
    me = lax.axis_index("tensor")
    c = lax.rem(me, 2)
    z = lax.rem(lax.div(me, 2), NZ)
    y = lax.div(me, 2 * NZ)
    own = y * NZ + z
    yp = lax.rem(y + 1, NY)
    ym = lax.rem(y + NY - 1, NY)

    def tid(yy, zz, cc):
        return (yy * NZ + zz) * 2 + cc

    sib = {"tensor": tid(y, z, 1 - c)}
    up = {"tensor": tid(yp, z, c)}
    down = {"tensor": tid(ym, z, c)}

    def zdev(i):
        return {"tensor": tid(y, xor4(z, i), c)}

    def expert_of(k):
        dx, dd = ROUTES[k]
        return {"expert": lax.rem(xi + dx, NX), "dp": lax.rem(di + dd, ND)}

    def group_of(k):
        dx, dd = ROUTES[k]
        return {"expert": lax.rem(xi + NX - dx, NX), "dp": lax.rem(di + dd, ND)}

    def rcopy(src, dst, ssem, rsem, dev):
        return pltpu.make_async_remote_copy(
            src_ref=src, dst_ref=dst, send_sem=ssem, recv_sem=rsem, device_id=dev, device_id_type=MESH
        )

    barrier = pltpu.get_barrier_semaphore()
    partners = [sib, up, down] + [zdev(i) for i in range(1, NZ)] + [expert_of(k) for k in range(1, len(ROUTES))]
    for dev in partners:
        pl.semaphore_signal(barrier, inc=1, device_id=dev, device_id_type=MESH)

    share = FEAT // 2
    small = [
        pltpu.make_async_copy(ids_hbm, ids_ref, wsem.at[0]),
        pltpu.make_async_copy(tok_hbm, tokx.at[pl.ds(0, share)], wsem.at[1]),
        pltpu.make_async_copy(rw_hbm, rw_ref, wsem.at[2]),
    ]
    for load in small:
        load.start()
    tokx[share:, :] = jnp.zeros((16, GROUP), BF16)
    tokx[share:, 0:share] = jnp.broadcast_to(gain_ref[...].astype(F32).reshape(1, share), (16, share)).astype(BF16)

    before = (
        lax.broadcasted_iota(jnp.int32, (GROUP, GROUP), 0) < lax.broadcasted_iota(jnp.int32, (GROUP, GROUP), 1)
    ).astype(F32).astype(BF16)
    labels = lax.broadcasted_iota(jnp.int32, (16, GROUP), 0)
    spot = lax.broadcasted_iota(jnp.int32, (HALF, 1), 0) + HALF * c
    place = []
    for k in range(len(ROUTES)):
        dev = expert_of(k)
        place.append(spot + (dev["expert"] * ND + dev["dp"]) * CAP)
    place = jnp.concatenate(place, axis=0)
    small[0].wait()
    e0 = ids_ref[0:1, :]
    e1 = ids_ref[1:2, :]
    hit0 = (e0 == labels).astype(F32)
    hit1 = (e1 == labels).astype(F32)
    earlier = jnp.dot((hit0 + hit1).astype(BF16), before, preferred_element_type=F32)
    slot0 = jnp.sum(earlier * hit0, axis=0, keepdims=True).astype(jnp.int32)
    slot1 = jnp.sum(earlier * hit1, axis=0, keepdims=True).astype(jnp.int32)
    dest0 = e0 * CAP + slot0
    dest1 = e1 * CAP + slot1
    small[1].wait()

    pl.semaphore_wait(barrier, len(partners))

    tok_copy = rcopy(tokx, sibtok, tok_s, tok_r, sib)
    tok_copy.start()
    select = ((place == dest0) | (place == dest1)).astype(F32).astype(BF16)

    loads = []
    for zz in range(NZ):
        for yy in range(NY):
            for k, source in enumerate((wg_hbm, wu_hbm)):
                loads.append(
                    pltpu.make_async_copy(
                        source.at[0, :, pl.ds((yy * NZ + zz) * FEAT, FEAT)],
                        wgu.at[zz, pl.ds(k * HID, HID), pl.ds(yy * FEAT, FEAT)],
                        wsem.at[3 + len(loads)],
                    )
                )
    dloads = [
        pltpu.make_async_copy(wd_hbm.at[0, :, pl.ds(j * FEAT, FEAT)], wd.at[j], dsem.at[j])
        for j in range(NY * NZ)
    ]

    tok_copy.wait_recv()
    here = tokx[...].astype(F32)
    there = sibtok[...].astype(F32)
    first_core = jnp.where(c == 0, here, there)
    second_core = jnp.where(c == 0, there, here)
    both = jnp.concatenate([first_core[:share], second_core[:share]], axis=0).astype(BF16)
    rows = lax.dot_general(
        select, both, (((1,), (1,)), ((), ())), preferred_element_type=F32
    ).astype(BF16)
    x[0, own, c, 0:HALF, :] = rows[0:HALF]

    def disp_copy(k):
        target = x.at[k // PER, own, c, pl.ds((k % PER) * HALF, HALF)]
        return rcopy(stage.at[k], target, disp_s.at[k], disp_r.at[k], expert_of(k))

    for k in range(1, len(ROUTES)):
        stage[k] = rows[k * HALF : (k + 1) * HALF]
        if k < 2 * PER:
            disp_copy(k).start()

    gain_row = jnp.concatenate(
        [first_core[share : share + 1, 0:share], second_core[share : share + 1, 0:share]], axis=1
    )
    index = lax.broadcasted_iota(jnp.int32, (16, 128), 0)
    tile = jnp.zeros((16, 128), F32)
    for j in range(3):
        tile = jnp.where(index == j, jnp.broadcast_to(gain_row[:, 128 * j : 128 * (j + 1)], (16, 128)), tile)
    gains[y, z] = tile.astype(BF16)

    def gzc(i):
        return rcopy(gains.at[y, z], gains.at[y, z], gz_s.at[i], gz_r.at[i], zdev(i))

    def gyc(i, way):
        ref = gains.at[y, xor4(z, i)]
        return rcopy(ref, ref, gy_s.at[i, way], gy_r.at[i, way], (up, down)[way])

    def gfc(i):
        ref = gains.at[ym, xor4(z, i)]
        return rcopy(ref, ref, gf_s.at[i], gf_r.at[i], up)

    for i in range(1, NZ):
        gzc(i).start()

    def at_step(s):
        q = lax.div(s, NZ)
        i = lax.rem(s, NZ)
        return q, i, xor4(z, i)

    def zc(q, i):
        return rcopy(x.at[q, own, c], x.at[q, own, c], z_s.at[q, i], z_r.at[q, i], zdev(i))

    def yc(s, way):
        q, i, zi = at_step(s)
        b = y * NZ + zi
        return rcopy(x.at[q, b, c], x.at[q, b, c], y_s.at[s, way], y_r.at[s, way], (up, down)[way])

    def fc(s, way):
        q, i, zi = at_step(s)
        b = (ym, yp)[way] * NZ + zi
        ref = x.at[q, b, c, pl.ds(way * (ROWS // 2), ROWS // 2)]
        return rcopy(ref, ref, f_s.at[s, way], f_r.at[s, way], (up, down)[way])

    def bc(s, r):
        q, i, zi = at_step(s)
        b = lax.rem(y + r, NY) * NZ + zi
        return rcopy(x.at[q, b, c], x.at[q, b, c], b_s.at[s, r], b_r.at[s, r], sib)

    def open_chunk(chunk):
        for k in range(max(1, chunk * PER), (chunk + 1) * PER):
            disp_copy(k).wait_recv()
        for j in range(1, NZ):
            zc(chunk, j).start()

    def first(s):
        q, i, zi = at_step(s)

        @pl.when(i > 0)
        def _():
            zc(q, i).wait_recv()

        yc(s, 0).start()
        yc(s, 1).start()
        bc(s, 0).start()

        @pl.when((s > 0) & (s < NZ))
        def _():
            gzc(i).wait_recv()

        @pl.when(s < NZ)
        def _():
            gyc(i, 0).start()
            gyc(i, 1).start()

        for chunk in range(1, CHUNKS):

            @pl.when(s == chunk * NZ - 1)
            def _():
                open_chunk(chunk)

    def second(s):
        q, i, zi = at_step(s)
        yc(s, 0).wait_recv()
        fc(s, 0).start()
        yc(s, 1).wait_recv()
        fc(s, 1).start()
        bc(s, 3).start()
        bc(s, 1).start()

        @pl.when(s < NZ)
        def _():
            gyc(i, 0).wait_recv()
            gfc(i).start()
            gyc(i, 1).wait_recv()

    def third(s):
        q, i, zi = at_step(s)
        fc(s, 0).wait_recv()
        fc(s, 1).wait_recv()
        bc(s, 2).start()

        @pl.when(s < NZ)
        def _():
            gfc(i).wait_recv()

    def gate_up(s):
        q, i, zi = at_step(s)
        for r in range(NY):
            bc(s, r).wait_recv()
        squares = sq[...]
        for yy in range(NY):
            block = x[q, yy * NZ + zi].reshape(2 * ROWS, FEAT)
            gain = gains[yy, zi].astype(F32)
            for j in range(3):
                slab = block[:, 128 * j : 128 * (j + 1)].astype(F32)
                squares = squares + slab * slab
                at = yy * FEAT + 128 * j
                scaled[:, at : at + 128] = (slab * gain[j : j + 1, :]).astype(BF16)
        sq[...] = squares
        acc[...] += lax.dot_general(
            wgu[zi], scaled[...], (((1,), (1,)), ((), ())), preferred_element_type=F32
        )

        @pl.when(i == NZ - 1)
        def _():
            total = jnp.sum(jnp.transpose(sq[...]), axis=0, keepdims=True)
            scale = lax.rsqrt(total / D + NORM_EPS)
            gate = acc[0:HID, :] * scale
            lift = acc[HID:, :] * scale
            value = jnp.transpose(gate / (1.0 + jnp.exp(-gate)) * lift).astype(BF16)
            for h in range(2):
                hid[q, lax.rem(c + h, 2)] = value[h * ROWS : (h + 1) * ROWS]
            acc[...] = jnp.zeros_like(acc)
            sq[...] = jnp.zeros_like(sq)

    def out_step(s):
        return lax.div(s, NZ), (NZ - 1) - lax.rem(s, NZ)

    def sc(s, r):
        return rcopy(given.at[s, r], srecv.at[s, r], sib_s.at[s, r], sib_r.at[s, r], sib)

    def hc(s, way):
        span = pl.ds(way * (ROWS // 2), ROWS // 2)
        return rcopy(mine.at[s, 2, span], halves.at[s, way], h_s.at[s, way], h_r.at[s, way], (up, down)[way])

    def wc(s, way):
        return rcopy(mine.at[s, (1, 3)[way]], fulls.at[s, way], w_s.at[s, way], w_r.at[s, way], (up, down)[way])

    def zzc(s):
        q, i = out_step(s)
        return rcopy(mine.at[s, 0], zrecv.at[q, i], zz_s.at[q, i], zz_r.at[q, i], zdev(i))

    def retc(k):
        source = mine.at[k // PER * NZ + NZ - 1, 0, pl.ds((k % PER) * HALF, HALF)]
        return rcopy(source, ret.at[k], ret_s.at[k], ret_r.at[k], group_of(k))

    def produce(s):
        q, i = out_step(s)
        zi = xor4(z, i)
        left = hid[q].reshape(2 * ROWS, HID)
        for r in (2, 1, 3, 0):
            b = lax.rem(y + r, NY) * NZ + zi
            block = jnp.dot(left, wd[b], preferred_element_type=F32).astype(BF16)
            given[s, r] = block[ROWS:]
            sc(s, r).start()
            mine[s, r] = block[:ROWS]

    def chip_sum(s, r):
        sc(s, r).wait_recv()
        return mine[s, r].astype(F32) + srecv[s, r].astype(F32)

    def farthest(s):
        mine[s, 2] = chip_sum(s, 2).astype(BF16)
        hc(s, 0).start()
        hc(s, 1).start()

    def neighbours(s):
        half = ROWS // 2
        total = chip_sum(s, 1)
        hc(s, 0).wait_recv()
        total = jnp.concatenate([total[:half] + halves[s, 0].astype(F32), total[half:]], axis=0)
        mine[s, 1] = total.astype(BF16)
        wc(s, 0).start()
        total = chip_sum(s, 3)
        hc(s, 1).wait_recv()
        total = jnp.concatenate([total[:half], total[half:] + halves[s, 1].astype(F32)], axis=0)
        mine[s, 3] = total.astype(BF16)
        wc(s, 1).start()

    def finish(s):
        q, i = out_step(s)
        total = chip_sum(s, 0)
        wc(s, 0).wait_recv()
        total = total + fulls[s, 0].astype(F32)
        wc(s, 1).wait_recv()
        total = total + fulls[s, 1].astype(F32)

        @pl.when(i > 0)
        def _():
            mine[s, 0] = total.astype(BF16)
            zzc(s).start()

        @pl.when(i == 0)
        def _():
            whole = total
            for j in range(1, NZ):
                zzc(s - j).wait_recv()
                whole = whole + zrecv[q, j].astype(F32)
            whole = whole.astype(BF16)
            mine[s, 0] = whole

            @pl.when(q == 0)
            def _():
                ret[0] = whole[0:HALF]

            for chunk in range(CHUNKS):

                @pl.when(q == chunk)
                def _():
                    for k in range(max(1, chunk * PER), (chunk + 1) * PER):
                        retc(k).start()

    def drain_gather(s):
        q, i, zi = at_step(s)
        for way in range(2):
            yc(s, way).wait_send()
            fc(s, way).wait_send()
        for r in range(NY):
            bc(s, r).wait_send()

        @pl.when(i > 0)
        def _():
            zc(q, i).wait_send()

    def drain_reduce(s):
        q, i = out_step(s)
        for way in range(2):
            hc(s, way).wait_send()
            wc(s, way).wait_send()
        for r in range(NY):
            sc(s, r).wait_send()

        @pl.when(i > 0)
        def _():
            zzc(s).wait_send()

    def drain(stage_of, steps):
        def one(s, carry):
            stage_of(s)
            return carry

        lax.fori_loop(0, steps, one, 0)

    def step(t, carry):
        u = t - LAG

        def run(stages):
            for stage_of, now, behind in stages:

                @pl.when((now >= behind) & (now < STEPS + behind))
                def _():
                    stage_of(now - behind)

        run((
            (first, t, 0), (second, t, SECOND), (third, t, THIRD),
            (finish, u, FINISH), (neighbours, u, NEIGHBOURS), (farthest, u, FARTHEST),
        ))

        for chunk in range(2, CHUNKS):

            @pl.when(t == 2 * chunk - 1)
            def _():
                for k in range(chunk * PER, (chunk + 1) * PER):
                    disp_copy(k).start()

        @pl.when(t == MULTIPLY)
        def _():
            for load in loads:
                load.wait()

        @pl.when(u == 0)
        def _():
            for load in dloads:
                load.wait()

        run(((gate_up, t, MULTIPLY), (produce, u, 0)))

        @pl.when(u == STEPS)
        def _():
            drain(drain_gather, STEPS)

        @pl.when(u == STEPS + 1)
        def _():
            drain(drain_reduce, STEPS - NZ)

        return carry

    open_chunk(0)
    first(jnp.int32(0))
    for load in loads + dloads:
        load.start()
    acc[...] = jnp.zeros_like(acc)
    sq[...] = jnp.zeros_like(sq)
    lax.fori_loop(1, LAG + STEPS + FINISH, step, 0)

    small[2].wait()
    combined = jnp.zeros((FEAT, GROUP), F32)
    for chunk in range(CHUNKS):
        for k in range(max(1, chunk * PER), (chunk + 1) * PER):
            retc(k).wait_recv()
        came = ret[chunk * PER : (chunk + 1) * PER].reshape(ROWS, FEAT)
        spots = place[chunk * ROWS : (chunk + 1) * ROWS]
        for k, dest in enumerate((dest0, dest1)):
            pick = (spots == dest).astype(F32).astype(BF16)
            combined += rw_ref[k : k + 1, :] * lax.dot_general(
                came, pick, (((0,), (0,)), ((), ())), preferred_element_type=F32
            )
    left = combined[:share]
    right = combined[share:]
    part[...] = jnp.where(c == 0, right, left)
    part_copy = rcopy(part, partr, part_s, part_r, sib)
    part_copy.start()
    kept = jnp.where(c == 0, left, right)
    part_copy.wait_recv()
    out_ref[...] = (kept + partr[...]).astype(BF16)

    part_copy.wait_send()
    tok_copy.wait_send()
    for k in range(1, len(ROUTES)):
        disp_copy(k).wait_send()
        retc(k).wait_send()
    for i in range(NZ):
        if i > 0:
            gzc(i).wait_send()
        gyc(i, 0).wait_send()
        gyc(i, 1).wait_send()
        gfc(i).wait_send()

    for s in range(STEPS - NZ, STEPS):
        drain_reduce(jnp.int32(s))


def per_device(tokens, norm_gain, expert_ids, route_weights, gate_weight, up_weight, down_weight):
    vmem = pl.BlockSpec(memory_space=pltpu.VMEM)
    hbm = pl.BlockSpec(memory_space=pl.ANY)
    blocks = NY * NZ
    dma = pltpu.SemaphoreType.DMA
    scratch = [
        pltpu.VMEM((NZ, 2 * HID, NY * FEAT), BF16),
        pltpu.VMEM((blocks, HID, FEAT), BF16),
        pltpu.VMEM((CHUNKS, blocks, 2, ROWS, FEAT), BF16),
        pltpu.VMEM((2 * ROWS, NY * FEAT), BF16),
        pltpu.VMEM((2 * HID, 2 * ROWS), F32),
        pltpu.VMEM((2 * ROWS, 128), F32),
        pltpu.VMEM((CHUNKS, 2, ROWS, HID), BF16),
        pltpu.VMEM((NY, NZ, 16, 128), BF16),
        pltpu.VMEM((2, GROUP), jnp.int32),
        pltpu.VMEM((2, GROUP), F32),
        pltpu.VMEM((FEAT // 2 + 16, GROUP), BF16),
        pltpu.VMEM((FEAT // 2 + 16, GROUP), BF16),
        pltpu.VMEM((len(ROUTES), HALF, FEAT), BF16),
        pltpu.VMEM((STEPS, NY, ROWS, FEAT), BF16),
        pltpu.VMEM((STEPS, NY, ROWS, FEAT), BF16),
        pltpu.VMEM((STEPS, NY, ROWS, FEAT), BF16),
        pltpu.VMEM((STEPS, 2, ROWS // 2, FEAT), BF16),
        pltpu.VMEM((STEPS, 2, ROWS, FEAT), BF16),
        pltpu.VMEM((CHUNKS, NZ, ROWS, FEAT), BF16),
        pltpu.VMEM((len(ROUTES), HALF, FEAT), BF16),
        pltpu.VMEM((FEAT // 2, GROUP), F32),
        pltpu.VMEM((FEAT // 2, GROUP), F32),
        dma((3 + 2 * blocks,)), dma((blocks,)),
        dma, dma, dma((len(ROUTES),)), dma((len(ROUTES),)),
        dma((NZ,)), dma((NZ,)), dma((NZ, 2)), dma((NZ, 2)), dma((NZ,)), dma((NZ,)),
        dma((CHUNKS, NZ)), dma((CHUNKS, NZ)), dma((STEPS, 2)), dma((STEPS, 2)),
        dma((STEPS, 2)), dma((STEPS, 2)), dma((STEPS, NY)), dma((STEPS, NY)),
        dma((STEPS, NY)), dma((STEPS, NY)), dma((STEPS, 2)), dma((STEPS, 2)),
        dma((STEPS, 2)), dma((STEPS, 2)), dma((CHUNKS, NZ)), dma((CHUNKS, NZ)),
        dma((len(ROUTES),)), dma((len(ROUTES),)), dma, dma,
    ]
    rows = CHUNKS * 2 * ROWS
    out = pl.pallas_call(
        kernel,
        out_shape=jax.ShapeDtypeStruct((FEAT // 2, GROUP), BF16),
        in_specs=[hbm, vmem, hbm, hbm, hbm, hbm, hbm],
        out_specs=vmem,
        scratch_shapes=scratch,
        cost_estimate=pl.CostEstimate(
            flops=6 * rows * D * HID, bytes_accessed=6 * D * HID, transcendentals=rows * HID
        ),
        compiler_params=pltpu.CompilerParams(
            collective_id=0, has_side_effects=True, vmem_limit_bytes=61 * 1024 * 1024
        ),
    )(
        tokens.T,
        norm_gain,
        expert_ids.T,
        route_weights.T,
        gate_weight.swapaxes(1, 2),
        up_weight.swapaxes(1, 2),
        down_weight,
    )
    return out.T


def solution(mesh):
    placed = (
        P(("expert", "dp"), "tensor"),
        P("tensor"),
        P(("expert", "dp"), None),
        P(("expert", "dp"), None),
        P(("expert", "dp"), None, "tensor"),
        P(("expert", "dp"), None, "tensor"),
        P(("expert", "dp"), "tensor", None),
    )
    return jax.shard_map(
        per_device,
        mesh=mesh,
        in_specs=placed,
        out_specs=P(("expert", "dp"), "tensor"),
        check_vma=False,
    )
```

```python
import jax
import jax.numpy as jnp
from jax import lax
from jax.experimental import pallas as pl
from jax.experimental.pallas import tpu as pltpu
from jax.sharding import PartitionSpec as P

D = 6144
NORM_EPS = 1e-05
MESH = pl.DeviceIdType.MESH
NX, NY, NZ, ND = 4, 4, 4, 2
GROUP = 256
CAP = 128
HALF = CAP // 2
FEAT = 384
HID = 352
ROUTES = ((0, 0), (1, 0), (0, 1), (1, 1), (2, 1), (3, 1), (2, 0), (3, 0))
PER = 2
CHUNKS = len(ROUTES) // PER
ROWS = PER * HALF
STEPS = CHUNKS * NZ
GIVER, HANDED = 2, 3
SECOND, THIRD, MULTIPLY = 2, 4, 5
FARTHEST, NEIGHBOURS, FINISH = 1, 3, 5
LAG = NZ + MULTIPLY
F32 = jnp.float32
BF16 = jnp.bfloat16


def xor4(a, b):
    low = lax.rem(lax.rem(a, 2) + lax.rem(b, 2), 2)
    high = lax.rem(lax.div(a, 2) + lax.div(b, 2), 2)
    return low + 2 * high


def kernel(
    tok_hbm, gain_ref, ids_hbm, rw_hbm, wg_hbm, wu_hbm, wd_hbm,
    out_ref,
    wgu, wd, x, scaled, acc, sq, hid, gains,
    ids_ref, rw_ref, tokx, sibtok, stage, farin, mine, given, srecv, halves, fulls, zrecv, ret, part, partr,
    wsem, dsem, tok_s, tok_r, disp_s, disp_r, gz_s, gz_r, gy_s, gy_r, gf_s, gf_r,
    z_s, z_r, y_s, y_r, f_s, f_r, b_s, b_r,
    fz_s, fz_r, fr_s, fr_r,
    sib_s, sib_r, h_s, h_r, w_s, w_r, zz_s, zz_r, ret_s, ret_r, part_s, part_r,
):
    xi = lax.axis_index("expert")
    di = lax.axis_index("dp")
    me = lax.axis_index("tensor")
    c = lax.rem(me, 2)
    z = lax.rem(lax.div(me, 2), NZ)
    y = lax.div(me, 2 * NZ)
    own = y * NZ + z
    yp = lax.rem(y + 1, NY)
    ym = lax.rem(y + NY - 1, NY)

    def tid(yy, zz, cc):
        return (yy * NZ + zz) * 2 + cc

    sib = {"tensor": tid(y, z, 1 - c)}
    up = {"tensor": tid(yp, z, c)}
    down = {"tensor": tid(ym, z, c)}

    def zdev(i):
        return {"tensor": tid(y, xor4(z, i), c)}

    def expert_of(k):
        dx, dd = ROUTES[k]
        return {"expert": lax.rem(xi + dx, NX), "dp": lax.rem(di + dd, ND)}

    def group_of(k):
        dx, dd = ROUTES[k]
        return {"expert": lax.rem(xi + NX - dx, NX), "dp": lax.rem(di + dd, ND)}

    def rcopy(src, dst, ssem, rsem, dev):
        return pltpu.make_async_remote_copy(
            src_ref=src, dst_ref=dst, send_sem=ssem, recv_sem=rsem, device_id=dev, device_id_type=MESH
        )

    barrier = pltpu.get_barrier_semaphore()
    partners = [sib, up, down] + [zdev(i) for i in range(1, NZ)] + [expert_of(k) for k in range(1, len(ROUTES))]
    for dev in partners:
        pl.semaphore_signal(barrier, inc=1, device_id=dev, device_id_type=MESH)

    share = FEAT // 2
    small = [
        pltpu.make_async_copy(ids_hbm, ids_ref, wsem.at[0]),
        pltpu.make_async_copy(tok_hbm, tokx.at[pl.ds(0, share)], wsem.at[1]),
        pltpu.make_async_copy(rw_hbm, rw_ref, wsem.at[2]),
    ]
    for load in small:
        load.start()
    tokx[share:, :] = jnp.zeros((16, GROUP), BF16)
    tokx[share:, 0:share] = jnp.broadcast_to(gain_ref[...].astype(F32).reshape(1, share), (16, share)).astype(BF16)

    before = (
        lax.broadcasted_iota(jnp.int32, (GROUP, GROUP), 0) < lax.broadcasted_iota(jnp.int32, (GROUP, GROUP), 1)
    ).astype(F32).astype(BF16)
    labels = lax.broadcasted_iota(jnp.int32, (16, GROUP), 0)
    spot = lax.broadcasted_iota(jnp.int32, (HALF, 1), 0) + HALF * c
    place = []
    for k in range(len(ROUTES)):
        dev = expert_of(k)
        place.append(spot + (dev["expert"] * ND + dev["dp"]) * CAP)
    place = jnp.concatenate(place, axis=0)
    small[0].wait()
    e0 = ids_ref[0:1, :]
    e1 = ids_ref[1:2, :]
    hit0 = (e0 == labels).astype(F32)
    hit1 = (e1 == labels).astype(F32)
    earlier = jnp.dot((hit0 + hit1).astype(BF16), before, preferred_element_type=F32)
    slot0 = jnp.sum(earlier * hit0, axis=0, keepdims=True).astype(jnp.int32)
    slot1 = jnp.sum(earlier * hit1, axis=0, keepdims=True).astype(jnp.int32)
    dest0 = e0 * CAP + slot0
    dest1 = e1 * CAP + slot1
    small[1].wait()

    pl.semaphore_wait(barrier, len(partners))

    tok_copy = rcopy(tokx, sibtok, tok_s, tok_r, sib)
    tok_copy.start()
    select = ((place == dest0) | (place == dest1)).astype(F32).astype(BF16)

    loads = []
    for zz in range(NZ):
        for yy in range(NY):
            for k, source in enumerate((wg_hbm, wu_hbm)):
                loads.append(
                    pltpu.make_async_copy(
                        source.at[0, :, pl.ds((yy * NZ + zz) * FEAT, FEAT)],
                        wgu.at[zz, pl.ds(k * HID, HID), pl.ds(yy * FEAT, FEAT)],
                        wsem.at[3 + len(loads)],
                    )
                )
    dloads = [
        pltpu.make_async_copy(wd_hbm.at[0, :, pl.ds(j * FEAT, FEAT)], wd.at[j], dsem.at[j])
        for j in range(NY * NZ)
    ]

    tok_copy.wait_recv()
    here = tokx[...].astype(F32)
    there = sibtok[...].astype(F32)
    first_core = jnp.where(c == 0, here, there)
    second_core = jnp.where(c == 0, there, here)
    both = jnp.concatenate([first_core[:share], second_core[:share]], axis=0).astype(BF16)
    rows = lax.dot_general(
        select, both, (((1,), (1,)), ((), ())), preferred_element_type=F32
    ).astype(BF16)
    x[0, own, c, 0:HALF, :] = rows[0:HALF]

    def disp_copy(k):
        target = x.at[k // PER, own, c, pl.ds((k % PER) * HALF, HALF)]
        return rcopy(stage.at[k], target, disp_s.at[k], disp_r.at[k], expert_of(k))

    for k in range(1, len(ROUTES)):
        stage[k] = rows[k * HALF : (k + 1) * HALF]
        if k < 2 * PER:
            disp_copy(k).start()

    gain_row = jnp.concatenate(
        [first_core[share : share + 1, 0:share], second_core[share : share + 1, 0:share]], axis=1
    )
    index = lax.broadcasted_iota(jnp.int32, (16, 128), 0)
    tile = jnp.zeros((16, 128), F32)
    for j in range(3):
        tile = jnp.where(index == j, jnp.broadcast_to(gain_row[:, 128 * j : 128 * (j + 1)], (16, 128)), tile)
    gains[y, z] = tile.astype(BF16)

    def gzc(i):
        return rcopy(gains.at[y, z], gains.at[y, z], gz_s.at[i], gz_r.at[i], zdev(i))

    def gyc(i, way):
        ref = gains.at[y, xor4(z, i)]
        return rcopy(ref, ref, gy_s.at[i, way], gy_r.at[i, way], (up, down)[way])

    def gfc(i):
        ref = gains.at[ym, xor4(z, i)]
        return rcopy(ref, ref, gf_s.at[i], gf_r.at[i], up)

    for i in range(1, NZ):
        gzc(i).start()

    def at_step(s):
        q = lax.div(s, NZ)
        i = lax.rem(s, NZ)
        return q, i, xor4(z, i)

    def zc(q, i):
        return rcopy(x.at[q, own, c], x.at[q, own, c], z_s.at[q, i], z_r.at[q, i], zdev(i))

    def yc(s, way):
        q, i, zi = at_step(s)
        b = y * NZ + zi
        return rcopy(x.at[q, b, c], x.at[q, b, c], y_s.at[s, way], y_r.at[s, way], (up, down)[way])

    def fc(s, way):
        q, i, zi = at_step(s)
        b = (ym, yp)[way] * NZ + zi
        ref = x.at[q, b, c, pl.ds(way * (ROWS // 2), ROWS // 2)]
        return rcopy(ref, ref, f_s.at[s, way], f_r.at[s, way], (up, down)[way])

    def fzc(q):
        ref = x.at[q, lax.rem(y + 2, NY) * NZ + xor4(z, GIVER), c]
        return rcopy(ref, ref, fz_s.at[q], fz_r.at[q], zdev(1))

    def bc(s, r):
        q, i, zi = at_step(s)
        b = lax.rem(y + r, NY) * NZ + zi
        return rcopy(x.at[q, b, c], x.at[q, b, c], b_s.at[s, r], b_r.at[s, r], sib)

    def open_chunk(chunk):
        for k in range(max(1, chunk * PER), (chunk + 1) * PER):
            disp_copy(k).wait_recv()
        for j in range(1, NZ):
            zc(chunk, j).start()

    def first(s):
        q, i, zi = at_step(s)

        @pl.when(i > 0)
        def _():
            zc(q, i).wait_recv()

        yc(s, 0).start()
        yc(s, 1).start()
        bc(s, 0).start()

        @pl.when((s > 0) & (s < NZ))
        def _():
            gzc(i).wait_recv()

        @pl.when(s < NZ)
        def _():
            gyc(i, 0).start()
            gyc(i, 1).start()

        for chunk in range(1, CHUNKS):

            @pl.when(s == chunk * NZ - 1)
            def _():
                open_chunk(chunk)

    def second(s):
        q, i, zi = at_step(s)
        yc(s, 0).wait_recv()

        @pl.when(i != HANDED)
        def _():
            fc(s, 0).start()

        yc(s, 1).wait_recv()

        @pl.when(i != HANDED)
        def _():
            fc(s, 1).start()

        bc(s, 3).start()
        bc(s, 1).start()

        @pl.when(s < NZ)
        def _():
            gyc(i, 0).wait_recv()
            gfc(i).start()
            gyc(i, 1).wait_recv()

    def third(s):
        q, i, zi = at_step(s)
        @pl.when(i != HANDED)
        def _():
            fc(s, 0).wait_recv()
            fc(s, 1).wait_recv()

        @pl.when(i == GIVER)
        def _():
            fzc(q).start()

        @pl.when(i == HANDED)
        def _():
            fzc(q).wait_recv()

        bc(s, 2).start()

        @pl.when(s < NZ)
        def _():
            gfc(i).wait_recv()

    def gate_up(s):
        q, i, zi = at_step(s)
        for r in range(NY):
            bc(s, r).wait_recv()
        squares = sq[...]
        for yy in range(NY):
            block = x[q, yy * NZ + zi].reshape(2 * ROWS, FEAT)
            gain = gains[yy, zi].astype(F32)
            for j in range(3):
                slab = block[:, 128 * j : 128 * (j + 1)].astype(F32)
                squares = squares + slab * slab
                at = yy * FEAT + 128 * j
                scaled[:, at : at + 128] = (slab * gain[j : j + 1, :]).astype(BF16)
        sq[...] = squares
        acc[...] += lax.dot_general(
            wgu[zi], scaled[...], (((1,), (1,)), ((), ())), preferred_element_type=F32
        )

        @pl.when(i == NZ - 1)
        def _():
            total = jnp.sum(jnp.transpose(sq[...]), axis=0, keepdims=True)
            scale = lax.rsqrt(total / D + NORM_EPS)
            gate = acc[0:HID, :] * scale
            lift = acc[HID:, :] * scale
            value = jnp.transpose(gate / (1.0 + jnp.exp(-gate)) * lift).astype(BF16)
            for h in range(2):
                hid[q, lax.rem(c + h, 2)] = value[h * ROWS : (h + 1) * ROWS]
            acc[...] = jnp.zeros_like(acc)
            sq[...] = jnp.zeros_like(sq)

    def out_step(s):
        return lax.div(s, NZ), (NZ - 1) - lax.rem(s, NZ)

    def sc(s, r):
        return rcopy(given.at[s, r], srecv.at[s, r], sib_s.at[s, r], sib_r.at[s, r], sib)

    def hc(s, way):
        span = pl.ds(way * (ROWS // 2), ROWS // 2)
        return rcopy(mine.at[s, 2, span], halves.at[s, way], h_s.at[s, way], h_r.at[s, way], (up, down)[way])

    def wc(s, way):
        return rcopy(mine.at[s, (1, 3)[way]], fulls.at[s, way], w_s.at[s, way], w_r.at[s, way], (up, down)[way])

    def zzc(s):
        q, i = out_step(s)
        return rcopy(mine.at[s, 0], zrecv.at[q, i], zz_s.at[q, i], zz_r.at[q, i], zdev(i))

    def frc(s):
        q, i = out_step(s)
        return rcopy(mine.at[s, 2], farin.at[q], fr_s.at[q], fr_r.at[q], zdev(1))

    def retc(k):
        source = mine.at[k // PER * NZ + NZ - 1, 0, pl.ds((k % PER) * HALF, HALF)]
        return rcopy(source, ret.at[k], ret_s.at[k], ret_r.at[k], group_of(k))

    def produce(s):
        q, i = out_step(s)
        zi = xor4(z, i)
        left = hid[q].reshape(2 * ROWS, HID)
        for r in (2, 1, 3, 0):
            b = lax.rem(y + r, NY) * NZ + zi
            block = jnp.dot(left, wd[b], preferred_element_type=F32).astype(BF16)
            given[s, r] = block[ROWS:]
            sc(s, r).start()
            mine[s, r] = block[:ROWS]

    def chip_sum(s, r):
        sc(s, r).wait_recv()
        return mine[s, r].astype(F32) + srecv[s, r].astype(F32)

    def farthest(s):
        q, i = out_step(s)
        total = chip_sum(s, 2)

        @pl.when(i == HANDED)
        def _():
            mine[s, 2] = total.astype(BF16)
            frc(s).start()

        @pl.when(i == GIVER)
        def _():
            frc(s - 1).wait_recv()
            mine[s, 2] = (total + farin[q].astype(F32)).astype(BF16)

        @pl.when((i != HANDED) & (i != GIVER))
        def _():
            mine[s, 2] = total.astype(BF16)

        @pl.when(i != HANDED)
        def _():
            hc(s, 0).start()
            hc(s, 1).start()

    def neighbours(s):
        q, i = out_step(s)
        half = ROWS // 2
        for way, r in enumerate((1, 3)):
            total = chip_sum(s, r)

            @pl.when(i == HANDED)
            def _():
                mine[s, r] = total.astype(BF16)

            @pl.when(i != HANDED)
            def _():
                hc(s, way).wait_recv()
                parts = [total[:half], total[half:]]
                parts[way] = parts[way] + halves[s, way].astype(F32)
                mine[s, r] = jnp.concatenate(parts, axis=0).astype(BF16)

            wc(s, way).start()

    def finish(s):
        q, i = out_step(s)
        total = chip_sum(s, 0)
        wc(s, 0).wait_recv()
        total = total + fulls[s, 0].astype(F32)
        wc(s, 1).wait_recv()
        total = total + fulls[s, 1].astype(F32)

        @pl.when(i > 0)
        def _():
            mine[s, 0] = total.astype(BF16)
            zzc(s).start()

        @pl.when(i == 0)
        def _():
            whole = total
            for j in range(1, NZ):
                zzc(s - j).wait_recv()
                whole = whole + zrecv[q, j].astype(F32)
            whole = whole.astype(BF16)
            mine[s, 0] = whole

            @pl.when(q == 0)
            def _():
                ret[0] = whole[0:HALF]

            for chunk in range(CHUNKS):

                @pl.when(q == chunk)
                def _():
                    for k in range(max(1, chunk * PER), (chunk + 1) * PER):
                        retc(k).start()

    def drain_gather(s):
        q, i, zi = at_step(s)
        for way in range(2):
            yc(s, way).wait_send()
        for r in range(NY):
            bc(s, r).wait_send()

        @pl.when(i != HANDED)
        def _():
            fc(s, 0).wait_send()
            fc(s, 1).wait_send()

        @pl.when(i == GIVER)
        def _():
            fzc(q).wait_send()

        @pl.when(i > 0)
        def _():
            zc(q, i).wait_send()

    def drain_reduce(s):
        q, i = out_step(s)
        for way in range(2):
            wc(s, way).wait_send()
        for r in range(NY):
            sc(s, r).wait_send()

        @pl.when(i != HANDED)
        def _():
            hc(s, 0).wait_send()
            hc(s, 1).wait_send()

        @pl.when(i == HANDED)
        def _():
            frc(s).wait_send()

        @pl.when(i > 0)
        def _():
            zzc(s).wait_send()

    def drain(stage_of, steps):
        def one(s, carry):
            stage_of(s)
            return carry

        lax.fori_loop(0, steps, one, 0)

    def step(t, carry):
        u = t - LAG

        def run(stages):
            for stage_of, now, behind in stages:

                @pl.when((now >= behind) & (now < STEPS + behind))
                def _():
                    stage_of(now - behind)

        run((
            (first, t, 0), (second, t, SECOND), (third, t, THIRD),
            (finish, u, FINISH), (neighbours, u, NEIGHBOURS), (farthest, u, FARTHEST),
        ))

        for chunk in range(2, CHUNKS):

            @pl.when(t == 2 * chunk - 1)
            def _():
                for k in range(chunk * PER, (chunk + 1) * PER):
                    disp_copy(k).start()

        @pl.when(t == MULTIPLY)
        def _():
            for load in loads:
                load.wait()

        @pl.when(u == 0)
        def _():
            for load in dloads:
                load.wait()

        run(((gate_up, t, MULTIPLY), (produce, u, 0)))

        @pl.when(u == STEPS)
        def _():
            drain(drain_gather, STEPS)

        @pl.when(u == STEPS + 1)
        def _():
            drain(drain_reduce, STEPS - NZ)

        return carry

    open_chunk(0)
    first(jnp.int32(0))
    for load in loads + dloads:
        load.start()
    acc[...] = jnp.zeros_like(acc)
    sq[...] = jnp.zeros_like(sq)
    lax.fori_loop(1, LAG + STEPS + FINISH, step, 0)

    small[2].wait()
    combined = jnp.zeros((FEAT, GROUP), F32)
    for chunk in range(CHUNKS):
        for k in range(max(1, chunk * PER), (chunk + 1) * PER):
            retc(k).wait_recv()
        came = ret[chunk * PER : (chunk + 1) * PER].reshape(ROWS, FEAT)
        spots = place[chunk * ROWS : (chunk + 1) * ROWS]
        for k, dest in enumerate((dest0, dest1)):
            pick = (spots == dest).astype(F32).astype(BF16)
            combined += rw_ref[k : k + 1, :] * lax.dot_general(
                came, pick, (((0,), (0,)), ((), ())), preferred_element_type=F32
            )
    left = combined[:share]
    right = combined[share:]
    part[...] = jnp.where(c == 0, right, left)
    part_copy = rcopy(part, partr, part_s, part_r, sib)
    part_copy.start()
    kept = jnp.where(c == 0, left, right)
    part_copy.wait_recv()
    out_ref[...] = (kept + partr[...]).astype(BF16)

    part_copy.wait_send()
    tok_copy.wait_send()
    for k in range(1, len(ROUTES)):
        disp_copy(k).wait_send()
        retc(k).wait_send()
    for i in range(NZ):
        if i > 0:
            gzc(i).wait_send()
        gyc(i, 0).wait_send()
        gyc(i, 1).wait_send()
        gfc(i).wait_send()

    for s in range(STEPS - NZ, STEPS):
        drain_reduce(jnp.int32(s))


def per_device(tokens, norm_gain, expert_ids, route_weights, gate_weight, up_weight, down_weight):
    vmem = pl.BlockSpec(memory_space=pltpu.VMEM)
    hbm = pl.BlockSpec(memory_space=pl.ANY)
    blocks = NY * NZ
    dma = pltpu.SemaphoreType.DMA
    scratch = [
        pltpu.VMEM((NZ, 2 * HID, NY * FEAT), BF16),
        pltpu.VMEM((blocks, HID, FEAT), BF16),
        pltpu.VMEM((CHUNKS, blocks, 2, ROWS, FEAT), BF16),
        pltpu.VMEM((2 * ROWS, NY * FEAT), BF16),
        pltpu.VMEM((2 * HID, 2 * ROWS), F32),
        pltpu.VMEM((2 * ROWS, 128), F32),
        pltpu.VMEM((CHUNKS, 2, ROWS, HID), BF16),
        pltpu.VMEM((NY, NZ, 16, 128), BF16),
        pltpu.VMEM((2, GROUP), jnp.int32),
        pltpu.VMEM((2, GROUP), F32),
        pltpu.VMEM((FEAT // 2 + 16, GROUP), BF16),
        pltpu.VMEM((FEAT // 2 + 16, GROUP), BF16),
        pltpu.VMEM((len(ROUTES), HALF, FEAT), BF16),
        pltpu.VMEM((CHUNKS, ROWS, FEAT), BF16),
        pltpu.VMEM((STEPS, NY, ROWS, FEAT), BF16),
        pltpu.VMEM((STEPS, NY, ROWS, FEAT), BF16),
        pltpu.VMEM((STEPS, NY, ROWS, FEAT), BF16),
        pltpu.VMEM((STEPS, 2, ROWS // 2, FEAT), BF16),
        pltpu.VMEM((STEPS, 2, ROWS, FEAT), BF16),
        pltpu.VMEM((CHUNKS, NZ, ROWS, FEAT), BF16),
        pltpu.VMEM((len(ROUTES), HALF, FEAT), BF16),
        pltpu.VMEM((FEAT // 2, GROUP), F32),
        pltpu.VMEM((FEAT // 2, GROUP), F32),
        dma((3 + 2 * blocks,)), dma((blocks,)),
        dma, dma, dma((len(ROUTES),)), dma((len(ROUTES),)),
        dma((NZ,)), dma((NZ,)), dma((NZ, 2)), dma((NZ, 2)), dma((NZ,)), dma((NZ,)),
        dma((CHUNKS, NZ)), dma((CHUNKS, NZ)), dma((STEPS, 2)), dma((STEPS, 2)),
        dma((STEPS, 2)), dma((STEPS, 2)), dma((STEPS, NY)), dma((STEPS, NY)),
        dma((CHUNKS,)), dma((CHUNKS,)), dma((CHUNKS,)), dma((CHUNKS,)),
        dma((STEPS, NY)), dma((STEPS, NY)), dma((STEPS, 2)), dma((STEPS, 2)),
        dma((STEPS, 2)), dma((STEPS, 2)), dma((CHUNKS, NZ)), dma((CHUNKS, NZ)),
        dma((len(ROUTES),)), dma((len(ROUTES),)), dma, dma,
    ]
    rows = CHUNKS * 2 * ROWS
    out = pl.pallas_call(
        kernel,
        out_shape=jax.ShapeDtypeStruct((FEAT // 2, GROUP), BF16),
        in_specs=[hbm, vmem, hbm, hbm, hbm, hbm, hbm],
        out_specs=vmem,
        scratch_shapes=scratch,
        cost_estimate=pl.CostEstimate(
            flops=6 * rows * D * HID, bytes_accessed=6 * D * HID, transcendentals=rows * HID
        ),
        compiler_params=pltpu.CompilerParams(
            collective_id=0, has_side_effects=True, vmem_limit_bytes=61 * 1024 * 1024
        ),
    )(
        tokens.T,
        norm_gain,
        expert_ids.T,
        route_weights.T,
        gate_weight.swapaxes(1, 2),
        up_weight.swapaxes(1, 2),
        down_weight,
    )
    return out.T


def solution(mesh):
    placed = (
        P(("expert", "dp"), "tensor"),
        P("tensor"),
        P(("expert", "dp"), None),
        P(("expert", "dp"), None),
        P(("expert", "dp"), None, "tensor"),
        P(("expert", "dp"), None, "tensor"),
        P(("expert", "dp"), "tensor", None),
    )
    return jax.shard_map(
        per_device,
        mesh=mesh,
        in_specs=placed,
        out_specs=P(("expert", "dp"), "tensor"),
        check_vma=False,
    )
```

```python
import jax
import jax.numpy as jnp
from jax import lax
from jax.experimental import pallas as pl
from jax.experimental.pallas import tpu as pltpu
from jax.sharding import PartitionSpec as P

D = 6144
NORM_EPS = 1e-05
MESH = pl.DeviceIdType.MESH
NX, NY, NZ, ND = 4, 4, 4, 2
GROUP = 256
CAP = 128
HALF = CAP // 2
FEAT = 384
HID = 352
ROUTES = ((0, 0), (1, 0), (0, 1), (1, 1), (2, 1), (3, 1), (2, 0), (3, 0))
PER = 2
CHUNKS = len(ROUTES) // PER
ROWS = PER * HALF
STEPS = CHUNKS * NZ
GIVER, HANDED = 2, 3
SECOND, THIRD, MULTIPLY = 3, 6, 7
FARTHEST, NEIGHBOURS, FINISH = 1, 4, 7
LAG = NZ + MULTIPLY
F32 = jnp.float32
BF16 = jnp.bfloat16


def xor4(a, b):
    low = lax.rem(lax.rem(a, 2) + lax.rem(b, 2), 2)
    high = lax.rem(lax.div(a, 2) + lax.div(b, 2), 2)
    return low + 2 * high


def kernel(
    tok_hbm, gain_ref, ids_hbm, rw_hbm, wg_hbm, wu_hbm, wd_hbm,
    out_ref,
    wgu, wd, x, scaled, acc, sq, hid, gains,
    ids_ref, rw_ref, tokx, sibtok, stage, farin, mine, given, srecv, halves, fulls, zrecv, ret, part, partr,
    wsem, dsem, tok_s, tok_r, disp_s, disp_r, gz_s, gz_r, gy_s, gy_r, gf_s, gf_r,
    z_s, z_r, y_s, y_r, f_s, f_r, b_s, b_r,
    fz_s, fz_r, fr_s, fr_r,
    sib_s, sib_r, h_s, h_r, w_s, w_r, zz_s, zz_r, ret_s, ret_r, part_s, part_r,
):
    xi = lax.axis_index("expert")
    di = lax.axis_index("dp")
    me = lax.axis_index("tensor")
    c = lax.rem(me, 2)
    z = lax.rem(lax.div(me, 2), NZ)
    y = lax.div(me, 2 * NZ)
    own = y * NZ + z
    yp = lax.rem(y + 1, NY)
    ym = lax.rem(y + NY - 1, NY)

    def tid(yy, zz, cc):
        return (yy * NZ + zz) * 2 + cc

    sib = {"tensor": tid(y, z, 1 - c)}
    up = {"tensor": tid(yp, z, c)}
    down = {"tensor": tid(ym, z, c)}

    def zdev(i):
        return {"tensor": tid(y, xor4(z, i), c)}

    def expert_of(k):
        dx, dd = ROUTES[k]
        return {"expert": lax.rem(xi + dx, NX), "dp": lax.rem(di + dd, ND)}

    def group_of(k):
        dx, dd = ROUTES[k]
        return {"expert": lax.rem(xi + NX - dx, NX), "dp": lax.rem(di + dd, ND)}

    def rcopy(src, dst, ssem, rsem, dev):
        return pltpu.make_async_remote_copy(
            src_ref=src, dst_ref=dst, send_sem=ssem, recv_sem=rsem, device_id=dev, device_id_type=MESH
        )

    barrier = pltpu.get_barrier_semaphore()
    partners = [sib, up, down] + [zdev(i) for i in range(1, NZ)] + [expert_of(k) for k in range(1, len(ROUTES))]
    for dev in partners:
        pl.semaphore_signal(barrier, inc=1, device_id=dev, device_id_type=MESH)

    share = FEAT // 2
    small = [
        pltpu.make_async_copy(ids_hbm, ids_ref, wsem.at[0]),
        pltpu.make_async_copy(tok_hbm, tokx.at[pl.ds(0, share)], wsem.at[1]),
        pltpu.make_async_copy(rw_hbm, rw_ref, wsem.at[2]),
    ]
    for load in small:
        load.start()
    tokx[share:, :] = jnp.zeros((16, GROUP), BF16)
    tokx[share:, 0:share] = jnp.broadcast_to(gain_ref[...].astype(F32).reshape(1, share), (16, share)).astype(BF16)

    before = (
        lax.broadcasted_iota(jnp.int32, (GROUP, GROUP), 0) < lax.broadcasted_iota(jnp.int32, (GROUP, GROUP), 1)
    ).astype(F32).astype(BF16)
    labels = lax.broadcasted_iota(jnp.int32, (16, GROUP), 0)
    spot = lax.broadcasted_iota(jnp.int32, (HALF, 1), 0) + HALF * c
    place = []
    for k in range(len(ROUTES)):
        dev = expert_of(k)
        place.append(spot + (dev["expert"] * ND + dev["dp"]) * CAP)
    place = jnp.concatenate(place, axis=0)
    small[0].wait()
    e0 = ids_ref[0:1, :]
    e1 = ids_ref[1:2, :]
    hit0 = (e0 == labels).astype(F32)
    hit1 = (e1 == labels).astype(F32)
    earlier = jnp.dot((hit0 + hit1).astype(BF16), before, preferred_element_type=F32)
    slot0 = jnp.sum(earlier * hit0, axis=0, keepdims=True).astype(jnp.int32)
    slot1 = jnp.sum(earlier * hit1, axis=0, keepdims=True).astype(jnp.int32)
    dest0 = e0 * CAP + slot0
    dest1 = e1 * CAP + slot1
    small[1].wait()

    pl.semaphore_wait(barrier, len(partners))

    tok_copy = rcopy(tokx, sibtok, tok_s, tok_r, sib)
    tok_copy.start()
    select = ((place == dest0) | (place == dest1)).astype(F32).astype(BF16)

    loads = []
    for zz in range(NZ):
        for yy in range(NY):
            for k, source in enumerate((wg_hbm, wu_hbm)):
                loads.append(
                    pltpu.make_async_copy(
                        source.at[0, :, pl.ds((yy * NZ + zz) * FEAT, FEAT)],
                        wgu.at[zz, pl.ds(k * HID, HID), pl.ds(yy * FEAT, FEAT)],
                        wsem.at[3 + len(loads)],
                    )
                )
    dloads = [
        pltpu.make_async_copy(wd_hbm.at[0, :, pl.ds(j * FEAT, FEAT)], wd.at[j], dsem.at[j])
        for j in range(NY * NZ)
    ]

    tok_copy.wait_recv()
    here = tokx[...].astype(F32)
    there = sibtok[...].astype(F32)
    first_core = jnp.where(c == 0, here, there)
    second_core = jnp.where(c == 0, there, here)
    both = jnp.concatenate([first_core[:share], second_core[:share]], axis=0).astype(BF16)
    rows = lax.dot_general(
        select, both, (((1,), (1,)), ((), ())), preferred_element_type=F32
    ).astype(BF16)
    x[0, own, c, 0:HALF, :] = rows[0:HALF]

    def disp_copy(k):
        target = x.at[k // PER, own, c, pl.ds((k % PER) * HALF, HALF)]
        return rcopy(stage.at[k], target, disp_s.at[k], disp_r.at[k], expert_of(k))

    for k in range(1, len(ROUTES)):
        stage[k] = rows[k * HALF : (k + 1) * HALF]
        if k < 2 * PER:
            disp_copy(k).start()

    gain_row = jnp.concatenate(
        [first_core[share : share + 1, 0:share], second_core[share : share + 1, 0:share]], axis=1
    )
    index = lax.broadcasted_iota(jnp.int32, (16, 128), 0)
    tile = jnp.zeros((16, 128), F32)
    for j in range(3):
        tile = jnp.where(index == j, jnp.broadcast_to(gain_row[:, 128 * j : 128 * (j + 1)], (16, 128)), tile)
    gains[y, z] = tile.astype(BF16)

    def gzc(i):
        return rcopy(gains.at[y, z], gains.at[y, z], gz_s.at[i], gz_r.at[i], zdev(i))

    def gyc(i, way):
        ref = gains.at[y, xor4(z, i)]
        return rcopy(ref, ref, gy_s.at[i, way], gy_r.at[i, way], (up, down)[way])

    def gfc(i):
        ref = gains.at[ym, xor4(z, i)]
        return rcopy(ref, ref, gf_s.at[i], gf_r.at[i], up)

    for i in range(1, NZ):
        gzc(i).start()

    def at_step(s):
        q = lax.div(s, NZ)
        i = lax.rem(s, NZ)
        return q, i, xor4(z, i)

    def zc(q, i):
        return rcopy(x.at[q, own, c], x.at[q, own, c], z_s.at[q, i], z_r.at[q, i], zdev(i))

    def yc(s, way):
        q, i, zi = at_step(s)
        b = y * NZ + zi
        return rcopy(x.at[q, b, c], x.at[q, b, c], y_s.at[s, way], y_r.at[s, way], (up, down)[way])

    def fc(s, way):
        q, i, zi = at_step(s)
        b = (ym, yp)[way] * NZ + zi
        ref = x.at[q, b, c, pl.ds(way * (ROWS // 2), ROWS // 2)]
        return rcopy(ref, ref, f_s.at[s, way], f_r.at[s, way], (up, down)[way])

    def fzc(q):
        ref = x.at[q, lax.rem(y + 2, NY) * NZ + xor4(z, GIVER), c]
        return rcopy(ref, ref, fz_s.at[q], fz_r.at[q], zdev(1))

    def bc(s, r):
        q, i, zi = at_step(s)
        b = lax.rem(y + r, NY) * NZ + zi
        return rcopy(x.at[q, b, c], x.at[q, b, c], b_s.at[s, r], b_r.at[s, r], sib)

    def open_chunk(chunk):
        for k in range(max(1, chunk * PER), (chunk + 1) * PER):
            disp_copy(k).wait_recv()
        for j in range(1, NZ):
            zc(chunk, j).start()

    def first(s):
        q, i, zi = at_step(s)

        @pl.when(i > 0)
        def _():
            zc(q, i).wait_recv()

        yc(s, 0).start()
        yc(s, 1).start()
        bc(s, 0).start()

        @pl.when((s > 0) & (s < NZ))
        def _():
            gzc(i).wait_recv()

        @pl.when(s < NZ)
        def _():
            gyc(i, 0).start()
            gyc(i, 1).start()

        for chunk in range(1, CHUNKS):

            @pl.when(s == chunk * NZ - 1)
            def _():
                open_chunk(chunk)

    def second(s):
        q, i, zi = at_step(s)
        yc(s, 0).wait_recv()

        @pl.when(i != HANDED)
        def _():
            fc(s, 0).start()

        yc(s, 1).wait_recv()

        @pl.when(i != HANDED)
        def _():
            fc(s, 1).start()

        bc(s, 3).start()
        bc(s, 1).start()

        @pl.when(s < NZ)
        def _():
            gyc(i, 0).wait_recv()
            gfc(i).start()
            gyc(i, 1).wait_recv()

    def third(s):
        q, i, zi = at_step(s)
        @pl.when(i != HANDED)
        def _():
            fc(s, 0).wait_recv()
            fc(s, 1).wait_recv()

        @pl.when(i == GIVER)
        def _():
            fzc(q).start()

        @pl.when(i == HANDED)
        def _():
            fzc(q).wait_recv()

        bc(s, 2).start()

        @pl.when(s < NZ)
        def _():
            gfc(i).wait_recv()

    def gate_up(s):
        q, i, zi = at_step(s)
        for r in range(NY):
            bc(s, r).wait_recv()
        squares = sq[...]
        for yy in range(NY):
            block = x[q, yy * NZ + zi].reshape(2 * ROWS, FEAT)
            gain = gains[yy, zi].astype(F32)
            for j in range(3):
                slab = block[:, 128 * j : 128 * (j + 1)].astype(F32)
                squares = squares + slab * slab
                at = yy * FEAT + 128 * j
                scaled[:, at : at + 128] = (slab * gain[j : j + 1, :]).astype(BF16)
        sq[...] = squares
        acc[...] += lax.dot_general(
            wgu[zi], scaled[...], (((1,), (1,)), ((), ())), preferred_element_type=F32
        )

        @pl.when(i == NZ - 1)
        def _():
            total = jnp.sum(jnp.transpose(sq[...]), axis=0, keepdims=True)
            scale = lax.rsqrt(total / D + NORM_EPS)
            gate = acc[0:HID, :] * scale
            lift = acc[HID:, :] * scale
            value = jnp.transpose(gate / (1.0 + jnp.exp(-gate)) * lift).astype(BF16)
            for h in range(2):
                hid[q, lax.rem(c + h, 2)] = value[h * ROWS : (h + 1) * ROWS]
            acc[...] = jnp.zeros_like(acc)
            sq[...] = jnp.zeros_like(sq)

    def out_step(s):
        return lax.div(s, NZ), (NZ - 1) - lax.rem(s, NZ)

    def sc(s, r):
        return rcopy(given.at[s, r], srecv.at[s, r], sib_s.at[s, r], sib_r.at[s, r], sib)

    def hc(s, way):
        span = pl.ds(way * (ROWS // 2), ROWS // 2)
        return rcopy(mine.at[s, 2, span], halves.at[s, way], h_s.at[s, way], h_r.at[s, way], (up, down)[way])

    def wc(s, way):
        return rcopy(mine.at[s, (1, 3)[way]], fulls.at[s, way], w_s.at[s, way], w_r.at[s, way], (up, down)[way])

    def zzc(s):
        q, i = out_step(s)
        return rcopy(mine.at[s, 0], zrecv.at[q, i], zz_s.at[q, i], zz_r.at[q, i], zdev(i))

    def frc(s):
        q, i = out_step(s)
        return rcopy(mine.at[s, 2], farin.at[q], fr_s.at[q], fr_r.at[q], zdev(1))

    def retc(k):
        source = mine.at[k // PER * NZ + NZ - 1, 0, pl.ds((k % PER) * HALF, HALF)]
        return rcopy(source, ret.at[k], ret_s.at[k], ret_r.at[k], group_of(k))

    def produce(s):
        q, i = out_step(s)
        zi = xor4(z, i)
        left = hid[q].reshape(2 * ROWS, HID)
        for r in (2, 1, 3, 0):
            b = lax.rem(y + r, NY) * NZ + zi
            block = jnp.dot(left, wd[b], preferred_element_type=F32).astype(BF16)
            given[s, r] = block[ROWS:]
            sc(s, r).start()
            mine[s, r] = block[:ROWS]

    def chip_sum(s, r):
        sc(s, r).wait_recv()
        return mine[s, r].astype(F32) + srecv[s, r].astype(F32)

    def farthest(s):
        q, i = out_step(s)
        total = chip_sum(s, 2)

        @pl.when(i == HANDED)
        def _():
            mine[s, 2] = total.astype(BF16)
            frc(s).start()

        @pl.when(i == GIVER)
        def _():
            frc(s - 1).wait_recv()
            mine[s, 2] = (total + farin[q].astype(F32)).astype(BF16)

        @pl.when((i != HANDED) & (i != GIVER))
        def _():
            mine[s, 2] = total.astype(BF16)

        @pl.when(i != HANDED)
        def _():
            hc(s, 0).start()
            hc(s, 1).start()

    def neighbours(s):
        q, i = out_step(s)
        half = ROWS // 2
        for way, r in enumerate((1, 3)):
            total = chip_sum(s, r)

            @pl.when(i == HANDED)
            def _():
                mine[s, r] = total.astype(BF16)

            @pl.when(i != HANDED)
            def _():
                hc(s, way).wait_recv()
                parts = [total[:half], total[half:]]
                parts[way] = parts[way] + halves[s, way].astype(F32)
                mine[s, r] = jnp.concatenate(parts, axis=0).astype(BF16)

            wc(s, way).start()

    def finish(s):
        q, i = out_step(s)
        total = chip_sum(s, 0)
        wc(s, 0).wait_recv()
        total = total + fulls[s, 0].astype(F32)
        wc(s, 1).wait_recv()
        total = total + fulls[s, 1].astype(F32)

        @pl.when(i > 0)
        def _():
            mine[s, 0] = total.astype(BF16)
            zzc(s).start()

        @pl.when(i == 0)
        def _():
            whole = total
            for j in range(1, NZ):
                zzc(s - j).wait_recv()
                whole = whole + zrecv[q, j].astype(F32)
            whole = whole.astype(BF16)
            mine[s, 0] = whole

            @pl.when(q == 0)
            def _():
                ret[0] = whole[0:HALF]

            for chunk in range(CHUNKS):

                @pl.when(q == chunk)
                def _():
                    for k in range(max(1, chunk * PER), (chunk + 1) * PER):
                        retc(k).start()

    def drain_gather(s):
        q, i, zi = at_step(s)
        for way in range(2):
            yc(s, way).wait_send()
        for r in range(NY):
            bc(s, r).wait_send()

        @pl.when(i != HANDED)
        def _():
            fc(s, 0).wait_send()
            fc(s, 1).wait_send()

        @pl.when(i == GIVER)
        def _():
            fzc(q).wait_send()

        @pl.when(i > 0)
        def _():
            zc(q, i).wait_send()

    def drain_reduce(s):
        q, i = out_step(s)
        for way in range(2):
            wc(s, way).wait_send()
        for r in range(NY):
            sc(s, r).wait_send()

        @pl.when(i != HANDED)
        def _():
            hc(s, 0).wait_send()
            hc(s, 1).wait_send()

        @pl.when(i == HANDED)
        def _():
            frc(s).wait_send()

        @pl.when(i > 0)
        def _():
            zzc(s).wait_send()

    def drain(stage_of, steps):
        def one(s, carry):
            stage_of(s)
            return carry

        lax.fori_loop(0, steps, one, 0)

    def step(t, carry):
        u = t - LAG

        def run(stages):
            for stage_of, now, behind in stages:

                @pl.when((now >= behind) & (now < STEPS + behind))
                def _():
                    stage_of(now - behind)

        run((
            (first, t, 0), (second, t, SECOND), (third, t, THIRD),
            (finish, u, FINISH), (neighbours, u, NEIGHBOURS), (farthest, u, FARTHEST),
        ))

        for chunk in range(2, CHUNKS):

            @pl.when(t == 2 * chunk - 1)
            def _():
                for k in range(chunk * PER, (chunk + 1) * PER):
                    disp_copy(k).start()

        @pl.when(t == MULTIPLY)
        def _():
            for load in loads:
                load.wait()

        @pl.when(u == 0)
        def _():
            for load in dloads:
                load.wait()

        run(((gate_up, t, MULTIPLY), (produce, u, 0)))

        @pl.when(u == STEPS)
        def _():
            drain(drain_gather, STEPS)

        @pl.when(u == STEPS + FINISH - 3)
        def _():
            drain(drain_reduce, STEPS - NZ)

        return carry

    open_chunk(0)
    first(jnp.int32(0))
    for load in loads + dloads:
        load.start()
    acc[...] = jnp.zeros_like(acc)
    sq[...] = jnp.zeros_like(sq)
    lax.fori_loop(1, LAG + STEPS + FINISH, step, 0)

    small[2].wait()
    combined = jnp.zeros((FEAT, GROUP), F32)
    for chunk in range(CHUNKS):
        for k in range(max(1, chunk * PER), (chunk + 1) * PER):
            retc(k).wait_recv()
        came = ret[chunk * PER : (chunk + 1) * PER].reshape(ROWS, FEAT)
        spots = place[chunk * ROWS : (chunk + 1) * ROWS]
        for k, dest in enumerate((dest0, dest1)):
            pick = (spots == dest).astype(F32).astype(BF16)
            combined += rw_ref[k : k + 1, :] * lax.dot_general(
                came, pick, (((0,), (0,)), ((), ())), preferred_element_type=F32
            )
    left = combined[:share]
    right = combined[share:]
    part[...] = jnp.where(c == 0, right, left)
    part_copy = rcopy(part, partr, part_s, part_r, sib)
    part_copy.start()
    kept = jnp.where(c == 0, left, right)
    part_copy.wait_recv()
    out_ref[...] = (kept + partr[...]).astype(BF16)

    part_copy.wait_send()
    tok_copy.wait_send()
    for k in range(1, len(ROUTES)):
        disp_copy(k).wait_send()
        retc(k).wait_send()
    for i in range(NZ):
        if i > 0:
            gzc(i).wait_send()
        gyc(i, 0).wait_send()
        gyc(i, 1).wait_send()
        gfc(i).wait_send()

    for s in range(STEPS - NZ, STEPS):
        drain_reduce(jnp.int32(s))


def per_device(tokens, norm_gain, expert_ids, route_weights, gate_weight, up_weight, down_weight):
    vmem = pl.BlockSpec(memory_space=pltpu.VMEM)
    hbm = pl.BlockSpec(memory_space=pl.ANY)
    blocks = NY * NZ
    dma = pltpu.SemaphoreType.DMA
    scratch = [
        pltpu.VMEM((NZ, 2 * HID, NY * FEAT), BF16),
        pltpu.VMEM((blocks, HID, FEAT), BF16),
        pltpu.VMEM((CHUNKS, blocks, 2, ROWS, FEAT), BF16),
        pltpu.VMEM((2 * ROWS, NY * FEAT), BF16),
        pltpu.VMEM((2 * HID, 2 * ROWS), F32),
        pltpu.VMEM((2 * ROWS, 128), F32),
        pltpu.VMEM((CHUNKS, 2, ROWS, HID), BF16),
        pltpu.VMEM((NY, NZ, 16, 128), BF16),
        pltpu.VMEM((2, GROUP), jnp.int32),
        pltpu.VMEM((2, GROUP), F32),
        pltpu.VMEM((FEAT // 2 + 16, GROUP), BF16),
        pltpu.VMEM((FEAT // 2 + 16, GROUP), BF16),
        pltpu.VMEM((len(ROUTES), HALF, FEAT), BF16),
        pltpu.VMEM((CHUNKS, ROWS, FEAT), BF16),
        pltpu.VMEM((STEPS, NY, ROWS, FEAT), BF16),
        pltpu.VMEM((STEPS, NY, ROWS, FEAT), BF16),
        pltpu.VMEM((STEPS, NY, ROWS, FEAT), BF16),
        pltpu.VMEM((STEPS, 2, ROWS // 2, FEAT), BF16),
        pltpu.VMEM((STEPS, 2, ROWS, FEAT), BF16),
        pltpu.VMEM((CHUNKS, NZ, ROWS, FEAT), BF16),
        pltpu.VMEM((len(ROUTES), HALF, FEAT), BF16),
        pltpu.VMEM((FEAT // 2, GROUP), F32),
        pltpu.VMEM((FEAT // 2, GROUP), F32),
        dma((3 + 2 * blocks,)), dma((blocks,)),
        dma, dma, dma((len(ROUTES),)), dma((len(ROUTES),)),
        dma((NZ,)), dma((NZ,)), dma((NZ, 2)), dma((NZ, 2)), dma((NZ,)), dma((NZ,)),
        dma((CHUNKS, NZ)), dma((CHUNKS, NZ)), dma((STEPS, 2)), dma((STEPS, 2)),
        dma((STEPS, 2)), dma((STEPS, 2)), dma((STEPS, NY)), dma((STEPS, NY)),
        dma((CHUNKS,)), dma((CHUNKS,)), dma((CHUNKS,)), dma((CHUNKS,)),
        dma((STEPS, NY)), dma((STEPS, NY)), dma((STEPS, 2)), dma((STEPS, 2)),
        dma((STEPS, 2)), dma((STEPS, 2)), dma((CHUNKS, NZ)), dma((CHUNKS, NZ)),
        dma((len(ROUTES),)), dma((len(ROUTES),)), dma, dma,
    ]
    rows = CHUNKS * 2 * ROWS
    out = pl.pallas_call(
        kernel,
        out_shape=jax.ShapeDtypeStruct((FEAT // 2, GROUP), BF16),
        in_specs=[hbm, vmem, hbm, hbm, hbm, hbm, hbm],
        out_specs=vmem,
        scratch_shapes=scratch,
        cost_estimate=pl.CostEstimate(
            flops=6 * rows * D * HID, bytes_accessed=6 * D * HID, transcendentals=rows * HID
        ),
        compiler_params=pltpu.CompilerParams(
            collective_id=0, has_side_effects=True, vmem_limit_bytes=61 * 1024 * 1024
        ),
    )(
        tokens.T,
        norm_gain,
        expert_ids.T,
        route_weights.T,
        gate_weight.swapaxes(1, 2),
        up_weight.swapaxes(1, 2),
        down_weight,
    )
    return out.T


def solution(mesh):
    placed = (
        P(("expert", "dp"), "tensor"),
        P("tensor"),
        P(("expert", "dp"), None),
        P(("expert", "dp"), None),
        P(("expert", "dp"), None, "tensor"),
        P(("expert", "dp"), None, "tensor"),
        P(("expert", "dp"), "tensor", None),
    )
    return jax.shard_map(
        per_device,
        mesh=mesh,
        in_specs=placed,
        out_specs=P(("expert", "dp"), "tensor"),
        check_vma=False,
    )
```
